32 devices in a mesh: ctx: 4 (over z), tp: 8 (over y, x, core).
Axes of the slice: x: 2, y: 2, z: 4, core: 2. Of those that a mesh axis runs over, the one named last changes fastest.
Arguments:
- hidden_in: bfloat16 [2048, 8192], P('ctx', 'tp'), may hold values from -30 to 30
- norm_gain: bfloat16 [8192], P('tp'), may hold values from 0.099609375 to 1.8984375
- w_query: bfloat16 [8192, 4096], P(None, 'tp'), may hold values from -1 to 1
- w_key: bfloat16 [8192, 1024], P(None, 'tp'), may hold values from -1 to 1
- w_value: bfloat16 [8192, 1024], P(None, 'tp'), may hold values from -0.0625 to 0.0625
- sign_bits: int32 [32, 128], P('tp'), may hold values from 0 to 1
- w_out: bfloat16 [4096, 8192], P(None, 'tp'), may hold values from -1 to 1
- teacher: bfloat16 [2048, 8192], P('ctx', 'tp'), may hold values from -30 to 30
Outputs:
- student: bfloat16 [2048, 8192], P('ctx', 'tp')
- row_loss: float32 [2048], P('ctx')
The draws below stay inside these ranges and needn't reach their ends.
Inputs may be any that keep to these rules, and one draw needn't show every extreme that they name: `sign_bits`: 1 stands for the sign +1 and 0 for -1.
All inputs are finite; a program needn't handle non-finite values.
Results may differ from the reference program's by a relative error of at most 0.012.
The reference program's roundings to bfloat16 on the way (of `quantized`, `queries`, `attended` and `rotated_q`) count: a program that leaves them out, or rounds other values in their place, can miss the bound.
Values may be sent and summed in bfloat16 or wider, within the bound.
No kernel may reach another device: no remote copies, remote signals or barrier semaphores. Data moves between devices by JAX's collectives and lax.ppermute only.
A program may use at most 128 MiB of HBM per device.

```python
import math
import jax
import jax.numpy as jnp
from jax import lax

D = 8192
QH = 32
KVH = 8
HD = 128
GROUP = 128
TOK_DEV = 512
SEQ = 2048


def column_profile(lowest, highest):
    columns = jnp.arange(D, dtype=jnp.float32)
    return lowest * (highest / lowest) ** (columns / max(D - 1, 1))


def draw_hidden_in(key, part):
    row_scale = jnp.exp(jax.random.uniform(jax.random.fold_in(key, 2), (SEQ, 1), jnp.float32, math.log(0.5), math.log(5.0)))
    noise = jax.random.normal(jax.random.fold_in(key, 1), (SEQ, D), jnp.float32)
    rows = noise * column_profile(0.58, 1.73) * row_scale
    return jnp.clip(rows, -30.0, 30.0).astype(jnp.bfloat16)


def draw_w_query(key, part):
    entries = jax.random.normal(jax.random.fold_in(key, 11), (D, QH * HD), jnp.float32) * D ** (-0.5)
    return jnp.clip(entries, -1.0, 1.0).astype(jnp.bfloat16)


def draw_w_key(key, part):
    entries = jax.random.normal(jax.random.fold_in(key, 12), (D, KVH * HD), jnp.float32) * D ** (-0.5)
    return jnp.clip(entries, -1.0, 1.0).astype(jnp.bfloat16)


def draw_w_out(key, part):
    entries = jax.random.normal(jax.random.fold_in(key, 13), (QH * HD, D), jnp.float32) * (QH * HD) ** (-0.5)
    entries = entries * column_profile(0.3, 3.0)
    return jnp.clip(entries, -1.0, 1.0).astype(jnp.bfloat16)


def draw_teacher(key, part):
    entries = jax.random.normal(jax.random.fold_in(key, 14), (SEQ, D), jnp.float32) * column_profile(0.3, 3.0)
    return jnp.clip(entries, -30.0, 30.0).astype(jnp.bfloat16)


def plant(values, stream_key, least, high):
    longest = values.shape.index(max(values.shape))
    spots = []
    for shift in (0, 1):
        where = [jax.random.randint(jax.random.fold_in(stream_key, axis), (), 0, length) for axis, length in enumerate(values.shape)]
        where[longest] = (where[longest] + shift) % values.shape[longest]
        spots.append(tuple(where))
    return values.at[spots[0]].set(least).at[spots[1]].set(high)


def block_scale(key, extent, split, least, high):
    gain = 1.0
    for axis_at, blocks in split:
        heights = jax.random.uniform(jax.random.fold_in(jax.random.fold_in(key, 6), axis_at), (blocks,), jnp.float32, least / len(split), high / len(split))
        gain = gain * jnp.repeat(jnp.exp(heights), extent[axis_at] // blocks).reshape((-1,) + (1,) * (len(extent) - 1 - axis_at))
    return gain


def normal_values(rng, shape, scale, most, pieces=(), held_as=jnp.bfloat16):
    values = scale * jax.random.normal(rng, shape, jnp.float32)
    if pieces:
        values = values * block_scale(rng, shape, pieces, -0.22, 0.18)
    return jnp.clip(values, -most, most).astype(held_as)


def setup_inputs(seed: int = 0) -> dict:
    arg_keys = jax.random.split(jax.random.key(seed), 9)
    return {
        "hidden_in": draw_hidden_in(jax.random.fold_in(arg_keys[8], 71), 0),
        "norm_gain": jnp.clip(1.0 + 0.18 * jax.random.normal(arg_keys[1], (D,), jnp.float32), 0.099609375, 1.8984375).astype(jnp.bfloat16),
        "w_query": draw_w_query(jax.random.fold_in(arg_keys[8], 71), 0),
        "w_key": draw_w_key(jax.random.fold_in(arg_keys[8], 71), 0),
        "w_value": normal_values(arg_keys[4], (D, KVH * HD), D ** -0.5, 0.0625, ((1, 8),)),
        "sign_bits": plant(jax.random.randint(arg_keys[5], (QH, HD), 0, 2), jax.random.fold_in(arg_keys[5], 1), 0, 1).astype(jnp.int32),
        "w_out": draw_w_out(jax.random.fold_in(arg_keys[8], 71), 0),
        "teacher": draw_teacher(jax.random.fold_in(arg_keys[8], 71), 0),
    }


EPS_IN = 1e-05
EPS_OUT = 1e-06
CLIP_RATIO = 0.9

def clip_groups(values):
    lead_shape = values.shape[:-1]
    width = values.shape[-1]
    grouped = values.reshape(lead_shape + (width // GROUP, GROUP))
    limit = CLIP_RATIO * lax.optimization_barrier(jnp.max(jnp.abs(grouped), axis=-1, keepdims=True))
    return jnp.clip(grouped, -limit, limit).reshape(values.shape)

def hadamard(order, dtype):
    index_row = jnp.arange(order, dtype=jnp.int32)
    both_bits = index_row[:, None] & index_row[None, :]
    parity = jnp.zeros_like(both_bits)
    for bit_index in range(max(order - 1, 1).bit_length()):
        parity = parity ^ both_bits >> bit_index & 1
    return (1 - 2 * parity).astype(dtype)

def reference(hidden_in, norm_gain, w_query, w_key, w_value, sign_bits, w_out, teacher):
    inputs = hidden_in.astype(jnp.float32)
    mean_sq = lax.optimization_barrier(jnp.mean(inputs * inputs, axis=-1, keepdims=True))
    normed = inputs * lax.rsqrt(mean_sq + EPS_IN) * norm_gain.astype(jnp.float32)
    quantized = clip_groups(normed).astype(jnp.bfloat16)
    queries = jnp.dot(quantized, w_query, preferred_element_type=jnp.float32).astype(jnp.bfloat16)
    keys_all = jnp.dot(quantized, w_key, preferred_element_type=jnp.float32).astype(jnp.bfloat16)
    values_all = jnp.dot(quantized, w_value, preferred_element_type=jnp.float32).astype(jnp.bfloat16)
    group_size = QH // KVH
    block_count = SEQ // TOK_DEV
    positions = jnp.arange(SEQ, dtype=jnp.int32)
    score_scale = HD ** (-0.5)

    def one_head(head):
        kv_head = head // group_size
        head_queries = lax.dynamic_slice_in_dim(queries, head * HD, HD, 1)
        head_keys = lax.dynamic_slice_in_dim(keys_all, kv_head * HD, HD, 1)
        head_values = lax.dynamic_slice_in_dim(values_all, kv_head * HD, HD, 1)

        def one_block(block):
            block_queries = lax.dynamic_slice_in_dim(head_queries, block * TOK_DEV, TOK_DEV, 0)
            query_pos = block * TOK_DEV + jnp.arange(TOK_DEV, dtype=jnp.int32)
            scores = jnp.dot(block_queries, head_keys.T, preferred_element_type=jnp.float32) * score_scale
            causal = positions[None, :] <= query_pos[:, None]
            masked = jnp.where(causal, scores, -jnp.inf)
            highest = lax.optimization_barrier(jnp.max(masked, axis=-1, keepdims=True))
            weights = jnp.where(causal, jnp.exp(scores - highest), 0.0)
            total = lax.optimization_barrier(jnp.sum(weights, axis=-1, keepdims=True))
            mixed = jnp.dot(weights.astype(jnp.bfloat16), head_values, preferred_element_type=jnp.float32)
            return mixed / total
        return lax.map(one_block, jnp.arange(block_count, dtype=jnp.int32))
    per_head = lax.map(one_head, jnp.arange(QH, dtype=jnp.int32))
    attended = per_head.reshape(QH, SEQ, HD).transpose(1, 0, 2).astype(jnp.bfloat16)
    signs = (2 * sign_bits - 1).astype(jnp.float32)
    signed = attended.astype(jnp.float32) * signs[None, :, :]
    mixing = hadamard(QH, jnp.float32)
    rotated = jnp.einsum('hg,sgd->shd', mixing, signed, precision=lax.Precision.HIGHEST) * QH ** (-0.5)
    rotated_q = clip_groups(rotated.reshape(SEQ, QH * HD)).astype(jnp.bfloat16)
    branch = jnp.dot(rotated_q, w_out, preferred_element_type=jnp.float32)
    inverse = lax.rsqrt(lax.optimization_barrier(jnp.mean(branch * branch, axis=-1, keepdims=True)) + EPS_OUT)
    normal_rows = branch * inverse
    difference = normal_rows - teacher.astype(jnp.float32)
    row_loss = lax.optimization_barrier(jnp.mean(difference * difference, axis=-1))
    return (normal_rows.astype(jnp.bfloat16), row_loss)
```

```python
import functools
import math

import jax
import jax.numpy as jnp
from jax import lax
from jax.experimental import pallas as pl
from jax.experimental.pallas import tpu as pltpu
from jax.sharding import PartitionSpec as P

HD = 128
GROUP = 128
EPS_IN = 1e-05
EPS_OUT = 1e-06
CLIP_RATIO = 0.9
FAR_BELOW = -1e30
LOG2E = math.log2(math.e)
VMEM_BYTES = 48 * 1024 * 1024

CHUNK_ROWS = 128
PROJ_ROWS = 256
ATT_ROWS = 128
OUT_ROWS = 128


def params(**kw):
    return pltpu.CompilerParams(vmem_limit_bytes=VMEM_BYTES, **kw)


def whole(shape):
    zeros = (0,) * len(shape)
    return pl.BlockSpec(shape, lambda *_: zeros)


def cost(flops, moved, trans=0):
    return pl.CostEstimate(flops=int(flops), bytes_accessed=int(moved), transcendentals=int(trans))


def clip_tile(v):
    limit = CLIP_RATIO * jnp.max(jnp.abs(v), axis=-1, keepdims=True)
    return jnp.clip(v, -limit, limit)


def to_lanes(column):
    rows = column.shape[0]
    return jnp.transpose(jnp.broadcast_to(column, (rows, 128)))[:8]


def pre_kernel(h_ref, g_ref, c_ref, s_ref):
    rows, width = h_ref.shape
    total = jnp.zeros((rows, GROUP), jnp.float32)
    for at in range(0, width, GROUP):
        h = h_ref[:, at : at + GROUP].astype(jnp.float32)
        total = total + h * h
        v = h * g_ref[:, at : at + GROUP].astype(jnp.float32)
        c_ref[:, at : at + GROUP] = clip_tile(v).astype(jnp.bfloat16)
    s_ref[...] = to_lanes(jnp.sum(total, axis=-1, keepdims=True))


def pre(hidden, gain, chunk, rows):
    width = hidden.shape[1]
    return pl.pallas_call(
        pre_kernel,
        grid=(1,),
        in_specs=[pl.BlockSpec((rows, width), lambda i: (chunk, 0)), whole((1, width))],
        out_specs=[whole((rows, width)), whole((8, rows))],
        out_shape=[
            jax.ShapeDtypeStruct((rows, width), jnp.bfloat16),
            jax.ShapeDtypeStruct((8, rows), jnp.float32),
        ],
        compiler_params=params(),
        cost_estimate=cost(8 * rows * width, 4 * rows * width),
        name="pre",
    )(hidden, gain)


def proj_kernel(depth, pieces, order_ref, *refs):
    blocks = refs[: pieces * depth]
    wq_ref, wk_ref, wv_ref, ss_ref, q_ref, kv_ref, accq, acck, accv = refs[pieces * depth :]
    step = pl.program_id(0)
    for at in range(depth):

        @pl.when(step == at)
        def _():
            mine = [blocks[at * pieces + p][...] for p in range(pieces)]
            lhs = mine[0] if pieces == 1 else jnp.concatenate(mine, axis=0)
            for w_ref, acc in ((wq_ref, accq), (wk_ref, acck), (wv_ref, accv)):
                part = jnp.dot(lhs, w_ref[...], preferred_element_type=jnp.float32)
                if at == 0:
                    acc[...] = part
                else:
                    acc[...] += part

    @pl.when(step == depth - 1)
    def _():
        features = wq_ref.shape[0] * depth
        inverse = lax.rsqrt(ss_ref[...] * (1.0 / features) + EPS_IN)
        scale = jnp.transpose(inverse)[:, :1]
        kcols = wk_ref.shape[1]
        q_ref[...] = (accq[...] * scale).astype(jnp.bfloat16)
        kv_ref[:, :kcols] = (acck[...] * scale).astype(jnp.bfloat16)
        kv_ref[:, kcols:] = (accv[...] * scale).astype(jnp.bfloat16)


def proj(order, blocks, pieces, wq, wk, wv, squares):
    depth = len(blocks) // pieces
    part_rows, part_cols = blocks[0].shape
    rows = part_rows * pieces
    nq, nk, nv = wq.shape[1], wk.shape[1], wv.shape[1]
    weight = lambda n: pl.BlockSpec((part_cols, n), lambda k, order: (order[k], 0))
    spec = pltpu.PrefetchScalarGridSpec(
        num_scalar_prefetch=1,
        grid=(depth,),
        in_specs=[whole((part_rows, part_cols))] * len(blocks)
        + [weight(nq), weight(nk), weight(nv), whole((8, rows))],
        out_specs=[whole((rows, nq)), whole((rows, nk + nv))],
        scratch_shapes=[pltpu.VMEM((rows, n), jnp.float32) for n in (nq, nk, nv)],
    )
    n = nq + nk + nv
    return pl.pallas_call(
        functools.partial(proj_kernel, depth, pieces),
        grid_spec=spec,
        out_shape=[
            jax.ShapeDtypeStruct((rows, nq), jnp.bfloat16),
            jax.ShapeDtypeStruct((rows, nk + nv), jnp.bfloat16),
        ],
        compiler_params=params(),
        cost_estimate=cost(
            2 * rows * part_cols * depth * n, 2 * part_cols * depth * (rows + n)
        ),
        name="proj",
    )(order, *blocks, wq, wk, wv, squares)


def att_kernel(first, heads, kv_heads, hops, pieces, me_ref, q_ref, sign_ref, *refs):
    kvs = refs[: pieces * (hops + 1)]
    o_ref, high, total, accum = refs[pieces * (hops + 1) :]
    rows = q_ref.shape[0]
    part = kvs[0].shape[0]
    group = heads // kv_heads
    scale = HD ** (-0.5) * LOG2E

    def visit(kv_ref, start, fresh):
        masked = start is not None and start + part > first
        for head in range(heads):
            kv = head // group
            q = q_ref[:, head * HD : (head + 1) * HD]
            k = kv_ref[:, kv * HD : (kv + 1) * HD]
            v = kv_ref[:, (kv_heads + kv) * HD : (kv_heads + kv + 1) * HD]
            s = lax.dot_general(
                q, k, (((1,), (1,)), ((), ())), preferred_element_type=jnp.float32
            )
            if masked:
                qpos = first + lax.broadcasted_iota(jnp.int32, s.shape, 0)
                kpos = start + lax.broadcasted_iota(jnp.int32, s.shape, 1)
                s = jnp.where(kpos <= qpos, s, FAR_BELOW)
            best = jnp.max(s, axis=-1, keepdims=True)
            if not fresh:
                before = high[head]
                best = jnp.maximum(best, before[:, :1])
            w = jnp.exp2((s - best) * scale)
            sums = w[:, :HD]
            for at in range(HD, part, HD):
                sums = sums + w[:, at : at + HD]
            mixed = jnp.dot(w.astype(jnp.bfloat16), v, preferred_element_type=jnp.float32)
            if fresh:
                total[head] = sums
                accum[head] = mixed
            else:
                decay = jnp.exp2((before[:, :1] - best) * scale)
                total[head] = total[head] * decay + sums
                accum[head] = accum[head] * decay + mixed
            high[head] = jnp.broadcast_to(best, (rows, HD))

    order = [p for p in range(pieces) if p * part < first + rows]
    for at, p in enumerate(order):
        visit(kvs[p], p * part, at == 0)
    for hop in range(1, hops + 1):

        @pl.when(me_ref[0] >= hop)
        def _():
            for p in range(pieces):
                visit(kvs[hop * pieces + p], None, False)

    for head in range(heads):
        bottom = jnp.sum(total[head], axis=-1, keepdims=True)
        att = (accum[head] / bottom).astype(jnp.bfloat16).astype(jnp.float32)
        o_ref[:, head * HD : (head + 1) * HD] = (att * sign_ref[head : head + 1, :]).astype(
            jnp.bfloat16
        )


def attend(me, q, at, rows, signs, kvs, pieces, kv_heads):
    heads = q.shape[1] // HD
    hops = len(kvs) // pieces - 1
    first = at
    block = (at % q.shape[0]) // rows
    spec = pltpu.PrefetchScalarGridSpec(
        num_scalar_prefetch=1,
        grid=(1,),
        in_specs=[
            pl.BlockSpec((rows, heads * HD), lambda i, me: (block, 0)),
            whole((heads, HD)),
        ]
        + [whole(kv.shape) for kv in kvs],
        out_specs=whole((rows, heads * HD)),
        scratch_shapes=[pltpu.VMEM((heads, rows, HD), jnp.float32)] * 3,
    )
    keys = sum(kv.shape[0] for kv in kvs)
    return pl.pallas_call(
        functools.partial(att_kernel, first, heads, kv_heads, hops, pieces),
        grid_spec=spec,
        out_shape=jax.ShapeDtypeStruct((rows, heads * HD), jnp.bfloat16),
        compiler_params=params(),
        cost_estimate=cost(4 * rows * keys * heads * HD, 4 * keys * HD, rows * keys * heads),
        name="attend",
    )(me, q, signs, *kvs)


def butterfly(tiles):
    count = len(tiles)
    span = 1
    while span < count:
        out = list(tiles)
        for at in range(count):
            if not at & span:
                a, b = tiles[at], tiles[at | span]
                out[at], out[at | span] = a + b, a - b
        tiles = out
        span *= 2
    return tiles


def out_kernel(parts, steps, sign_ref, *refs):
    blocks = refs[:parts]
    w_ref, t_ref, b_ref, s_ref, rot, acc = refs[parts:]
    step = pl.program_id(0)
    rows, width = blocks[0].shape
    here = width // HD
    heads = here * parts
    factor = heads ** (-0.5)

    @pl.when(step == 0)
    def _():
        strip = 16

        def turn(i, carry):
            at = pl.ds(pl.multiple_of(i * strip, strip), strip)
            tiles = []
            for m in range(parts):
                for h in range(here):
                    tiles.append(blocks[m][at, h * HD : (h + 1) * HD].astype(jnp.float32))
            tiles = butterfly(tiles)
            for h in range(heads):
                v = tiles[h] * (factor * sign_ref[h // here])
                rot[at, h * HD : (h + 1) * HD] = clip_tile(v).astype(jnp.bfloat16)
            return carry

        lax.fori_loop(0, rows // strip, turn, 0)

    depth = w_ref.shape[0]
    for at in range(steps):

        @pl.when(step == at)
        def _():
            part = jnp.dot(
                rot[:, at * depth : (at + 1) * depth],
                w_ref[...],
                preferred_element_type=jnp.float32,
            )
            if at == 0:
                acc[...] = part
            else:
                acc[...] += part

    @pl.when(step == steps - 1)
    def _():
        b = acc[...]
        t = t_ref[...].astype(jnp.float32)
        b_ref[...] = b
        sums = [jnp.sum(v, axis=-1, keepdims=True) for v in (b * b, b * t, t * t)]
        lane = lax.broadcasted_iota(jnp.int32, (rows, 128), 1)
        wide = jnp.where(lane == 0, sums[0], jnp.where(lane == 1, sums[1], sums[2]))
        s_ref[...] = jnp.transpose(wide)[:8]


def project_out(flips, blocks, w_out, teacher, chunk):
    parts = len(blocks)
    rows, width = blocks[0].shape
    depth = w_out.shape[0]
    cols = w_out.shape[1]
    steps = 4
    spec = pltpu.PrefetchScalarGridSpec(
        num_scalar_prefetch=1,
        grid=(steps,),
        in_specs=[whole((rows, width))] * parts
        + [
            pl.BlockSpec((depth // steps, cols), lambda k, f: (k, 0)),
            pl.BlockSpec((rows, cols), lambda k, f: (chunk, 0)),
        ],
        out_specs=[whole((rows, cols)), whole((8, rows))],
        scratch_shapes=[
            pltpu.VMEM((rows, depth), jnp.bfloat16),
            pltpu.VMEM((rows, cols), jnp.float32),
        ],
    )
    return pl.pallas_call(
        functools.partial(out_kernel, parts, steps),
        grid_spec=spec,
        out_shape=[
            jax.ShapeDtypeStruct((rows, cols), jnp.float32),
            jax.ShapeDtypeStruct((8, rows), jnp.float32),
        ],
        compiler_params=params(),
        cost_estimate=cost(2 * rows * depth * cols, 2 * depth * (rows + cols) + 6 * rows * cols),
        name="project_out",
    )(flips, *blocks, w_out, teacher)


def final_kernel(features, chunks, parts, *refs):
    branches, stats = refs[:chunks], refs[chunks : chunks + parts]
    student_ref, loss_ref = refs[chunks + parts :]
    total = stats[0][...]
    for at in range(1, parts):
        total = total + stats[at][...]
    inverse = lax.rsqrt(total[0:1] * (1.0 / features) + EPS_OUT)
    loss = inverse * inverse * total[0:1] - 2.0 * inverse * total[1:2] + total[2:3]
    loss_ref[...] = jnp.maximum(loss, 0.0) * (1.0 / features)
    column = jnp.transpose(jnp.broadcast_to(inverse, total.shape))[:, :1]
    rows = branches[0].shape[0]
    for at in range(chunks):
        scale = column[at * rows : (at + 1) * rows]
        student_ref[at * rows : (at + 1) * rows, :] = (branches[at][...] * scale).astype(
            jnp.bfloat16
        )


def final(features, branches, stats):
    chunks, parts = len(branches), len(stats)
    part_rows, cols = branches[0].shape
    rows = part_rows * chunks
    return pl.pallas_call(
        functools.partial(final_kernel, features, chunks, parts),
        grid=(1,),
        in_specs=[whole((part_rows, cols))] * chunks + [whole((8, rows))] * parts,
        out_specs=[whole((rows, cols)), whole((1, rows))],
        out_shape=[
            jax.ShapeDtypeStruct((rows, cols), jnp.bfloat16),
            jax.ShapeDtypeStruct((1, rows), jnp.float32),
        ],
        compiler_params=params(),
        cost_estimate=cost(2 * rows * cols, 6 * rows * cols),
        name="final",
    )(*branches, *stats)


def swap(x, mask):
    count = lax.axis_size("tp")
    return lax.ppermute(x, "tp", [(i, i ^ mask) for i in range(count)])


def up(x):
    count = lax.axis_size("ctx")
    return lax.ppermute(x, "ctx", [(i, i + 1) for i in range(count - 1)])


def gather(own, odd):
    count = lax.axis_size("tp")
    got = {0: own}
    masks = [1 << b for b in range(1, count.bit_length() - 1)]
    if len(masks) >= 2:
        a, b = (masks[1], masks[0]) if odd else (masks[0], masks[1])
        got[a] = swap(own, a)
        got[b] = swap(own, b)
        got[a | b] = swap(got[a], b)
        masks = masks[2:]
    if count > 1:
        for m in list(got):
            got[m | 1] = swap(got[m], 1)
    for mask in masks:
        for m in list(got):
            got[m | mask] = swap(got[m], mask)
    return [got[m] for m in range(count)]


def body(hidden_in, norm_gain, w_query, w_key, w_value, sign_bits, w_out, teacher):
    rows = hidden_in.shape[0]
    tp_count = lax.axis_size("tp")
    ctx_count = lax.axis_size("ctx")
    features = hidden_in.shape[1] * tp_count
    tp_at = lax.axis_index("tp")
    ctx_at = jnp.reshape(lax.axis_index("ctx"), (1,)).astype(jnp.int32)
    masks = jnp.arange(tp_count, dtype=jnp.int32)
    order = tp_at ^ masks
    shared = tp_at & masks
    parity = jnp.zeros_like(shared)
    for bit in range(tp_count.bit_length()):
        parity = parity ^ (shared >> bit & 1)
    flips = (1 - 2 * parity).astype(jnp.float32)
    signs = (2 * sign_bits - 1).astype(jnp.float32)
    gain = norm_gain.reshape(1, -1)

    chunks = [pre(hidden_in, gain, i, CHUNK_ROWS) for i in range(rows // CHUNK_ROWS)]
    clipped = [c for c, _ in chunks]
    squares = jnp.concatenate([s for _, s in chunks], axis=1)
    for bit in range(tp_count.bit_length() - 1):
        squares = squares + swap(squares, 1 << bit)

    gathered = [gather(c, i % 2) for i, c in enumerate(clipped)]

    kv_cols = w_key.shape[1]
    sharing = HD // kv_cols if kv_cols < HD else 1
    kv_heads = kv_cols * sharing // HD
    pieces = PROJ_ROWS // CHUNK_ROWS
    queries, own_kv = [], []
    for at in range(rows // PROJ_ROWS):
        mine = gathered[at * pieces : (at + 1) * pieces]
        blocks = [mine[p][m] for m in range(tp_count) for p in range(pieces)]
        part = squares[:, at * PROJ_ROWS : (at + 1) * PROJ_ROWS]
        q, kv = proj(order, blocks, pieces, w_query, w_key, w_value, part)
        if sharing > 1:
            k, v = kv[:, :kv_cols], kv[:, kv_cols:]
            for bit in range(sharing.bit_length() - 1):
                upper = tp_at >> bit & 1 == 1
                k2, v2 = swap(k, 1 << bit), swap(v, 1 << bit)
                k, v = (
                    jnp.where(
                        upper,
                        jnp.concatenate([far, near], axis=1),
                        jnp.concatenate([near, far], axis=1),
                    )
                    for near, far in ((k, k2), (v, v2))
                )
            kv = jnp.concatenate([k, v], axis=1)
        queries.append(q)
        own_kv.append(kv)
    kvs = list(own_kv)
    for kv_hop in range(1, ctx_count):
        kvs += [up(kv) for kv in kvs[-len(own_kv) :]]

    branches, stats = [], []
    for at in range(0, rows, ATT_ROWS):
        q = queries[at // PROJ_ROWS]
        signed = attend(ctx_at, q, at, ATT_ROWS, signs, kvs, len(own_kv), kv_heads)
        blocks = gather(signed, (at // ATT_ROWS) % 2)
        b, s = project_out(flips, blocks, w_out, teacher, at // ATT_ROWS)
        branches.append(b)
        stats.append(s)
    stat = jnp.concatenate(stats, axis=1)
    totals = [stat] + [swap(stat, m) for m in range(1, tp_count)]
    student, loss = final(features, branches, totals)
    return student, loss.reshape(rows)


def solution(mesh):
    in_specs = (
        P("ctx", "tp"),
        P("tp"),
        P(None, "tp"),
        P(None, "tp"),
        P(None, "tp"),
        P("tp", None),
        P(None, "tp"),
        P("ctx", "tp"),
    )
    out_specs = (P("ctx", "tp"), P("ctx"))
    return jax.shard_map(body, mesh=mesh, in_specs=in_specs, out_specs=out_specs, check_vma=False)
```

```python
import functools
import math

import jax
import jax.numpy as jnp
from jax import lax
from jax.experimental import pallas as pl
from jax.experimental.pallas import tpu as pltpu
from jax.sharding import PartitionSpec as P

HD = 128
GROUP = 128
EPS_IN = 1e-05
EPS_OUT = 1e-06
CLIP_RATIO = 0.9
FAR_BELOW = -1e30
LOG2E = math.log2(math.e)
HALVES = 2
MIB = 1024 * 1024


def params(mib, **kw):
    return pltpu.CompilerParams(vmem_limit_bytes=mib * MIB, **kw)


def whole(shape):
    zeros = (0,) * len(shape)
    return pl.BlockSpec(shape, lambda *_: zeros)


IN_SMEM = pl.BlockSpec(memory_space=pltpu.SMEM)
IN_VMEM = pl.BlockSpec(memory_space=pltpu.VMEM)
ANYWHERE = pl.BlockSpec(memory_space=pl.ANY)


def cost(flops, moved, trans=0):
    return pl.CostEstimate(flops=int(flops), bytes_accessed=int(moved), transcendentals=int(trans))


def clip_tile(v):
    limit = CLIP_RATIO * jnp.max(jnp.abs(v), axis=-1, keepdims=True)
    return jnp.clip(v, -limit, limit)


def to_lanes(column):
    rows = column.shape[0]
    return jnp.transpose(jnp.broadcast_to(column, (rows, 128)))[:8]


def pre_kernel(h_ref, g_ref, c_ref, s_ref):
    rows, width = h_ref.shape
    total = jnp.zeros((rows, GROUP), jnp.float32)
    for at in range(0, width, GROUP):
        h = h_ref[:, at : at + GROUP].astype(jnp.float32)
        total = total + h * h
        v = h * g_ref[:, at : at + GROUP].astype(jnp.float32)
        c_ref[:, at : at + GROUP] = clip_tile(v).astype(jnp.bfloat16)
    s_ref[...] = to_lanes(jnp.sum(total, axis=-1, keepdims=True))


def pre(hidden, gain, chunk, rows):
    width = hidden.shape[1]
    return pl.pallas_call(
        pre_kernel,
        grid=(1,),
        in_specs=[pl.BlockSpec((rows, width), lambda i: (chunk, 0)), whole((1, width))],
        out_specs=[whole((rows, width)), whole((8, rows))],
        out_shape=[
            jax.ShapeDtypeStruct((rows, width), jnp.bfloat16),
            jax.ShapeDtypeStruct((8, rows), jnp.float32),
        ],
        compiler_params=params(8),
        cost_estimate=cost(8 * rows * width, 4 * rows * width),
        name="pre",
    )(hidden, gain)


def proj_kernel(counts, joined, order_ref, ss_ref, *refs):
    depth = len(counts)
    blocks = refs[: sum(counts)]
    wq_hbm, wk_hbm, wv_hbm, q_ref, kv_ref, lhs, *rest = refs[sum(counts) :]
    nq, nk, nv = wq_hbm.shape[1], wk_hbm.shape[1], wv_hbm.shape[1]
    k_rows = lhs.shape[2]
    if joined:
        w_all, acc, wsem, lsem = rest
    else:
        wq_all, wk_all, wv_all, accq, acck, accv, wsem, lsem = rest

    def weight_copies(k):
        at = pl.ds(pl.multiple_of(order_ref[k] * k_rows, k_rows), k_rows)
        if joined:
            goals = (
                w_all.at[k, :, :nq],
                w_all.at[k, :, nq : nq + nk],
                w_all.at[k, :, nq + nk : nq + nk + nv],
            )
        else:
            goals = (wq_all.at[k], wk_all.at[k], wv_all.at[k])
        return [
            pltpu.make_async_copy(src.at[at], goal, wsem.at[k, i])
            for i, (src, goal) in enumerate(zip((wq_hbm, wk_hbm, wv_hbm), goals))
        ]

    copies = []
    at_block = 0
    for k in range(depth):
        mine = weight_copies(k)
        row = 0
        for p in range(counts[k]):
            block = blocks[at_block]
            at_block += 1
            rows = block.shape[0]
            mine.append(
                pltpu.make_async_copy(block, lhs.at[k, row : row + rows], lsem.at[k, p])
            )
            row += rows
        for copy in mine:
            copy.start()
        copies.append(mine)
    for k in range(depth):
        for copy in copies[k]:
            copy.wait()
        left = lhs[k]
        if joined:
            pairs = ((w_all, acc),)
        else:
            pairs = ((wq_all, accq), (wk_all, acck), (wv_all, accv))
        for w, total in pairs:
            part = jnp.dot(left, w[k], preferred_element_type=jnp.float32)
            if k == 0:
                total[...] = part
            else:
                total[...] += part

    features = k_rows * depth
    inverse = lax.rsqrt(ss_ref[...] * (1.0 / features) + EPS_IN)
    scale = jnp.transpose(inverse)[:, :1]
    if joined:
        q_ref[...] = (acc[:, :nq] * scale).astype(jnp.bfloat16)
        kv_ref[...] = (acc[:, nq:] * scale).astype(jnp.bfloat16)
    else:
        q_ref[...] = (accq[...] * scale).astype(jnp.bfloat16)
        kv_ref[:, :nk] = (acck[...] * scale).astype(jnp.bfloat16)
        kv_ref[:, nk:] = (accv[...] * scale).astype(jnp.bfloat16)


def proj(order, blocks, wq, wk, wv, squares):
    depth = len(blocks)
    counts = [len(b) for b in blocks]
    rows = squares.shape[1]
    part_cols = blocks[0][0].shape[1]
    nq, nk, nv = wq.shape[1], wk.shape[1], wv.shape[1]
    n = nq + nk + nv
    joined = nk % 128 == 0
    sizes = [n] if joined else [nq, nk, nv]
    scratch = [pltpu.VMEM((depth, rows, part_cols), jnp.bfloat16)]
    scratch += [pltpu.VMEM((depth, part_cols, m), jnp.bfloat16) for m in sizes]
    scratch += [pltpu.VMEM((rows, m), jnp.float32) for m in sizes]
    scratch += [pltpu.SemaphoreType.DMA((depth, 3)), pltpu.SemaphoreType.DMA((depth, 2))]
    flat = [p for b in blocks for p in b]
    return pl.pallas_call(
        functools.partial(proj_kernel, counts, joined),
        in_specs=[IN_SMEM, IN_VMEM] + [ANYWHERE] * (len(flat) + 3),
        out_specs=[IN_VMEM, IN_VMEM],
        out_shape=[
            jax.ShapeDtypeStruct((rows, nq), jnp.bfloat16),
            jax.ShapeDtypeStruct((rows, nk + nv), jnp.bfloat16),
        ],
        scratch_shapes=scratch,
        compiler_params=params(24),
        cost_estimate=cost(
            2 * rows * part_cols * depth * n, 2 * part_cols * depth * (rows + n)
        ),
        name="proj",
    )(order, squares, *flat, wq, wk, wv)


def att_kernel(first, heads, kv_heads, hops, pieces, me_ref, q_ref, sign_ref, *refs):
    kvs = refs[: pieces * (hops + 1)]
    o_ref, high, total, accum = refs[pieces * (hops + 1) :]
    rows = q_ref.shape[0]
    part = kvs[0].shape[0]
    group = heads // kv_heads
    scale = HD ** (-0.5) * LOG2E

    def visit(kv_ref, start, fresh):
        masked = start is not None and start + part > first
        scores, turned = [], []
        for kv in range(kv_heads):
            at = (kv_heads + kv) * HD
            turned.append(jnp.transpose(kv_ref[:, at : at + HD]))
        for head in range(heads):
            kv = head // group
            q = q_ref[:, head * HD : (head + 1) * HD]
            k = kv_ref[:, kv * HD : (kv + 1) * HD]
            s = lax.dot_general(
                k, q, (((1,), (1,)), ((), ())), preferred_element_type=jnp.float32
            )
            if masked:
                kpos = start + lax.broadcasted_iota(jnp.int32, s.shape, 0)
                qpos = first + lax.broadcasted_iota(jnp.int32, s.shape, 1)
                s = jnp.where(kpos <= qpos, s, FAR_BELOW)
            scores.append(s)
        for head in range(heads):
            s = scores[head]
            best = jnp.max(s, axis=0, keepdims=True)
            if not fresh:
                before = high[head : head + 1]
                best = jnp.maximum(best, before)
            w = jnp.exp2((s - best) * scale)
            sums = jnp.sum(w, axis=0, keepdims=True)
            mixed = jnp.dot(
                turned[head // group], w.astype(jnp.bfloat16), preferred_element_type=jnp.float32
            )
            if fresh:
                total[head : head + 1] = sums
                accum[head] = mixed
            else:
                decay = jnp.exp2((before - best) * scale)
                total[head : head + 1] = total[head : head + 1] * decay + sums
                accum[head] = accum[head] * decay + mixed
            high[head : head + 1] = best

    near = [p for p in range(pieces) if p * part < first + rows]
    for at, p in enumerate(near):
        visit(kvs[p], p * part, at == 0)
    for hop in range(1, hops + 1):

        @pl.when(me_ref[0] >= hop)
        def _():
            for p in range(pieces):
                visit(kvs[hop * pieces + p], None, False)

    for head in range(heads):
        att = jnp.transpose(accum[head] / total[head : head + 1])
        att = att.astype(jnp.bfloat16).astype(jnp.float32)
        o_ref[:, head * HD : (head + 1) * HD] = (att * sign_ref[head : head + 1, :]).astype(
            jnp.bfloat16
        )


def attend(me, q, first, signs, kvs, pieces, kv_heads):
    rows = q.shape[0]
    heads = q.shape[1] // HD
    hops = len(kvs) // pieces - 1
    keys = sum(kv.shape[0] for kv in kvs)
    return pl.pallas_call(
        functools.partial(att_kernel, first, heads, kv_heads, hops, pieces),
        in_specs=[IN_SMEM] + [IN_VMEM] * (len(kvs) + 2),
        out_specs=IN_VMEM,
        out_shape=jax.ShapeDtypeStruct((rows, heads * HD), jnp.bfloat16),
        scratch_shapes=[
            pltpu.VMEM((max(heads, 8), rows), jnp.float32),
            pltpu.VMEM((max(heads, 8), rows), jnp.float32),
            pltpu.VMEM((heads, HD, rows), jnp.float32),
        ],
        compiler_params=params(20),
        cost_estimate=cost(4 * rows * keys * heads * HD, 4 * keys * HD, rows * keys * heads),
        name="attend",
    )(me, q, signs, *kvs)


def butterfly(tiles):
    count = len(tiles)
    span = 1
    while span < count:
        out = list(tiles)
        for at in range(count):
            if not at & span:
                a, b = tiles[at], tiles[at | span]
                out[at], out[at | span] = a + b, a - b
        tiles = out
        span *= 2
    return tiles


def out_kernel(counts, steps, sign_ref, t_ref, *refs):
    parts = len(counts)
    blocks, at_block = [], 0
    for n in counts:
        blocks.append(refs[at_block : at_block + n])
        at_block += n
    w_hbm, b_ref, s_ref, w_all, mid, rot, acc, wsem = refs[at_block:]
    rows = b_ref.shape[0]
    width = blocks[0][0].shape[1]
    here = width // HD
    heads = here * parts
    factor = heads ** (-0.5)
    depth = w_hbm.shape[0] // steps
    copies = [
        pltpu.make_async_copy(
            w_hbm.at[i * depth : (i + 1) * depth],
            w_all.at[i * depth : (i + 1) * depth],
            wsem.at[i],
        )
        for i in range(steps)
    ]
    for copy in copies:
        copy.start()

    strip = 16
    most = max(counts)
    span = rows // most
    for section in range(most):

        def turn(i, carry):
            at = pl.multiple_of(section * span + i * strip, strip)
            for m in range(parts):
                if len(blocks[m]) == 1:
                    ref, start = blocks[m][0], at
                else:
                    ref, start = blocks[m][section], pl.multiple_of(i * strip, strip)
                tiles = [
                    ref[pl.ds(start, strip), h * HD : (h + 1) * HD].astype(jnp.float32)
                    for h in range(here)
                ]
                for h, v in enumerate(butterfly(tiles)):
                    mid[m * here + h] = v
            for h in range(here):
                tiles = butterfly([mid[m * here + h] for m in range(parts)])
                for m in range(parts):
                    v = tiles[m] * (factor * sign_ref[m])
                    col = (m * here + h) * HD
                    rot[pl.ds(at, strip), col : col + HD] = clip_tile(v).astype(jnp.bfloat16)
            return carry

        lax.fori_loop(0, span // strip, turn, 0)

    for i in range(steps):
        copies[i].wait()
        part = jnp.dot(
            rot[:, i * depth : (i + 1) * depth],
            w_all[i * depth : (i + 1) * depth, :],
            preferred_element_type=jnp.float32,
        )
        if i == 0:
            acc[...] = part
        else:
            acc[...] += part

    b = acc[...]
    t = t_ref[...].astype(jnp.float32)
    b_ref[...] = b
    sums = [jnp.sum(v, axis=-1, keepdims=True) for v in (b * b, b * t, t * t)]
    lane = lax.broadcasted_iota(jnp.int32, (rows, 128), 1)
    wide = jnp.where(lane == 0, sums[0], jnp.where(lane == 1, sums[1], sums[2]))
    s_ref[...] = jnp.transpose(wide)[:8]


def project_out(flips, blocks, w_out, teacher, chunk):
    parts = len(blocks)
    counts = [len(b) for b in blocks]
    rows, width = blocks[0][0].shape
    depth, cols = w_out.shape
    steps = 4
    flat = [p for b in blocks for p in b]
    return pl.pallas_call(
        functools.partial(out_kernel, counts, steps),
        grid=(1,),
        in_specs=[IN_SMEM, pl.BlockSpec((rows, cols), lambda i: (chunk, 0))]
        + [whole(p.shape) for p in flat]
        + [ANYWHERE],
        out_specs=[whole((rows, cols)), whole((8, rows))],
        out_shape=[
            jax.ShapeDtypeStruct((rows, cols), jnp.float32),
            jax.ShapeDtypeStruct((8, rows), jnp.float32),
        ],
        scratch_shapes=[
            pltpu.VMEM((depth, cols), jnp.bfloat16),
            pltpu.VMEM((parts * width // HD, 16, HD), jnp.float32),
            pltpu.VMEM((rows, depth), jnp.bfloat16),
            pltpu.VMEM((rows, cols), jnp.float32),
            pltpu.SemaphoreType.DMA((steps,)),
        ],
        compiler_params=params(24),
        cost_estimate=cost(2 * rows * depth * cols, 2 * depth * (rows + cols) + 6 * rows * cols),
        name="project_out",
    )(flips, teacher, *flat, w_out)


def final_kernel(features, chunks, parts, *refs):
    branches, stats = refs[:chunks], refs[chunks : chunks + parts]
    student_ref, loss_ref = refs[chunks + parts :]
    total = stats[0][...]
    for at in range(1, parts):
        total = total + stats[at][...]
    inverse = lax.rsqrt(total[0:1] * (1.0 / features) + EPS_OUT)
    loss = inverse * inverse * total[0:1] - 2.0 * inverse * total[1:2] + total[2:3]
    loss_ref[...] = jnp.maximum(loss, 0.0) * (1.0 / features)
    column = jnp.transpose(jnp.broadcast_to(inverse, total.shape))[:, :1]
    rows = branches[0].shape[0]
    for at in range(chunks):
        scale = column[at * rows : (at + 1) * rows]
        student_ref[at * rows : (at + 1) * rows, :] = (branches[at][...] * scale).astype(
            jnp.bfloat16
        )


def final(features, branches, stats):
    chunks, parts = len(branches), len(stats)
    part_rows, cols = branches[0].shape
    rows = part_rows * chunks
    return pl.pallas_call(
        functools.partial(final_kernel, features, chunks, parts),
        grid=(1,),
        in_specs=[whole((part_rows, cols))] * chunks + [whole((8, rows))] * parts,
        out_specs=[whole((rows, cols)), whole((1, rows))],
        out_shape=[
            jax.ShapeDtypeStruct((rows, cols), jnp.bfloat16),
            jax.ShapeDtypeStruct((1, rows), jnp.float32),
        ],
        compiler_params=params(16),
        cost_estimate=cost(2 * rows * cols, 6 * rows * cols),
        name="final",
    )(*branches, *stats)


def swap(x, mask):
    count = lax.axis_size("tp")
    return lax.ppermute(x, "tp", [(i, i ^ mask) for i in range(count)])


def send_up(x, distance):
    count = lax.axis_size("ctx")
    return lax.ppermute(x, "ctx", [(i, i + distance) for i in range(count - distance)])


def after(x, *others):
    return lax.optimization_barrier((x,) + others)[0]


def gather(own):
    count = lax.axis_size("tp")
    got = {0: [own]}
    masks = [1 << b for b in range(1, count.bit_length() - 1)]
    if len(masks) >= 2:
        a, b = masks[0], masks[1]
        half = own.shape[0] // 2
        got[a] = [swap(own, a)]
        got[b] = [swap(own, b)]
        got[a | b] = [swap(got[a][0][:half], b), swap(got[b][0][half:], a)]
        masks = masks[2:]
    if count > 1:
        for m in list(got):
            got[m | 1] = [swap(p, 1) for p in got[m]]
    for mask in masks:
        for m in list(got):
            got[m | mask] = [swap(p, mask) for p in got[m]]
    return [got[m] for m in range(count)]


def body(hidden_in, norm_gain, w_query, w_key, w_value, sign_bits, w_out, teacher):
    rows = hidden_in.shape[0]
    half = rows // HALVES
    tp_count = lax.axis_size("tp")
    ctx_count = lax.axis_size("ctx")
    features = hidden_in.shape[1] * tp_count
    tp_at = lax.axis_index("tp")
    ctx_at = jnp.reshape(lax.axis_index("ctx"), (1,)).astype(jnp.int32)
    masks = jnp.arange(tp_count, dtype=jnp.int32)
    order = tp_at ^ masks
    shared = tp_at & masks
    parity = jnp.zeros_like(shared)
    for bit in range(tp_count.bit_length()):
        parity = parity ^ (shared >> bit & 1)
    flips = (1 - 2 * parity).astype(jnp.float32)
    signs = (2 * sign_bits - 1).astype(jnp.float32)
    gain = norm_gain.reshape(1, -1)

    chunks = [pre(hidden_in, gain, i, half) for i in range(HALVES)]
    gathered = []
    for clipped, _ in chunks:
        if gathered:
            clipped = after(clipped, *[b[0] for b in gathered[-1][2:6:2]])
        gathered.append(gather(clipped))
    squares = jnp.concatenate([s for _, s in chunks], axis=1)
    if tp_count > 2:
        squares = after(squares, gathered[0][2][0])
    for bit in range(tp_count.bit_length() - 1):
        squares = squares + swap(squares, 1 << bit)

    kv_cols = w_key.shape[1]
    sharing = HD // kv_cols if kv_cols < HD else 1
    kv_heads = kv_cols * sharing // HD
    queries, kvs = [], []
    for at in range(HALVES):
        part = squares[:, at * half : (at + 1) * half]
        q, kv = proj(order, gathered[at], w_query, w_key, w_value, part)
        if sharing > 1:
            k, v = kv[:, :kv_cols], kv[:, kv_cols:]
            for bit in range(sharing.bit_length() - 1):
                upper = tp_at >> bit & 1 == 1
                k2, v2 = swap(k, 1 << bit), swap(v, 1 << bit)
                k, v = (
                    jnp.where(
                        upper,
                        jnp.concatenate([far, near], axis=1),
                        jnp.concatenate([near, far], axis=1),
                    )
                    for near, far in ((k, k2), (v, v2))
                )
            kv = jnp.concatenate([k, v], axis=1)
        queries.append(q)
        kvs.append([kv] + [send_up(kv, hop) for hop in range(1, ctx_count)])
    kvs = [kvs[p][hop] for hop in range(ctx_count) for p in range(HALVES)]

    branches, stats = [], []
    for at in range(HALVES):
        signed = attend(ctx_at, queries[at], at * half, signs, kvs, HALVES, kv_heads)
        b, s = project_out(flips, gather(signed), w_out, teacher, at)
        branches.append(b)
        stats.append(s)
    stat = jnp.concatenate(stats, axis=1)
    for bit in range(tp_count.bit_length() - 1):
        stat = stat + swap(stat, 1 << bit)
    student, loss = final(features, branches, [stat])
    return student, loss.reshape(rows)


def solution(mesh):
    in_specs = (
        P("ctx", "tp"),
        P("tp"),
        P(None, "tp"),
        P(None, "tp"),
        P(None, "tp"),
        P("tp", None),
        P(None, "tp"),
        P("ctx", "tp"),
    )
    out_specs = (P("ctx", "tp"), P("ctx"))
    return jax.shard_map(body, mesh=mesh, in_specs=in_specs, out_specs=out_specs, check_vma=False)
```

```python
import functools
import math

import jax
import jax.numpy as jnp
from jax import lax
from jax.experimental import pallas as pl
from jax.experimental.pallas import tpu as pltpu
from jax.sharding import PartitionSpec as P

HD = 128
GROUP = 128
EPS_IN = 1e-05
EPS_OUT = 1e-06
CLIP_RATIO = 0.9
FAR_BELOW = -1e30
LOG2E = math.log2(math.e)
HALVES = 2
PROJ_MIB = 12
ATT_MIB = 12
OUT_MIB = 12
MIB = 1024 * 1024


def params(mib, **kw):
    return pltpu.CompilerParams(vmem_limit_bytes=mib * MIB, **kw)


def whole(shape):
    zeros = (0,) * len(shape)
    return pl.BlockSpec(shape, lambda *_: zeros)


IN_SMEM = pl.BlockSpec(memory_space=pltpu.SMEM)
IN_VMEM = pl.BlockSpec(memory_space=pltpu.VMEM)
ANYWHERE = pl.BlockSpec(memory_space=pl.ANY)


def cost(flops, moved, trans=0):
    return pl.CostEstimate(flops=int(flops), bytes_accessed=int(moved), transcendentals=int(trans))


def clip_tile(v):
    limit = CLIP_RATIO * jnp.max(jnp.abs(v), axis=-1, keepdims=True)
    return jnp.clip(v, -limit, limit)


def to_lanes(column):
    rows = column.shape[0]
    return jnp.transpose(jnp.broadcast_to(column, (rows, 128)))[:8]


def pre_kernel(h_ref, g_ref, c_ref, s_ref):
    rows, width = h_ref.shape
    total = jnp.zeros((rows, GROUP), jnp.float32)
    for at in range(0, width, GROUP):
        h = h_ref[:, at : at + GROUP].astype(jnp.float32)
        total = total + h * h
        v = h * g_ref[at // GROUP : at // GROUP + 1, :].astype(jnp.float32)
        c_ref[:, at : at + GROUP] = clip_tile(v).astype(jnp.bfloat16)
    s_ref[...] = to_lanes(jnp.sum(total, axis=-1, keepdims=True))


def pre(hidden, gain, chunk, rows):
    width = hidden.shape[1]
    return pl.pallas_call(
        pre_kernel,
        grid=(1,),
        in_specs=[pl.BlockSpec((rows, width), lambda i: (chunk, 0)), whole(gain.shape)],
        out_specs=[whole((rows, width)), whole((8, rows))],
        out_shape=[
            jax.ShapeDtypeStruct((rows, width), jnp.bfloat16),
            jax.ShapeDtypeStruct((8, rows), jnp.float32),
        ],
        compiler_params=params(8),
        cost_estimate=cost(8 * rows * width, 4 * rows * width),
        name="pre",
    )(hidden, gain)


def proj_kernel(counts, order_ref, ss_ref, *refs):
    depth = len(counts)
    blocks = refs[: sum(counts)]
    wq_ref, wk_ref, wv_ref, q_ref, kv_ref, accq, acck, accv = refs[sum(counts) :]
    nk = wk_ref.shape[1]
    k_rows = blocks[0].shape[1]
    at_block = 0
    for k in range(depth):
        at = pl.ds(pl.multiple_of(order_ref[k] * k_rows, k_rows), k_rows)
        mine = [b[...] for b in blocks[at_block : at_block + counts[k]]]
        at_block += counts[k]
        left = mine[0] if len(mine) == 1 else jnp.concatenate(mine, axis=0)
        wq, wk, wv = wq_ref[at, :], wk_ref[at, :], wv_ref[at, :]
        if nk % 128 == 0:
            both = jnp.dot(
                left, jnp.concatenate([wk, wv], axis=1), preferred_element_type=jnp.float32
            )
            parts = (both[:, :nk], both[:, nk:])
        else:
            parts = [jnp.dot(left, w, preferred_element_type=jnp.float32) for w in (wk, wv)]
        first = jnp.dot(left, wq, preferred_element_type=jnp.float32)
        for part, acc in zip((first, *parts), (accq, acck, accv)):
            if k == 0:
                acc[...] = part
            else:
                acc[...] += part

    features = k_rows * depth
    inverse = lax.rsqrt(ss_ref[...] * (1.0 / features) + EPS_IN)
    scale = jnp.transpose(inverse)[:, :1]
    q_ref[...] = (accq[...] * scale).astype(jnp.bfloat16)
    kv_ref[:, :nk] = (acck[...] * scale).astype(jnp.bfloat16)
    kv_ref[:, nk:] = (accv[...] * scale).astype(jnp.bfloat16)


def proj(order, blocks, wq, wk, wv, squares):
    depth = len(blocks)
    counts = [len(b) for b in blocks]
    rows = squares.shape[1]
    part_cols = blocks[0][0].shape[1]
    nq, nk, nv = wq.shape[1], wk.shape[1], wv.shape[1]
    n = nq + nk + nv
    flat = [p for b in blocks for p in b]
    return pl.pallas_call(
        functools.partial(proj_kernel, counts),
        in_specs=[IN_SMEM] + [IN_VMEM] * (len(flat) + 4),
        out_specs=[IN_VMEM, IN_VMEM],
        out_shape=[
            jax.ShapeDtypeStruct((rows, nq), jnp.bfloat16),
            jax.ShapeDtypeStruct((rows, nk + nv), jnp.bfloat16),
        ],
        scratch_shapes=[pltpu.VMEM((rows, m), jnp.float32) for m in (nq, nk, nv)],
        compiler_params=params(PROJ_MIB),
        cost_estimate=cost(
            2 * rows * part_cols * depth * n, 2 * part_cols * depth * (rows + n)
        ),
        name="proj",
    )(order, squares, *flat, wq, wk, wv)


def att_kernel(first, kv_heads, near, far, begins, ends, me_ref, q_ref, *refs):
    count = len(near) + len(far)
    kvs, refs = refs[:count], refs[count:]
    if not begins:
        high_in, total_in, accum_in, *refs = refs
    if ends:
        sign_ref, o_ref, high, total, accum = refs
    else:
        high, total, accum = refs
    rows = q_ref.shape[0]
    heads = q_ref.shape[1] // HD
    part = kvs[0].shape[0]
    group = heads // kv_heads
    scale = HD ** (-0.5) * LOG2E

    if not begins:
        high[...] = high_in[...]
        total[...] = total_in[...]
        accum[...] = accum_in[...]

    def visit(kv_ref, start, fresh):
        masked = start is not None and start + part > first
        scores, turned = [], []
        for kv in range(kv_heads):
            at = (kv_heads + kv) * HD
            turned.append(jnp.transpose(kv_ref[:, at : at + HD]))
        for head in range(heads):
            kv = head // group
            q = q_ref[:, head * HD : (head + 1) * HD]
            k = kv_ref[:, kv * HD : (kv + 1) * HD]
            s = lax.dot_general(
                k, q, (((1,), (1,)), ((), ())), preferred_element_type=jnp.float32
            )
            if masked:
                kpos = start + lax.broadcasted_iota(jnp.int32, s.shape, 0)
                qpos = first + lax.broadcasted_iota(jnp.int32, s.shape, 1)
                s = jnp.where(kpos <= qpos, s, FAR_BELOW)
            scores.append(s)
        for head in range(heads):
            s = scores[head]
            best = jnp.max(s, axis=0, keepdims=True)
            if not fresh:
                before = high[head : head + 1]
                best = jnp.maximum(best, before)
            w = jnp.exp2((s - best) * scale)
            sums = jnp.sum(w, axis=0, keepdims=True)
            mixed = jnp.dot(
                turned[head // group], w.astype(jnp.bfloat16), preferred_element_type=jnp.float32
            )
            if fresh:
                total[head : head + 1] = sums
                accum[head] = mixed
            else:
                decay = jnp.exp2((before - best) * scale)
                total[head : head + 1] = total[head : head + 1] * decay + sums
                accum[head] = accum[head] * decay + mixed
            high[head : head + 1] = best

    for at, start in enumerate(near):
        visit(kvs[at], start, begins and at == 0)
    for at, hop in enumerate(far):

        @pl.when(me_ref[0] >= hop)
        def _():
            visit(kvs[len(near) + at], None, False)

    if ends:
        for head in range(heads):
            att = jnp.transpose(accum[head] / total[head : head + 1])
            att = att.astype(jnp.bfloat16).astype(jnp.float32)
            o_ref[:, head * HD : (head + 1) * HD] = (att * sign_ref[head : head + 1, :]).astype(
                jnp.bfloat16
            )


def attend(me, q, first, kv_heads, near, far, state, signs):
    rows = q.shape[0]
    heads = q.shape[1] // HD
    kvs = [kv for _, kv in near + far]
    keys = sum(kv.shape[0] for kv in kvs)
    shapes = [(max(heads, 8), rows), (max(heads, 8), rows), (heads, HD, rows)]
    args = [me, q, *kvs]
    if state is not None:
        args += list(state)
    if signs is None:
        out_shape = [jax.ShapeDtypeStruct(shape, jnp.float32) for shape in shapes]
        scratch = []
    else:
        args.append(signs)
        out_shape = jax.ShapeDtypeStruct((rows, heads * HD), jnp.bfloat16)
        scratch = [pltpu.VMEM(shape, jnp.float32) for shape in shapes]
    near_at, far_at = [n for n, _ in near], [n for n, _ in far]
    kernel = functools.partial(
        att_kernel, first, kv_heads, near_at, far_at, state is None, signs is not None
    )
    return pl.pallas_call(
        kernel,
        in_specs=[IN_SMEM] + [IN_VMEM] * (len(args) - 1),
        out_specs=IN_VMEM if signs is not None else [IN_VMEM] * 3,
        out_shape=out_shape,
        scratch_shapes=scratch,
        compiler_params=params(ATT_MIB),
        cost_estimate=cost(4 * rows * keys * heads * HD, 4 * keys * HD, rows * keys * heads),
        name="attend",
    )(*args)


def butterfly(tiles):
    count = len(tiles)
    span = 1
    while span < count:
        out = list(tiles)
        for at in range(count):
            if not at & span:
                a, b = tiles[at], tiles[at | span]
                out[at], out[at | span] = a + b, a - b
        tiles = out
        span *= 2
    return tiles


def out_kernel(counts, steps, chunk, sign_ref, t_ref, *refs):
    parts = len(counts)
    blocks, at_block = [], 0
    for n in counts:
        blocks.append(refs[at_block : at_block + n])
        at_block += n
    w_ref, b_ref, s_ref, mid, rot, acc = refs[at_block:]
    rows = b_ref.shape[0]
    width = blocks[0][0].shape[1]
    here = width // HD
    heads = here * parts
    factor = heads ** (-0.5)

    strip = 16
    most = max(counts)
    span = rows // most
    for section in range(most):

        def turn(i, carry):
            at = pl.multiple_of(section * span + i * strip, strip)
            for m in range(parts):
                if len(blocks[m]) == 1:
                    ref, start = blocks[m][0], at
                else:
                    ref, start = blocks[m][section], pl.multiple_of(i * strip, strip)
                tiles = [
                    ref[pl.ds(start, strip), h * HD : (h + 1) * HD].astype(jnp.float32)
                    for h in range(here)
                ]
                for h, v in enumerate(butterfly(tiles)):
                    mid[m * here + h] = v
            for h in range(here):
                tiles = butterfly([mid[m * here + h] for m in range(parts)])
                for m in range(parts):
                    v = tiles[m] * (factor * sign_ref[m])
                    col = (m * here + h) * HD
                    rot[pl.ds(at, strip), col : col + HD] = clip_tile(v).astype(jnp.bfloat16)
            return carry

        lax.fori_loop(0, span // strip, turn, 0)

    depth = w_ref.shape[0] // steps
    for i in range(steps):
        part = jnp.dot(
            rot[:, i * depth : (i + 1) * depth],
            w_ref[i * depth : (i + 1) * depth, :],
            preferred_element_type=jnp.float32,
        )
        if i == 0:
            acc[...] = part
        else:
            acc[...] += part

    b = acc[...]
    t = t_ref[chunk * rows : (chunk + 1) * rows, :].astype(jnp.float32)
    b_ref[...] = b
    sums = [jnp.sum(v, axis=-1, keepdims=True) for v in (b * b, b * t, t * t)]
    lane = lax.broadcasted_iota(jnp.int32, (rows, 128), 1)
    wide = jnp.where(lane == 0, sums[0], jnp.where(lane == 1, sums[1], sums[2]))
    s_ref[...] = jnp.transpose(wide)[:8]


def project_out(flips, blocks, w_out, teacher, chunk):
    parts = len(blocks)
    counts = [len(b) for b in blocks]
    rows, width = blocks[0][0].shape
    depth, cols = w_out.shape
    steps = 4
    flat = [p for b in blocks for p in b]
    return pl.pallas_call(
        functools.partial(out_kernel, counts, steps, chunk),
        in_specs=[IN_SMEM] + [IN_VMEM] * (len(flat) + 2),
        out_specs=[IN_VMEM, IN_VMEM],
        out_shape=[
            jax.ShapeDtypeStruct((rows, cols), jnp.float32),
            jax.ShapeDtypeStruct((8, rows), jnp.float32),
        ],
        scratch_shapes=[
            pltpu.VMEM((parts * width // HD, 16, HD), jnp.float32),
            pltpu.VMEM((rows, depth), jnp.bfloat16),
            pltpu.VMEM((rows, cols), jnp.float32),
        ],
        compiler_params=params(OUT_MIB),
        cost_estimate=cost(2 * rows * depth * cols, 2 * depth * (rows + cols) + 6 * rows * cols),
        name="project_out",
    )(flips, teacher, *flat, w_out)


def final_kernel(features, chunks, parts, *refs):
    branches, stats = refs[:chunks], refs[chunks : chunks + parts]
    student_ref, loss_ref = refs[chunks + parts :]
    total = stats[0][...]
    for at in range(1, parts):
        total = total + stats[at][...]
    inverse = lax.rsqrt(total[0:1] * (1.0 / features) + EPS_OUT)
    loss = inverse * inverse * total[0:1] - 2.0 * inverse * total[1:2] + total[2:3]
    loss_ref[...] = jnp.maximum(loss, 0.0) * (1.0 / features)
    column = jnp.transpose(jnp.broadcast_to(inverse, total.shape))[:, :1]
    rows = branches[0].shape[0]
    for at in range(chunks):
        scale = column[at * rows : (at + 1) * rows]
        student_ref[at * rows : (at + 1) * rows, :] = (branches[at][...] * scale).astype(
            jnp.bfloat16
        )


def final(features, branches, stats):
    chunks, parts = len(branches), len(stats)
    part_rows, cols = branches[0].shape
    rows = part_rows * chunks
    return pl.pallas_call(
        functools.partial(final_kernel, features, chunks, parts),
        grid=(1,),
        in_specs=[whole((part_rows, cols))] * chunks + [whole((8, rows))] * parts,
        out_specs=[whole((rows, cols)), whole((1, rows))],
        out_shape=[
            jax.ShapeDtypeStruct((rows, cols), jnp.bfloat16),
            jax.ShapeDtypeStruct((1, rows), jnp.float32),
        ],
        compiler_params=params(16),
        cost_estimate=cost(2 * rows * cols, 6 * rows * cols),
        name="final",
    )(*branches, *stats)


def swap(x, mask):
    count = lax.axis_size("tp")
    return lax.ppermute(x, "tp", [(i, i ^ mask) for i in range(count)])


def send_up(x, distance):
    count = lax.axis_size("ctx")
    return lax.ppermute(x, "ctx", [(i, i + distance) for i in range(count - distance)])


def after(x, *others):
    return lax.optimization_barrier((x,) + others)[0]


def gather(own, diagonal_after=None, core_after=None):
    count = lax.axis_size("tp")
    got = {0: [own]}
    masks = [1 << b for b in range(1, count.bit_length() - 1)]
    if len(masks) >= 2:
        a, b = masks[0], masks[1]
        half = own.shape[0] // 2
        got[a] = [swap(own, a)]
        got[b] = [swap(own, b)]
        via_a, via_b = got[a][0], got[b][0]
        if diagonal_after is not None:
            via_a, via_b = after(via_a, diagonal_after), after(via_b, diagonal_after)
        got[a | b] = [swap(via_a[:half], b), swap(via_b[half:], a)]
        masks = masks[2:]
    if core_after is not None:
        for m in got:
            if m:
                got[m] = [after(p, core_after) for p in got[m]]
    if count > 1:
        for m in list(got):
            got[m | 1] = [swap(p, 1) for p in got[m]]
    for mask in masks:
        for m in list(got):
            got[m | mask] = [swap(p, mask) for p in got[m]]
    return [got[m] for m in range(count)]


def body(hidden_in, norm_gain, w_query, w_key, w_value, sign_bits, w_out, teacher):
    rows = hidden_in.shape[0]
    half = rows // HALVES
    tp_count = lax.axis_size("tp")
    ctx_count = lax.axis_size("ctx")
    features = hidden_in.shape[1] * tp_count
    tp_at = lax.axis_index("tp")
    ctx_at = jnp.reshape(lax.axis_index("ctx"), (1,)).astype(jnp.int32)
    masks = jnp.arange(tp_count, dtype=jnp.int32)
    order = tp_at ^ masks
    shared = tp_at & masks
    parity = jnp.zeros_like(shared)
    for bit in range(tp_count.bit_length()):
        parity = parity ^ (shared >> bit & 1)
    flips = (1 - 2 * parity).astype(jnp.float32)
    signs = (2 * sign_bits - 1).astype(jnp.float32)
    gain = norm_gain.reshape(-1, GROUP)

    chunks = [pre(hidden_in, gain, i, half) for i in range(HALVES)]
    clipped = [c for c, _ in chunks]
    squares = jnp.concatenate([s for _, s in chunks], axis=1)

    kv_cols = w_key.shape[1]
    sharing = HD // kv_cols if kv_cols < HD else 1
    kv_heads = kv_cols * sharing // HD
    queries, kvs = [], []
    for at in range(HALVES):
        own = clipped[at]
        if at:
            own = after(own, *[b[0] for b in blocks[2:6:2]])
        blocks = gather(own, diagonal_after=queries[-1] if at else None)
        if not at:
            if tp_count > 1:
                squares = after(squares, blocks[1][0])
            for bit in range(tp_count.bit_length() - 1):
                squares = squares + swap(squares, 1 << bit)
        part = squares[:, at * half : (at + 1) * half]
        q, kv = proj(order, blocks, w_query, w_key, w_value, part)
        if sharing > 1:
            k, v = kv[:, :kv_cols], kv[:, kv_cols:]
            for bit in range(sharing.bit_length() - 1):
                upper = tp_at >> bit & 1 == 1
                k2, v2 = swap(k, 1 << bit), swap(v, 1 << bit)
                k, v = (
                    jnp.where(
                        upper,
                        jnp.concatenate([far, near], axis=1),
                        jnp.concatenate([near, far], axis=1),
                    )
                    for near, far in ((k, k2), (v, v2))
                )
            kv = jnp.concatenate([k, v], axis=1)
        queries.append(q)
        kvs.append([kv] + [send_up(kv, hop) for hop in range(1, ctx_count)])

    states = []
    for at in range(HALVES):
        near = [(p * half, kvs[p][0]) for p in range(at + 1)]
        far = [(hop, kvs[p][hop]) for p in range(HALVES - 1) for hop in range(1, ctx_count)]
        states.append(
            attend(ctx_at, queries[at], at * half, kv_heads, near, far, None, None)
        )
    branches, stats = [], []
    for at in range(HALVES):
        far = [(hop, kvs[HALVES - 1][hop]) for hop in range(1, ctx_count)]
        signed = attend(
            ctx_at, queries[at], at * half, kv_heads, [], far, states[at], signs
        )
        blocks = gather(signed, core_after=branches[-1] if at else None)
        b, s = project_out(flips, blocks, w_out, teacher, at)
        branches.append(b)
        stats.append(s)
    stat = jnp.concatenate(stats, axis=1)
    for bit in range(tp_count.bit_length() - 1):
        stat = stat + swap(stat, 1 << bit)
    student, loss = final(features, branches, [stat])
    return student, loss.reshape(rows)


def solution(mesh):
    in_specs = (
        P("ctx", "tp"),
        P("tp"),
        P(None, "tp"),
        P(None, "tp"),
        P(None, "tp"),
        P("tp", None),
        P(None, "tp"),
        P("ctx", "tp"),
    )
    out_specs = (P("ctx", "tp"), P("ctx"))
    return jax.shard_map(body, mesh=mesh, in_specs=in_specs, out_specs=out_specs, check_vma=False)
```

```python
import functools
import math

import jax
import jax.numpy as jnp
from jax import lax
from jax.experimental import pallas as pl
from jax.experimental.pallas import tpu as pltpu
from jax.sharding import PartitionSpec as P

HD = 128
GROUP = 128
EPS_IN = 1e-05
EPS_OUT = 1e-06
CLIP_RATIO = 0.9
FAR_BELOW = -1e30
LOG2E = math.log2(math.e)
HALVES = 2
EXTRA = 16
LOAD_PARTS = 4
LOAD_MIB = 38
PROJ_MIB = 12
ATT_MIB = 12
OUT_MIB = 12
MIB = 1024 * 1024


def params(mib, **kw):
    return pltpu.CompilerParams(vmem_limit_bytes=mib * MIB, **kw)


def whole(shape):
    zeros = (0,) * len(shape)
    return pl.BlockSpec(shape, lambda *_: zeros)


IN_SMEM = pl.BlockSpec(memory_space=pltpu.SMEM)
IN_VMEM = pl.BlockSpec(memory_space=pltpu.VMEM)
ANYWHERE = pl.BlockSpec(memory_space=pl.ANY)
IN_HBM = pl.BlockSpec(memory_space=pltpu.HBM)


def cost(flops, moved, trans=0):
    return pl.CostEstimate(flops=int(flops), bytes_accessed=int(moved), transcendentals=int(trans))


def clip_tile(v):
    limit = CLIP_RATIO * jnp.max(jnp.abs(v), axis=-1, keepdims=True)
    return jnp.clip(v, -limit, limit)


def pre_kernel(h_hbm, g_hbm, *refs):
    outs, (h_all, g_ref, sem) = refs[:HALVES], refs[HALVES:]
    rows, width = h_all.shape
    steps = sem.shape[0] - 1
    part = rows // steps
    copies = [pltpu.make_async_copy(g_hbm, g_ref, sem.at[steps])]
    for i in range(steps):
        at = slice(i * part, (i + 1) * part)
        copies.append(pltpu.make_async_copy(h_hbm.at[at], h_all.at[at], sem.at[i]))
    for copy in copies:
        copy.start()
    copies[0].wait()
    for i in range(steps):
        copies[i + 1].wait()
        total = jnp.zeros((part, GROUP), jnp.float32)
        row = i * part % (rows // HALVES)
        c_ref = outs[i * part // (rows // HALVES)]
        for at in range(0, width, GROUP):
            h = h_all[i * part : (i + 1) * part, at : at + GROUP].astype(jnp.float32)
            total = total + h * h
            v = h * g_ref[at // GROUP : at // GROUP + 1, :].astype(jnp.float32)
            c_ref[row : row + part, at : at + GROUP] = clip_tile(v).astype(jnp.bfloat16)
        sums = jnp.sum(total, axis=-1, keepdims=True)
        sums = jnp.transpose(jnp.broadcast_to(sums, (part, 128)))[:EXTRA]
        row = lax.broadcasted_iota(jnp.int32, sums.shape, 0)
        left = sums
        for place in range(3):
            piece = left.astype(jnp.bfloat16).astype(jnp.float32)
            left = left - piece
            sums = jnp.where(row == place, piece, sums)
        outs[0][rows // HALVES :, i * part : (i + 1) * part] = sums.astype(jnp.bfloat16)


def pre(hidden, gain):
    rows, width = hidden.shape
    steps = HALVES * 2
    return pl.pallas_call(
        pre_kernel,
        in_specs=[IN_HBM] * 2,
        out_specs=[IN_VMEM] * HALVES,
        out_shape=[
            pltpu.VMEM((rows // HALVES + (0 if i else EXTRA), width), jnp.bfloat16)
            for i in range(HALVES)
        ],
        scratch_shapes=[
            pltpu.VMEM((rows, width), jnp.bfloat16),
            pltpu.VMEM(gain.shape, jnp.bfloat16),
            pltpu.SemaphoreType.DMA((steps + 1,)),
        ],
        compiler_params=params(8),
        cost_estimate=cost(8 * rows * width, 4 * rows * width),
        name="pre",
    )(hidden, gain)


def load_kernel(count, token_ref, *refs):
    sources, goals, sem = refs[:count], refs[count : 2 * count], refs[-1]
    copies = []
    for i in range(count):
        depth = sources[i].shape[0] // LOAD_PARTS
        for p in range(LOAD_PARTS):
            at = slice(p * depth, (p + 1) * depth)
            copies.append(
                pltpu.make_async_copy(sources[i].at[at], goals[i].at[at], sem.at[i, p])
            )
    for copy in copies:
        copy.start()
    for copy in copies:
        copy.wait()


def load(token, *weights):
    count = len(weights)
    return pl.pallas_call(
        functools.partial(load_kernel, count),
        in_specs=[ANYWHERE] + [IN_HBM] * count,
        out_specs=[IN_VMEM] * count,
        out_shape=[pltpu.VMEM(w.shape, w.dtype) for w in weights],
        scratch_shapes=[pltpu.SemaphoreType.DMA((count, LOAD_PARTS))],
        compiler_params=params(LOAD_MIB),
        cost_estimate=cost(0, 2 * sum(w.size * 2 for w in weights)),
        name="load",
    )(token, *weights)


def proj_kernel(counts, chunk, order_ref, *refs):
    depth = len(counts)
    blocks = refs[: sum(counts)]
    refs = refs[sum(counts) :]
    if chunk:
        wq_ref, wk_ref, wv_ref, ss_ref, q_ref, kv_ref, accq, acck, accv = refs
        squares = ss_ref[...]
    else:
        wq_ref, wk_ref, wv_ref, q_ref, kv_ref, ss_ref, accq, acck, accv = refs
        squares = jnp.zeros((1, ss_ref.shape[1]), jnp.float32)
    rows = q_ref.shape[0]
    nk = wk_ref.shape[1]
    k_rows = blocks[0].shape[1]
    at_block = 0
    for k in range(depth):
        at = pl.ds(pl.multiple_of(order_ref[k] * k_rows, k_rows), k_rows)
        mine = [b[...] for b in blocks[at_block : at_block + counts[k]]]
        at_block += counts[k]
        if not chunk:
            body_rows = mine[-1].shape[0] - EXTRA
            tail = mine[-1][body_rows:, : ss_ref.shape[1]].astype(jnp.float32)
            squares = squares + (tail[0:1] + tail[1:2] + tail[2:3])
            mine[-1] = mine[-1][:body_rows]
        left = mine[0] if len(mine) == 1 else jnp.concatenate(mine, axis=0)
        wq, wk, wv = wq_ref[at, :], wk_ref[at, :], wv_ref[at, :]
        if nk % 128 == 0:
            both = jnp.dot(
                left, jnp.concatenate([wk, wv], axis=1), preferred_element_type=jnp.float32
            )
            parts = (both[:, :nk], both[:, nk:])
        else:
            parts = [jnp.dot(left, w, preferred_element_type=jnp.float32) for w in (wk, wv)]
        first = jnp.dot(left, wq, preferred_element_type=jnp.float32)
        for part, acc in zip((first, *parts), (accq, acck, accv)):
            if k == 0:
                acc[...] = part
            else:
                acc[...] += part

    features = k_rows * depth
    if not chunk:
        squares = jnp.broadcast_to(squares, ss_ref.shape)
        ss_ref[...] = squares
    squares = squares[:, chunk * rows : (chunk + 1) * rows]
    inverse = lax.rsqrt(squares * (1.0 / features) + EPS_IN)
    scale = jnp.transpose(inverse)[:, :1]
    q_ref[...] = (accq[...] * scale).astype(jnp.bfloat16)
    kv_ref[:, :nk] = (acck[...] * scale).astype(jnp.bfloat16)
    kv_ref[:, nk:] = (accv[...] * scale).astype(jnp.bfloat16)


def proj(order, blocks, chunk, rows, squares, wq, wk, wv):
    depth = len(blocks)
    counts = [len(b) for b in blocks]
    part_cols = blocks[0][0].shape[1]
    nq, nk, nv = wq.shape[1], wk.shape[1], wv.shape[1]
    n = nq + nk + nv
    flat = [p for b in blocks for p in b]
    args = [order, *flat, wq, wk, wv]
    out_shape = [
        jax.ShapeDtypeStruct((rows, nq), jnp.bfloat16),
        jax.ShapeDtypeStruct((rows, nk + nv), jnp.bfloat16),
    ]
    if chunk:
        args.append(squares)
    else:
        out_shape.append(jax.ShapeDtypeStruct((8, rows * HALVES), jnp.float32))
    return pl.pallas_call(
        functools.partial(proj_kernel, counts, chunk),
        in_specs=[IN_SMEM] + [IN_VMEM] * (len(args) - 1),
        out_specs=[IN_VMEM] * len(out_shape),
        out_shape=out_shape,
        scratch_shapes=[pltpu.VMEM((rows, m), jnp.float32) for m in (nq, nk, nv)],
        compiler_params=params(PROJ_MIB),
        cost_estimate=cost(
            2 * rows * part_cols * depth * n, 2 * part_cols * depth * (rows + n)
        ),
        name="proj",
    )(*args)


def att_kernel(first, kv_heads, near, far, begins, ends, me_ref, q_ref, *refs):
    count = len(near) + len(far)
    kvs, refs = refs[:count], refs[count:]
    if not begins:
        high_in, total_in, accum_in, *refs = refs
    if ends:
        sign_ref, o_ref, high, total, accum = refs
    else:
        high, total, accum = refs
    rows = q_ref.shape[0]
    heads = q_ref.shape[1] // HD
    part = kvs[0].shape[0]
    group = heads // kv_heads
    scale = HD ** (-0.5) * LOG2E

    if not begins:
        high[...] = high_in[...]
        total[...] = total_in[...]
        accum[...] = accum_in[...]

    def visit(kv_ref, start, fresh):
        masked = start is not None and start + part > first
        scores, turned = [], []
        for kv in range(kv_heads):
            at = (kv_heads + kv) * HD
            turned.append(jnp.transpose(kv_ref[:, at : at + HD]))
        for head in range(heads):
            kv = head // group
            q = q_ref[:, head * HD : (head + 1) * HD]
            k = kv_ref[:, kv * HD : (kv + 1) * HD]
            s = lax.dot_general(
                k, q, (((1,), (1,)), ((), ())), preferred_element_type=jnp.float32
            )
            if masked:
                kpos = start + lax.broadcasted_iota(jnp.int32, s.shape, 0)
                qpos = first + lax.broadcasted_iota(jnp.int32, s.shape, 1)
                s = jnp.where(kpos <= qpos, s, FAR_BELOW)
            scores.append(s)
        for head in range(heads):
            s = scores[head]
            best = jnp.max(s, axis=0, keepdims=True)
            if not fresh:
                before = high[head : head + 1]
                best = jnp.maximum(best, before)
            w = jnp.exp2((s - best) * scale)
            sums = jnp.sum(w, axis=0, keepdims=True)
            mixed = jnp.dot(
                turned[head // group], w.astype(jnp.bfloat16), preferred_element_type=jnp.float32
            )
            if fresh:
                total[head : head + 1] = sums
                accum[head] = mixed
            else:
                decay = jnp.exp2((before - best) * scale)
                total[head : head + 1] = total[head : head + 1] * decay + sums
                accum[head] = accum[head] * decay + mixed
            high[head : head + 1] = best

    for at, start in enumerate(near):
        visit(kvs[at], start, begins and at == 0)
    for at, hop in enumerate(far):

        @pl.when(me_ref[0] >= hop)
        def _():
            visit(kvs[len(near) + at], None, False)

    if ends:
        for head in range(heads):
            att = jnp.transpose(accum[head] / total[head : head + 1])
            att = att.astype(jnp.bfloat16).astype(jnp.float32)
            o_ref[:, head * HD : (head + 1) * HD] = (att * sign_ref[head : head + 1, :]).astype(
                jnp.bfloat16
            )


def attend(me, q, first, kv_heads, near, far, state, signs):
    rows = q.shape[0]
    heads = q.shape[1] // HD
    kvs = [kv for _, kv in near + far]
    keys = sum(kv.shape[0] for kv in kvs)
    shapes = [(max(heads, 8), rows), (max(heads, 8), rows), (heads, HD, rows)]
    args = [me, q, *kvs]
    if state is not None:
        args += list(state)
    if signs is None:
        out_shape = [jax.ShapeDtypeStruct(shape, jnp.float32) for shape in shapes]
        scratch = []
    else:
        args.append(signs)
        out_shape = jax.ShapeDtypeStruct((rows, heads * HD), jnp.bfloat16)
        scratch = [pltpu.VMEM(shape, jnp.float32) for shape in shapes]
    near_at, far_at = [n for n, _ in near], [n for n, _ in far]
    kernel = functools.partial(
        att_kernel, first, kv_heads, near_at, far_at, state is None, signs is not None
    )
    return pl.pallas_call(
        kernel,
        in_specs=[IN_SMEM] + [IN_VMEM] * (len(args) - 1),
        out_specs=IN_VMEM if signs is not None else [IN_VMEM] * 3,
        out_shape=out_shape,
        scratch_shapes=scratch,
        compiler_params=params(ATT_MIB),
        cost_estimate=cost(4 * rows * keys * heads * HD, 4 * keys * HD, rows * keys * heads),
        name="attend",
    )(*args)


def butterfly(tiles):
    count = len(tiles)
    span = 1
    while span < count:
        out = list(tiles)
        for at in range(count):
            if not at & span:
                a, b = tiles[at], tiles[at | span]
                out[at], out[at | span] = a + b, a - b
        tiles = out
        span *= 2
    return tiles


def out_kernel(counts, steps, chunk, sign_ref, t_ref, *refs):
    parts = len(counts)
    blocks, at_block = [], 0
    for n in counts:
        blocks.append(refs[at_block : at_block + n])
        at_block += n
    w_ref, b_ref, s_ref, mid, rot, acc = refs[at_block:]
    rows = b_ref.shape[0]
    width = blocks[0][0].shape[1]
    here = width // HD
    heads = here * parts
    factor = heads ** (-0.5)

    strip = 16
    most = max(counts)
    span = rows // most
    for section in range(most):

        def turn(i, carry):
            at = pl.multiple_of(section * span + i * strip, strip)
            for m in range(parts):
                if len(blocks[m]) == 1:
                    ref, start = blocks[m][0], at
                else:
                    ref, start = blocks[m][section], pl.multiple_of(i * strip, strip)
                tiles = [
                    ref[pl.ds(start, strip), h * HD : (h + 1) * HD].astype(jnp.float32)
                    for h in range(here)
                ]
                for h, v in enumerate(butterfly(tiles)):
                    mid[m * here + h] = v
            for h in range(here):
                tiles = butterfly([mid[m * here + h] for m in range(parts)])
                for m in range(parts):
                    v = tiles[m] * (factor * sign_ref[m])
                    col = (m * here + h) * HD
                    rot[pl.ds(at, strip), col : col + HD] = clip_tile(v).astype(jnp.bfloat16)
            return carry

        lax.fori_loop(0, span // strip, turn, 0)

    depth = w_ref.shape[0] // steps
    for i in range(steps):
        part = jnp.dot(
            rot[:, i * depth : (i + 1) * depth],
            w_ref[i * depth : (i + 1) * depth, :],
            preferred_element_type=jnp.float32,
        )
        if i == 0:
            acc[...] = part
        else:
            acc[...] += part

    b = acc[...]
    t = t_ref[chunk * rows : (chunk + 1) * rows, :].astype(jnp.float32)
    b_ref[...] = b
    sums = [jnp.sum(v, axis=-1, keepdims=True) for v in (b * b, b * t, t * t)]
    lane = lax.broadcasted_iota(jnp.int32, (rows, 128), 1)
    wide = jnp.where(lane == 0, sums[0], jnp.where(lane == 1, sums[1], sums[2]))
    s_ref[...] = jnp.transpose(wide)[:8]


def project_out(flips, blocks, w_out, teacher, chunk):
    parts = len(blocks)
    counts = [len(b) for b in blocks]
    rows, width = blocks[0][0].shape
    depth, cols = w_out.shape
    steps = 4
    flat = [p for b in blocks for p in b]
    return pl.pallas_call(
        functools.partial(out_kernel, counts, steps, chunk),
        in_specs=[IN_SMEM] + [IN_VMEM] * (len(flat) + 2),
        out_specs=[IN_VMEM, IN_VMEM],
        out_shape=[
            jax.ShapeDtypeStruct((rows, cols), jnp.float32),
            jax.ShapeDtypeStruct((8, rows), jnp.float32),
        ],
        scratch_shapes=[
            pltpu.VMEM((parts * width // HD, 16, HD), jnp.float32),
            pltpu.VMEM((rows, depth), jnp.bfloat16),
            pltpu.VMEM((rows, cols), jnp.float32),
        ],
        compiler_params=params(OUT_MIB),
        cost_estimate=cost(2 * rows * depth * cols, 2 * depth * (rows + cols) + 6 * rows * cols),
        name="project_out",
    )(flips, teacher, *flat, w_out)


def final_kernel(features, chunks, parts, *refs):
    branches, stats = refs[:chunks], refs[chunks : chunks + parts]
    student_ref, loss_ref = refs[chunks + parts :]
    total = stats[0][...]
    for at in range(1, parts):
        total = total + stats[at][...]
    inverse = lax.rsqrt(total[0:1] * (1.0 / features) + EPS_OUT)
    loss = inverse * inverse * total[0:1] - 2.0 * inverse * total[1:2] + total[2:3]
    loss_ref[...] = jnp.maximum(loss, 0.0) * (1.0 / features)
    column = jnp.transpose(jnp.broadcast_to(inverse, total.shape))[:, :1]
    rows = branches[0].shape[0]
    for at in range(chunks):
        scale = column[at * rows : (at + 1) * rows]
        student_ref[at * rows : (at + 1) * rows, :] = (branches[at][...] * scale).astype(
            jnp.bfloat16
        )


def final(features, branches, stats):
    chunks, parts = len(branches), len(stats)
    part_rows, cols = branches[0].shape
    rows = part_rows * chunks
    return pl.pallas_call(
        functools.partial(final_kernel, features, chunks, parts),
        grid=(1,),
        in_specs=[whole((part_rows, cols))] * chunks + [whole((8, rows))] * parts,
        out_specs=[whole((rows, cols)), whole((1, rows))],
        out_shape=[
            jax.ShapeDtypeStruct((rows, cols), jnp.bfloat16),
            jax.ShapeDtypeStruct((1, rows), jnp.float32),
        ],
        compiler_params=params(16),
        cost_estimate=cost(2 * rows * cols, 6 * rows * cols),
        name="final",
    )(*branches, *stats)


def swap(x, mask):
    count = lax.axis_size("tp")
    return lax.ppermute(x, "tp", [(i, i ^ mask) for i in range(count)])


def send_up(x, distance):
    count = lax.axis_size("ctx")
    return lax.ppermute(x, "ctx", [(i, i + distance) for i in range(count - distance)])


def after(x, *others):
    return lax.optimization_barrier((x,) + others)[0]


def gather(own, core_after=None, beside=None):
    count = lax.axis_size("tp")
    got = {0: [own]}
    masks = [1 << b for b in range(1, count.bit_length() - 1)]
    if len(masks) >= 2:
        a, b = masks[0], masks[1]
        half = own.shape[0] // (2 * EXTRA) * EXTRA
        got[a] = [swap(own, a)]
        got[b] = [swap(own, b)]
        via_a, via_b = got[a][0], got[b][0]
        got[1] = [swap(own, 1)]
        if beside is not None:
            first = beside(got[1][0])
            via_a, via_b = after(via_a, first), after(via_b, first)
        got[a | b] = [swap(via_a[:half], b), swap(via_b[half:], a)]
        masks = masks[2:]
    if core_after is not None:
        for m in got:
            if m > 1:
                got[m] = [after(p, core_after) for p in got[m]]
    if count > 1:
        for m in list(got):
            if m | 1 not in got:
                got[m | 1] = [swap(p, 1) for p in got[m]]
    for mask in masks:
        for m in list(got):
            got[m | mask] = [swap(p, mask) for p in got[m]]
    return [got[m] for m in range(count)]


def body(hidden_in, norm_gain, w_query, w_key, w_value, sign_bits, w_out, teacher):
    rows = hidden_in.shape[0]
    half = rows // HALVES
    tp_count = lax.axis_size("tp")
    ctx_count = lax.axis_size("ctx")
    features = hidden_in.shape[1] * tp_count
    tp_at = lax.axis_index("tp")
    ctx_at = jnp.reshape(lax.axis_index("ctx"), (1,)).astype(jnp.int32)
    masks = jnp.arange(tp_count, dtype=jnp.int32)
    order = tp_at ^ masks
    shared = tp_at & masks
    parity = jnp.zeros_like(shared)
    for bit in range(tp_count.bit_length()):
        parity = parity ^ (shared >> bit & 1)
    flips = (1 - 2 * parity).astype(jnp.float32)
    signs = (2 * sign_bits - 1).astype(jnp.float32)
    gain = norm_gain.reshape(-1, GROUP)

    clipped = pre(hidden_in, gain)
    squares = None

    kv_cols = w_key.shape[1]
    sharing = HD // kv_cols if kv_cols < HD else 1
    kv_heads = kv_cols * sharing // HD
    queries, kvs = [], []
    for at in range(HALVES):
        own = clipped[at]
        if at:
            own = after(own, *[b[0] for b in blocks[2:6:2]], loaded[1])
        if at:
            blocks = gather(own, core_after=queries[-1])
        else:
            loaded = []

            def bring(token):
                loaded.extend(load(token, w_query, w_key, w_value, w_out))
                return loaded[1]

            blocks = gather(own, beside=bring)
            if not loaded:
                bring(own)
        part = squares
        if at and ctx_count > 1:
            part = after(part, kvs[0][1])
        q, kv, *rest = proj(order, blocks, at, half, part, *loaded[:3])
        if rest:
            squares = rest[0]
        if sharing > 1:
            k, v = kv[:, :kv_cols], kv[:, kv_cols:]
            for bit in range(sharing.bit_length() - 1):
                upper = tp_at >> bit & 1 == 1
                k2, v2 = swap(k, 1 << bit), swap(v, 1 << bit)
                k, v = (
                    jnp.where(
                        upper,
                        jnp.concatenate([far, near], axis=1),
                        jnp.concatenate([near, far], axis=1),
                    )
                    for near, far in ((k, k2), (v, v2))
                )
            kv = jnp.concatenate([k, v], axis=1)
        queries.append(q)
        kvs.append([kv] + [send_up(kv, hop) for hop in range(1, ctx_count)])

    states = []
    for at in range(HALVES):
        near = [(p * half, kvs[p][0]) for p in range(at + 1)]
        far = [(hop, kvs[p][hop]) for p in range(HALVES - 1) for hop in range(1, ctx_count)]
        states.append(
            attend(ctx_at, queries[at], at * half, kv_heads, near, far, None, None)
        )
    branches, stats = [], []
    for at in range(HALVES):
        far = [(hop, kvs[HALVES - 1][hop]) for hop in range(1, ctx_count)]
        signed = attend(
            ctx_at, queries[at], at * half, kv_heads, [], far, states[at], signs
        )
        if at:
            signed = after(signed, *[b[0] for b in blocks[2:6:2]])
        blocks = gather(signed, branches[-1] if at else None)
        b, s = project_out(flips, blocks, loaded[3], teacher, at)
        branches.append(b)
        stats.append(s)
    stat = jnp.concatenate(stats, axis=1)
    for bit in range(tp_count.bit_length() - 1):
        stat = stat + swap(stat, 1 << bit)
    student, loss = final(features, branches, [stat])
    return student, loss.reshape(rows)


def solution(mesh):
    in_specs = (
        P("ctx", "tp"),
        P("tp"),
        P(None, "tp"),
        P(None, "tp"),
        P(None, "tp"),
        P("tp", None),
        P(None, "tp"),
        P("ctx", "tp"),
    )
    out_specs = (P("ctx", "tp"), P("ctx"))
    return jax.shard_map(body, mesh=mesh, in_specs=in_specs, out_specs=out_specs, check_vma=False)
```

```python
import functools
import math

import jax
import jax.numpy as jnp
from jax import lax
from jax.experimental import pallas as pl
from jax.experimental.pallas import tpu as pltpu
from jax.sharding import PartitionSpec as P

HD = 128
GROUP = 128
EPS_IN = 1e-05
EPS_OUT = 1e-06
CLIP_RATIO = 0.9
FAR_BELOW = -1e30
LOG2E = math.log2(math.e)
HALVES = 2
EXTRA = 16
LOAD_PARTS = 4
LOAD_MIB = 38
PROJ_MIB = 12
ATT_MIB = 12
OUT_MIB = 12
MIB = 1024 * 1024


def params(mib, **kw):
    return pltpu.CompilerParams(vmem_limit_bytes=mib * MIB, **kw)


def whole(shape):
    zeros = (0,) * len(shape)
    return pl.BlockSpec(shape, lambda *_: zeros)


IN_SMEM = pl.BlockSpec(memory_space=pltpu.SMEM)
IN_VMEM = pl.BlockSpec(memory_space=pltpu.VMEM)
ANYWHERE = pl.BlockSpec(memory_space=pl.ANY)
IN_HBM = pl.BlockSpec(memory_space=pltpu.HBM)


def cost(flops, moved, trans=0):
    return pl.CostEstimate(flops=int(flops), bytes_accessed=int(moved), transcendentals=int(trans))


def clip_tile(v):
    limit = CLIP_RATIO * jnp.max(jnp.abs(v), axis=-1, keepdims=True)
    return jnp.clip(v, -limit, limit)


def pre_kernel(h_hbm, g_hbm, *refs):
    outs, (h_all, g_ref, sem) = refs[:HALVES], refs[HALVES:]
    rows, width = h_all.shape
    steps = sem.shape[0] - 1
    part = rows // steps
    copies = [pltpu.make_async_copy(g_hbm, g_ref, sem.at[steps])]
    for i in range(steps):
        at = slice(i * part, (i + 1) * part)
        copies.append(pltpu.make_async_copy(h_hbm.at[at], h_all.at[at], sem.at[i]))
    for copy in copies:
        copy.start()
    copies[0].wait()
    for i in range(steps):
        copies[i + 1].wait()
        total = jnp.zeros((part, GROUP), jnp.float32)
        row = i * part % (rows // HALVES)
        c_ref = outs[i * part // (rows // HALVES)]
        for at in range(0, width, GROUP):
            h = h_all[i * part : (i + 1) * part, at : at + GROUP].astype(jnp.float32)
            total = total + h * h
            v = h * g_ref[at // GROUP : at // GROUP + 1, :].astype(jnp.float32)
            c_ref[row : row + part, at : at + GROUP] = clip_tile(v).astype(jnp.bfloat16)
        sums = jnp.sum(total, axis=-1, keepdims=True)
        sums = jnp.transpose(jnp.broadcast_to(sums, (part, 128)))[:EXTRA]
        row = lax.broadcasted_iota(jnp.int32, sums.shape, 0)
        left = sums
        for place in range(3):
            piece = left.astype(jnp.bfloat16).astype(jnp.float32)
            left = left - piece
            sums = jnp.where(row == place, piece, sums)
        outs[0][rows // HALVES :, i * part : (i + 1) * part] = sums.astype(jnp.bfloat16)


def pre(hidden, gain):
    rows, width = hidden.shape
    steps = HALVES * 2
    return pl.pallas_call(
        pre_kernel,
        in_specs=[IN_HBM] * 2,
        out_specs=[IN_VMEM] * HALVES,
        out_shape=[
            pltpu.VMEM((rows // HALVES + (0 if i else EXTRA), width), jnp.bfloat16)
            for i in range(HALVES)
        ],
        scratch_shapes=[
            pltpu.VMEM((rows, width), jnp.bfloat16),
            pltpu.VMEM(gain.shape, jnp.bfloat16),
            pltpu.SemaphoreType.DMA((steps + 1,)),
        ],
        compiler_params=params(62),
        cost_estimate=cost(8 * rows * width, 4 * rows * width),
        name="pre",
    )(hidden, gain)


def load_kernel(count, *refs):
    sources, goals, sem = refs[:count], refs[count : 2 * count], refs[-1]
    copies = []
    for i in range(count):
        depth = sources[i].shape[0] // LOAD_PARTS
        for p in range(LOAD_PARTS):
            at = slice(p * depth, (p + 1) * depth)
            copies.append(
                pltpu.make_async_copy(sources[i].at[at], goals[i].at[at], sem.at[i, p])
            )
    for copy in copies:
        copy.start()
    for copy in copies:
        copy.wait()


def load(*weights):
    count = len(weights)
    return pl.pallas_call(
        functools.partial(load_kernel, count),
        in_specs=[IN_HBM] * count,
        out_specs=[IN_VMEM] * count,
        out_shape=[pltpu.VMEM(w.shape, w.dtype) for w in weights],
        scratch_shapes=[pltpu.SemaphoreType.DMA((count, LOAD_PARTS))],
        compiler_params=params(LOAD_MIB),
        cost_estimate=cost(0, 2 * sum(w.size * 2 for w in weights)),
        name="load",
    )(*weights)


def proj_kernel(counts, chunk, order_ref, *refs):
    depth = len(counts)
    blocks = refs[: sum(counts)]
    refs = refs[sum(counts) :]
    if chunk:
        wq_ref, wk_ref, wv_ref, ss_ref, q_ref, kv_ref, accq, acck, accv = refs
        squares = ss_ref[...]
    else:
        wq_ref, wk_ref, wv_ref, q_ref, kv_ref, ss_ref, accq, acck, accv = refs
        squares = jnp.zeros((1, ss_ref.shape[1]), jnp.float32)
    rows = q_ref.shape[0]
    nk = wk_ref.shape[1]
    k_rows = blocks[0].shape[1]
    at_block = 0
    for k in range(depth):
        at = pl.ds(pl.multiple_of(order_ref[k] * k_rows, k_rows), k_rows)
        mine = [b[...] for b in blocks[at_block : at_block + counts[k]]]
        at_block += counts[k]
        if not chunk:
            body_rows = mine[-1].shape[0] - EXTRA
            tail = mine[-1][body_rows:, : ss_ref.shape[1]].astype(jnp.float32)
            squares = squares + (tail[0:1] + tail[1:2] + tail[2:3])
            mine[-1] = mine[-1][:body_rows]
        left = mine[0] if len(mine) == 1 else jnp.concatenate(mine, axis=0)
        wq, wk, wv = wq_ref[at, :], wk_ref[at, :], wv_ref[at, :]
        if nk % 128 == 0:
            both = jnp.dot(
                left, jnp.concatenate([wk, wv], axis=1), preferred_element_type=jnp.float32
            )
            parts = (both[:, :nk], both[:, nk:])
        else:
            parts = [jnp.dot(left, w, preferred_element_type=jnp.float32) for w in (wk, wv)]
        first = jnp.dot(left, wq, preferred_element_type=jnp.float32)
        for part, acc in zip((first, *parts), (accq, acck, accv)):
            if k == 0:
                acc[...] = part
            else:
                acc[...] += part

    features = k_rows * depth
    if not chunk:
        squares = jnp.broadcast_to(squares, ss_ref.shape)
        ss_ref[...] = squares
    squares = squares[:, chunk * rows : (chunk + 1) * rows]
    inverse = lax.rsqrt(squares * (1.0 / features) + EPS_IN)
    scale = jnp.transpose(inverse)[:, :1]
    q_ref[...] = (accq[...] * scale).astype(jnp.bfloat16)
    kv_ref[:, :nk] = (acck[...] * scale).astype(jnp.bfloat16)
    kv_ref[:, nk:] = (accv[...] * scale).astype(jnp.bfloat16)


def proj(order, blocks, chunk, rows, squares, wq, wk, wv):
    depth = len(blocks)
    counts = [len(b) for b in blocks]
    part_cols = blocks[0][0].shape[1]
    nq, nk, nv = wq.shape[1], wk.shape[1], wv.shape[1]
    n = nq + nk + nv
    flat = [p for b in blocks for p in b]
    args = [order, *flat, wq, wk, wv]
    out_shape = [
        jax.ShapeDtypeStruct((rows, nq), jnp.bfloat16),
        jax.ShapeDtypeStruct((rows, nk + nv), jnp.bfloat16),
    ]
    if chunk:
        args.append(squares)
    else:
        out_shape.append(jax.ShapeDtypeStruct((8, rows * HALVES), jnp.float32))
    return pl.pallas_call(
        functools.partial(proj_kernel, counts, chunk),
        in_specs=[IN_SMEM] + [IN_VMEM] * (len(args) - 1),
        out_specs=[IN_VMEM] * len(out_shape),
        out_shape=out_shape,
        scratch_shapes=[pltpu.VMEM((rows, m), jnp.float32) for m in (nq, nk, nv)],
        compiler_params=params(PROJ_MIB),
        cost_estimate=cost(
            2 * rows * part_cols * depth * n, 2 * part_cols * depth * (rows + n)
        ),
        name="proj",
    )(*args)


def att_kernel(first, kv_heads, near, far, begins, ends, me_ref, q_ref, *refs):
    count = len(near) + len(far)
    kvs, refs = refs[:count], refs[count:]
    if not begins:
        high_in, total_in, accum_in, *refs = refs
    if ends:
        sign_ref, o_ref, high, total, accum = refs
    else:
        high, total, accum = refs
    rows = q_ref.shape[0]
    heads = q_ref.shape[1] // HD
    part = kvs[0].shape[0]
    group = heads // kv_heads
    scale = HD ** (-0.5) * LOG2E

    if not begins:
        high[...] = high_in[...]
        total[...] = total_in[...]
        accum[...] = accum_in[...]

    def visit(kv_ref, start, fresh):
        masked = start is not None and start + part > first
        scores, turned = [], []
        for kv in range(kv_heads):
            at = (kv_heads + kv) * HD
            turned.append(jnp.transpose(kv_ref[:, at : at + HD]))
        for head in range(heads):
            kv = head // group
            q = q_ref[:, head * HD : (head + 1) * HD]
            k = kv_ref[:, kv * HD : (kv + 1) * HD]
            s = lax.dot_general(
                k, q, (((1,), (1,)), ((), ())), preferred_element_type=jnp.float32
            )
            if masked:
                kpos = start + lax.broadcasted_iota(jnp.int32, s.shape, 0)
                qpos = first + lax.broadcasted_iota(jnp.int32, s.shape, 1)
                s = jnp.where(kpos <= qpos, s, FAR_BELOW)
            scores.append(s)
        for head in range(heads):
            s = scores[head]
            best = jnp.max(s, axis=0, keepdims=True)
            if not fresh:
                before = high[head : head + 1]
                best = jnp.maximum(best, before)
            w = jnp.exp2((s - best) * scale)
            sums = jnp.sum(w, axis=0, keepdims=True)
            mixed = jnp.dot(
                turned[head // group], w.astype(jnp.bfloat16), preferred_element_type=jnp.float32
            )
            if fresh:
                total[head : head + 1] = sums
                accum[head] = mixed
            else:
                decay = jnp.exp2((before - best) * scale)
                total[head : head + 1] = total[head : head + 1] * decay + sums
                accum[head] = accum[head] * decay + mixed
            high[head : head + 1] = best

    for at, start in enumerate(near):
        visit(kvs[at], start, begins and at == 0)
    for at, hop in enumerate(far):

        @pl.when(me_ref[0] >= hop)
        def _():
            visit(kvs[len(near) + at], None, False)

    if ends:
        for head in range(heads):
            att = jnp.transpose(accum[head] / total[head : head + 1])
            att = att.astype(jnp.bfloat16).astype(jnp.float32)
            o_ref[:, head * HD : (head + 1) * HD] = (att * sign_ref[head : head + 1, :]).astype(
                jnp.bfloat16
            )


def attend(me, q, first, kv_heads, near, far, state, signs):
    rows = q.shape[0]
    heads = q.shape[1] // HD
    kvs = [kv for _, kv in near + far]
    keys = sum(kv.shape[0] for kv in kvs)
    shapes = [(max(heads, 8), rows), (max(heads, 8), rows), (heads, HD, rows)]
    args = [me, q, *kvs]
    if state is not None:
        args += list(state)
    if signs is None:
        out_shape = [jax.ShapeDtypeStruct(shape, jnp.float32) for shape in shapes]
        scratch = []
    else:
        args.append(signs)
        out_shape = jax.ShapeDtypeStruct((rows, heads * HD), jnp.bfloat16)
        scratch = [pltpu.VMEM(shape, jnp.float32) for shape in shapes]
    near_at, far_at = [n for n, _ in near], [n for n, _ in far]
    kernel = functools.partial(
        att_kernel, first, kv_heads, near_at, far_at, state is None, signs is not None
    )
    return pl.pallas_call(
        kernel,
        in_specs=[IN_SMEM] + [IN_VMEM] * (len(args) - 1),
        out_specs=IN_VMEM if signs is not None else [IN_VMEM] * 3,
        out_shape=out_shape,
        scratch_shapes=scratch,
        compiler_params=params(ATT_MIB),
        cost_estimate=cost(4 * rows * keys * heads * HD, 4 * keys * HD, rows * keys * heads),
        name="attend",
    )(*args)


def butterfly(tiles):
    count = len(tiles)
    span = 1
    while span < count:
        out = list(tiles)
        for at in range(count):
            if not at & span:
                a, b = tiles[at], tiles[at | span]
                out[at], out[at | span] = a + b, a - b
        tiles = out
        span *= 2
    return tiles


def out_kernel(counts, steps, chunk, sign_ref, t_ref, *refs):
    parts = len(counts)
    blocks, at_block = [], 0
    for n in counts:
        blocks.append(refs[at_block : at_block + n])
        at_block += n
    w_ref, b_ref, s_ref, mid, rot, acc = refs[at_block:]
    rows = b_ref.shape[0]
    width = blocks[0][0].shape[1]
    here = width // HD
    heads = here * parts
    factor = heads ** (-0.5)

    strip = 16
    most = max(counts)
    span = rows // most
    for section in range(most):

        def turn(i, carry):
            at = pl.multiple_of(section * span + i * strip, strip)
            for m in range(parts):
                if len(blocks[m]) == 1:
                    ref, start = blocks[m][0], at
                else:
                    ref, start = blocks[m][section], pl.multiple_of(i * strip, strip)
                tiles = [
                    ref[pl.ds(start, strip), h * HD : (h + 1) * HD].astype(jnp.float32)
                    for h in range(here)
                ]
                for h, v in enumerate(butterfly(tiles)):
                    mid[m * here + h] = v
            for h in range(here):
                tiles = butterfly([mid[m * here + h] for m in range(parts)])
                for m in range(parts):
                    v = tiles[m] * (factor * sign_ref[m])
                    col = (m * here + h) * HD
                    rot[pl.ds(at, strip), col : col + HD] = clip_tile(v).astype(jnp.bfloat16)
            return carry

        lax.fori_loop(0, span // strip, turn, 0)

    depth = w_ref.shape[0] // steps
    for i in range(steps):
        part = jnp.dot(
            rot[:, i * depth : (i + 1) * depth],
            w_ref[i * depth : (i + 1) * depth, :],
            preferred_element_type=jnp.float32,
        )
        if i == 0:
            acc[...] = part
        else:
            acc[...] += part

    b = acc[...]
    t = t_ref[chunk * rows : (chunk + 1) * rows, :].astype(jnp.float32)
    b_ref[...] = b
    sums = [jnp.sum(v, axis=-1, keepdims=True) for v in (b * b, b * t, t * t)]
    lane = lax.broadcasted_iota(jnp.int32, (rows, 128), 1)
    wide = jnp.where(lane == 0, sums[0], jnp.where(lane == 1, sums[1], sums[2]))
    s_ref[...] = jnp.transpose(wide)[:8]


def project_out(flips, blocks, w_out, teacher, chunk):
    parts = len(blocks)
    counts = [len(b) for b in blocks]
    rows, width = blocks[0][0].shape
    depth, cols = w_out.shape
    steps = 4
    flat = [p for b in blocks for p in b]
    return pl.pallas_call(
        functools.partial(out_kernel, counts, steps, chunk),
        in_specs=[IN_SMEM] + [IN_VMEM] * (len(flat) + 2),
        out_specs=[IN_VMEM, IN_VMEM],
        out_shape=[
            jax.ShapeDtypeStruct((rows, cols), jnp.float32),
            jax.ShapeDtypeStruct((8, rows), jnp.float32),
        ],
        scratch_shapes=[
            pltpu.VMEM((parts * width // HD, 16, HD), jnp.float32),
            pltpu.VMEM((rows, depth), jnp.bfloat16),
            pltpu.VMEM((rows, cols), jnp.float32),
        ],
        compiler_params=params(OUT_MIB),
        cost_estimate=cost(2 * rows * depth * cols, 2 * depth * (rows + cols) + 6 * rows * cols),
        name="project_out",
    )(flips, teacher, *flat, w_out)


def final_kernel(features, chunks, parts, *refs):
    branches, stats = refs[:chunks], refs[chunks : chunks + parts]
    student_ref, loss_ref = refs[chunks + parts :]
    total = stats[0][...]
    for at in range(1, parts):
        total = total + stats[at][...]
    inverse = lax.rsqrt(total[0:1] * (1.0 / features) + EPS_OUT)
    loss = inverse * inverse * total[0:1] - 2.0 * inverse * total[1:2] + total[2:3]
    loss_ref[...] = jnp.maximum(loss, 0.0) * (1.0 / features)
    column = jnp.transpose(jnp.broadcast_to(inverse, total.shape))[:, :1]
    rows = branches[0].shape[0]
    for at in range(chunks):
        scale = column[at * rows : (at + 1) * rows]
        student_ref[at * rows : (at + 1) * rows, :] = (branches[at][...] * scale).astype(
            jnp.bfloat16
        )


def final(features, branches, stats):
    chunks, parts = len(branches), len(stats)
    part_rows, cols = branches[0].shape
    rows = part_rows * chunks
    return pl.pallas_call(
        functools.partial(final_kernel, features, chunks, parts),
        grid=(1,),
        in_specs=[whole((part_rows, cols))] * chunks + [whole((8, rows))] * parts,
        out_specs=[whole((rows, cols)), whole((1, rows))],
        out_shape=[
            jax.ShapeDtypeStruct((rows, cols), jnp.bfloat16),
            jax.ShapeDtypeStruct((1, rows), jnp.float32),
        ],
        compiler_params=params(16),
        cost_estimate=cost(2 * rows * cols, 6 * rows * cols),
        name="final",
    )(*branches, *stats)


def swap(x, mask):
    count = lax.axis_size("tp")
    return lax.ppermute(x, "tp", [(i, i ^ mask) for i in range(count)])


def send_up(x, distance):
    count = lax.axis_size("ctx")
    return lax.ppermute(x, "ctx", [(i, i + distance) for i in range(count - distance)])


def after(x, *others):
    return lax.optimization_barrier((x,) + others)[0]


def gather(own, core_after=None, beside=None):
    count = lax.axis_size("tp")
    got = {0: [own]}
    masks = [1 << b for b in range(1, count.bit_length() - 1)]
    if len(masks) >= 2:
        a, b = masks[0], masks[1]
        half = own.shape[0] // (2 * EXTRA) * EXTRA
        got[a] = [swap(own, a)]
        got[b] = [swap(own, b)]
        via_a, via_b = got[a][0], got[b][0]
        got[1] = [swap(own, 1)]
        if beside is not None:
            first = beside(got[1][0])
            via_a, via_b = after(via_a, first), after(via_b, first)
        got[a | b] = [swap(via_a[:half], b), swap(via_b[half:], a)]
        masks = masks[2:]
    if core_after is not None:
        for m in got:
            if m > 1:
                got[m] = [after(p, core_after) for p in got[m]]
    if count > 1:
        for m in list(got):
            if m | 1 not in got:
                got[m | 1] = [swap(p, 1) for p in got[m]]
    for mask in masks:
        for m in list(got):
            got[m | mask] = [swap(p, mask) for p in got[m]]
    return [got[m] for m in range(count)]


def body(hidden_in, norm_gain, w_query, w_key, w_value, sign_bits, w_out, teacher):
    rows = hidden_in.shape[0]
    half = rows // HALVES
    tp_count = lax.axis_size("tp")
    ctx_count = lax.axis_size("ctx")
    features = hidden_in.shape[1] * tp_count
    tp_at = lax.axis_index("tp")
    ctx_at = jnp.reshape(lax.axis_index("ctx"), (1,)).astype(jnp.int32)
    masks = jnp.arange(tp_count, dtype=jnp.int32)
    order = tp_at ^ masks
    shared = tp_at & masks
    parity = jnp.zeros_like(shared)
    for bit in range(tp_count.bit_length()):
        parity = parity ^ (shared >> bit & 1)
    flips = (1 - 2 * parity).astype(jnp.float32)
    signs = (2 * sign_bits - 1).astype(jnp.float32)
    gain = norm_gain.reshape(-1, GROUP)

    gain, order, ctx_at, flips, signs = lax.optimization_barrier(
        (gain, order, ctx_at, flips, signs)
    )
    clipped = pre(hidden_in, gain)
    squares = None

    kv_cols = w_key.shape[1]
    sharing = HD // kv_cols if kv_cols < HD else 1
    kv_heads = kv_cols * sharing // HD
    queries, kvs = [], []
    for at in range(HALVES):
        own = clipped[at]
        if at:
            own = after(own, *[b[0] for b in blocks[2:6:2]], loaded[1])
        if at:
            blocks = gather(own, core_after=queries[-1])
        else:
            loaded = []

            def bring(token):
                first = after(w_query, token, order, ctx_at, flips, signs)
                loaded.extend(load(first, w_key, w_value, w_out))
                return loaded[1]

            blocks = gather(own, beside=bring)
            if not loaded:
                bring(own)
        part = squares
        if at and ctx_count > 1:
            part = after(part, kvs[0][1])
        q, kv, *rest = proj(order, blocks, at, half, part, *loaded[:3])
        if rest:
            squares = rest[0]
        if sharing > 1:
            k, v = kv[:, :kv_cols], kv[:, kv_cols:]
            for bit in range(sharing.bit_length() - 1):
                upper = tp_at >> bit & 1 == 1
                k2, v2 = swap(k, 1 << bit), swap(v, 1 << bit)
                k, v = (
                    jnp.where(
                        upper,
                        jnp.concatenate([far, near], axis=1),
                        jnp.concatenate([near, far], axis=1),
                    )
                    for near, far in ((k, k2), (v, v2))
                )
            kv = jnp.concatenate([k, v], axis=1)
        queries.append(q)
        kvs.append([kv] + [send_up(kv, hop) for hop in range(1, ctx_count)])

    states = []
    for at in range(HALVES):
        near = [(p * half, kvs[p][0]) for p in range(at + 1)]
        far = [(hop, kvs[p][hop]) for p in range(HALVES - 1) for hop in range(1, ctx_count)]
        states.append(
            attend(ctx_at, queries[at], at * half, kv_heads, near, far, None, None)
        )
    branches, stats = [], []
    for at in range(HALVES):
        far = [(hop, kvs[HALVES - 1][hop]) for hop in range(1, ctx_count)]
        signed = attend(
            ctx_at, queries[at], at * half, kv_heads, [], far, states[at], signs
        )
        if at:
            signed = after(signed, *[b[0] for b in blocks[2:6:2]])
        blocks = gather(signed, branches[-1] if at else None)
        b, s = project_out(flips, blocks, loaded[3], teacher, at)
        branches.append(b)
        stats.append(s)
    stat = jnp.concatenate(stats, axis=1)
    for bit in range(tp_count.bit_length() - 1):
        stat = stat + swap(stat, 1 << bit)
    student, loss = final(features, branches, [stat])
    return student, loss.reshape(rows)


def solution(mesh):
    in_specs = (
        P("ctx", "tp"),
        P("tp"),
        P(None, "tp"),
        P(None, "tp"),
        P(None, "tp"),
        P("tp", None),
        P(None, "tp"),
        P("ctx", "tp"),
    )
    out_specs = (P("ctx", "tp"), P("ctx"))
    return jax.shard_map(body, mesh=mesh, in_specs=in_specs, out_specs=out_specs, check_vma=False)
```

```python
import functools
import math

import jax
import jax.numpy as jnp
from jax import lax
from jax.experimental import pallas as pl
from jax.experimental.pallas import tpu as pltpu
from jax.sharding import PartitionSpec as P

HD = 128
GROUP = 128
EPS_IN = 1e-05
EPS_OUT = 1e-06
CLIP_RATIO = 0.9
FAR_BELOW = -1e30
LOG2E = math.log2(math.e)
HALVES = 2
EXTRA = 16
LOAD_PARTS = 4
LOAD_MIB = 38
PROJ_MIB = 12
ATT_MIB = 12
OUT_MIB = 12
MIB = 1024 * 1024


def params(mib, **kw):
    return pltpu.CompilerParams(vmem_limit_bytes=mib * MIB, **kw)


def whole(shape):
    zeros = (0,) * len(shape)
    return pl.BlockSpec(shape, lambda *_: zeros)


IN_SMEM = pl.BlockSpec(memory_space=pltpu.SMEM)
IN_VMEM = pl.BlockSpec(memory_space=pltpu.VMEM)
ANYWHERE = pl.BlockSpec(memory_space=pl.ANY)
IN_HBM = pl.BlockSpec(memory_space=pltpu.HBM)


def cost(flops, moved, trans=0):
    return pl.CostEstimate(flops=int(flops), bytes_accessed=int(moved), transcendentals=int(trans))


def clip_tile(v):
    limit = CLIP_RATIO * jnp.max(jnp.abs(v), axis=-1, keepdims=True)
    return jnp.clip(v, -limit, limit)


def pre_kernel(h_hbm, g_hbm, *refs):
    outs, (h_all, g_ref, sem) = refs[:HALVES], refs[HALVES:]
    rows, width = h_all.shape
    steps = sem.shape[0] - 1
    part = rows // steps
    copies = [pltpu.make_async_copy(g_hbm, g_ref, sem.at[steps])]
    for i in range(steps):
        at = slice(i * part, (i + 1) * part)
        copies.append(pltpu.make_async_copy(h_hbm.at[at], h_all.at[at], sem.at[i]))
    for copy in copies:
        copy.start()
    copies[0].wait()
    for i in range(steps):
        copies[i + 1].wait()
        total = jnp.zeros((part, GROUP), jnp.float32)
        row = i * part % (rows // HALVES)
        c_ref = outs[i * part // (rows // HALVES)]
        for at in range(0, width, GROUP):
            h = h_all[i * part : (i + 1) * part, at : at + GROUP].astype(jnp.float32)
            total = total + h * h
            v = h * g_ref[at // GROUP : at // GROUP + 1, :].astype(jnp.float32)
            c_ref[row : row + part, at : at + GROUP] = clip_tile(v).astype(jnp.bfloat16)
        sums = jnp.sum(total, axis=-1, keepdims=True)
        sums = jnp.transpose(jnp.broadcast_to(sums, (part, 128)))[:EXTRA]
        row = lax.broadcasted_iota(jnp.int32, sums.shape, 0)
        left = sums
        for place in range(3):
            piece = left.astype(jnp.bfloat16).astype(jnp.float32)
            left = left - piece
            sums = jnp.where(row == place, piece, sums)
        outs[0][rows // HALVES :, i * part : (i + 1) * part] = sums.astype(jnp.bfloat16)


def pre(hidden, gain):
    rows, width = hidden.shape
    steps = HALVES * 2
    return pl.pallas_call(
        pre_kernel,
        in_specs=[IN_HBM] * 2,
        out_specs=[IN_VMEM] * HALVES,
        out_shape=[
            pltpu.VMEM((rows // HALVES + (0 if i else EXTRA), width), jnp.bfloat16)
            for i in range(HALVES)
        ],
        scratch_shapes=[
            pltpu.VMEM((rows, width), jnp.bfloat16),
            pltpu.VMEM(gain.shape, jnp.bfloat16),
            pltpu.SemaphoreType.DMA((steps + 1,)),
        ],
        compiler_params=params(62),
        cost_estimate=cost(8 * rows * width, 4 * rows * width),
        name="pre",
    )(hidden, gain)


def load_kernel(count, *refs):
    sources, goals, sem = refs[:count], refs[count : 2 * count], refs[-1]
    copies = []
    for i in range(count):
        depth = sources[i].shape[0] // LOAD_PARTS
        for p in range(LOAD_PARTS):
            at = slice(p * depth, (p + 1) * depth)
            copies.append(
                pltpu.make_async_copy(sources[i].at[at], goals[i].at[at], sem.at[i, p])
            )
    for copy in copies:
        copy.start()
    for copy in copies:
        copy.wait()


def load(*weights):
    count = len(weights)
    return pl.pallas_call(
        functools.partial(load_kernel, count),
        in_specs=[IN_HBM] * count,
        out_specs=[IN_VMEM] * count,
        out_shape=[pltpu.VMEM(w.shape, w.dtype) for w in weights],
        scratch_shapes=[pltpu.SemaphoreType.DMA((count, LOAD_PARTS))],
        compiler_params=params(LOAD_MIB),
        cost_estimate=cost(0, 2 * sum(w.size * 2 for w in weights)),
        name="load",
    )(*weights)


def proj_kernel(counts, chunk, order_ref, *refs):
    depth = len(counts)
    blocks = refs[: sum(counts)]
    refs = refs[sum(counts) :]
    if chunk:
        wq_ref, wk_ref, wv_ref, ss_ref, q_ref, kv_ref, accq, acck, accv = refs
        squares = ss_ref[...]
    else:
        wq_ref, wk_ref, wv_ref, q_ref, kv_ref, ss_ref, accq, acck, accv = refs
        squares = jnp.zeros((1, ss_ref.shape[1]), jnp.float32)
    rows = q_ref.shape[0]
    nk = wk_ref.shape[1]
    k_rows = blocks[0].shape[1]
    at_block = 0
    for k in range(depth):
        at = pl.ds(pl.multiple_of(order_ref[k] * k_rows, k_rows), k_rows)
        mine = [b[...] for b in blocks[at_block : at_block + counts[k]]]
        at_block += counts[k]
        if not chunk:
            body_rows = mine[-1].shape[0] - EXTRA
            tail = mine[-1][body_rows:, : ss_ref.shape[1]].astype(jnp.float32)
            squares = squares + (tail[0:1] + tail[1:2] + tail[2:3])
            mine[-1] = mine[-1][:body_rows]
        left = mine[0] if len(mine) == 1 else jnp.concatenate(mine, axis=0)
        wq, wk, wv = wq_ref[at, :], wk_ref[at, :], wv_ref[at, :]
        if nk % 128 == 0:
            both = jnp.dot(
                left, jnp.concatenate([wk, wv], axis=1), preferred_element_type=jnp.float32
            )
            parts = (both[:, :nk], both[:, nk:])
        else:
            parts = [jnp.dot(left, w, preferred_element_type=jnp.float32) for w in (wk, wv)]
        first = jnp.dot(left, wq, preferred_element_type=jnp.float32)
        for part, acc in zip((first, *parts), (accq, acck, accv)):
            if k == 0:
                acc[...] = part
            else:
                acc[...] += part

    features = k_rows * depth
    if not chunk:
        squares = jnp.broadcast_to(squares, ss_ref.shape)
        ss_ref[...] = squares
    squares = squares[:, chunk * rows : (chunk + 1) * rows]
    inverse = lax.rsqrt(squares * (1.0 / features) + EPS_IN)
    scale = jnp.transpose(inverse)[:, :1]
    q_ref[...] = (accq[...] * scale).astype(jnp.bfloat16)
    kv_ref[:, :nk] = (acck[...] * scale).astype(jnp.bfloat16)
    kv_ref[:, nk:] = (accv[...] * scale).astype(jnp.bfloat16)


def proj(order, blocks, chunk, rows, squares, wq, wk, wv):
    depth = len(blocks)
    counts = [len(b) for b in blocks]
    part_cols = blocks[0][0].shape[1]
    nq, nk, nv = wq.shape[1], wk.shape[1], wv.shape[1]
    n = nq + nk + nv
    flat = [p for b in blocks for p in b]
    args = [order, *flat, wq, wk, wv]
    out_shape = [
        jax.ShapeDtypeStruct((rows, nq), jnp.bfloat16),
        jax.ShapeDtypeStruct((rows, nk + nv), jnp.bfloat16),
    ]
    if chunk:
        args.append(squares)
    else:
        out_shape.append(jax.ShapeDtypeStruct((8, rows * HALVES), jnp.float32))
    return pl.pallas_call(
        functools.partial(proj_kernel, counts, chunk),
        in_specs=[IN_SMEM] + [IN_VMEM] * (len(args) - 1),
        out_specs=[IN_VMEM] * len(out_shape),
        out_shape=out_shape,
        scratch_shapes=[pltpu.VMEM((rows, m), jnp.float32) for m in (nq, nk, nv)],
        compiler_params=params(PROJ_MIB),
        cost_estimate=cost(
            2 * rows * part_cols * depth * n, 2 * part_cols * depth * (rows + n)
        ),
        name="proj",
    )(*args)


def att_kernel(first, kv_heads, near, far, begins, ends, me_ref, q_ref, *refs):
    count = len(near) + len(far)
    kvs, refs = refs[:count], refs[count:]
    if not begins:
        high_in, total_in, accum_in, *refs = refs
    if ends:
        sign_ref, o_ref, high, total, accum = refs
    else:
        high, total, accum = refs
    rows = q_ref.shape[0]
    heads = q_ref.shape[1] // HD
    part = kvs[0].shape[0]
    group = heads // kv_heads
    scale = HD ** (-0.5) * LOG2E

    if not begins:
        high[...] = high_in[...]
        total[...] = total_in[...]
        accum[...] = accum_in[...]

    def visit(kv_ref, start, fresh):
        masked = start is not None and start + part > first
        scores, turned = [], []
        for kv in range(kv_heads):
            at = (kv_heads + kv) * HD
            turned.append(jnp.transpose(kv_ref[:, at : at + HD]))
        for head in range(heads):
            kv = head // group
            q = q_ref[:, head * HD : (head + 1) * HD]
            k = kv_ref[:, kv * HD : (kv + 1) * HD]
            s = lax.dot_general(
                k, q, (((1,), (1,)), ((), ())), preferred_element_type=jnp.float32
            )
            if masked:
                kpos = start + lax.broadcasted_iota(jnp.int32, s.shape, 0)
                qpos = first + lax.broadcasted_iota(jnp.int32, s.shape, 1)
                s = jnp.where(kpos <= qpos, s, FAR_BELOW)
            scores.append(s)
        for head in range(heads):
            s = scores[head]
            best = jnp.max(s, axis=0, keepdims=True)
            if not fresh:
                before = high[head : head + 1]
                best = jnp.maximum(best, before)
            w = jnp.exp2((s - best) * scale)
            sums = jnp.sum(w, axis=0, keepdims=True)
            mixed = jnp.dot(
                turned[head // group], w.astype(jnp.bfloat16), preferred_element_type=jnp.float32
            )
            if fresh:
                total[head : head + 1] = sums
                accum[head] = mixed
            else:
                decay = jnp.exp2((before - best) * scale)
                total[head : head + 1] = total[head : head + 1] * decay + sums
                accum[head] = accum[head] * decay + mixed
            high[head : head + 1] = best

    for at, start in enumerate(near):
        visit(kvs[at], start, begins and at == 0)
    for at, hop in enumerate(far):

        @pl.when(me_ref[0] >= hop)
        def _():
            visit(kvs[len(near) + at], None, False)

    if ends:
        for head in range(heads):
            att = jnp.transpose(accum[head] / total[head : head + 1])
            att = att.astype(jnp.bfloat16).astype(jnp.float32)
            o_ref[:, head * HD : (head + 1) * HD] = (att * sign_ref[head : head + 1, :]).astype(
                jnp.bfloat16
            )


def attend(me, q, first, kv_heads, near, far, state, signs):
    rows = q.shape[0]
    heads = q.shape[1] // HD
    kvs = [kv for _, kv in near + far]
    keys = sum(kv.shape[0] for kv in kvs)
    shapes = [(max(heads, 8), rows), (max(heads, 8), rows), (heads, HD, rows)]
    args = [me, q, *kvs]
    if state is not None:
        args += list(state)
    if signs is None:
        out_shape = [jax.ShapeDtypeStruct(shape, jnp.float32) for shape in shapes]
        scratch = []
    else:
        args.append(signs)
        out_shape = jax.ShapeDtypeStruct((rows, heads * HD), jnp.bfloat16)
        scratch = [pltpu.VMEM(shape, jnp.float32) for shape in shapes]
    near_at, far_at = [n for n, _ in near], [n for n, _ in far]
    kernel = functools.partial(
        att_kernel, first, kv_heads, near_at, far_at, state is None, signs is not None
    )
    return pl.pallas_call(
        kernel,
        in_specs=[IN_SMEM] + [IN_VMEM] * (len(args) - 1),
        out_specs=IN_VMEM if signs is not None else [IN_VMEM] * 3,
        out_shape=out_shape,
        scratch_shapes=scratch,
        compiler_params=params(ATT_MIB),
        cost_estimate=cost(4 * rows * keys * heads * HD, 4 * keys * HD, rows * keys * heads),
        name="attend",
    )(*args)


def butterfly(tiles):
    count = len(tiles)
    span = 1
    while span < count:
        out = list(tiles)
        for at in range(count):
            if not at & span:
                a, b = tiles[at], tiles[at | span]
                out[at], out[at | span] = a + b, a - b
        tiles = out
        span *= 2
    return tiles


def out_kernel(counts, steps, chunk, sign_ref, t_ref, *refs):
    parts = len(counts)
    blocks, at_block = [], 0
    for n in counts:
        blocks.append(refs[at_block : at_block + n])
        at_block += n
    w_ref, b_ref, s_ref, mid, rot, acc = refs[at_block:]
    rows = b_ref.shape[0]
    width = blocks[0][0].shape[1]
    here = width // HD
    heads = here * parts
    factor = heads ** (-0.5)

    strip = 16
    most = max(counts)
    span = rows // most
    for section in range(most):

        def turn(i, carry):
            at = pl.multiple_of(section * span + i * strip, strip)
            for m in range(parts):
                if len(blocks[m]) == 1:
                    ref, start = blocks[m][0], at
                else:
                    ref, start = blocks[m][section], pl.multiple_of(i * strip, strip)
                tiles = [
                    ref[pl.ds(start, strip), h * HD : (h + 1) * HD].astype(jnp.float32)
                    for h in range(here)
                ]
                for h, v in enumerate(butterfly(tiles)):
                    mid[m * here + h] = v
            for h in range(here):
                tiles = butterfly([mid[m * here + h] for m in range(parts)])
                for m in range(parts):
                    v = tiles[m] * (factor * sign_ref[m])
                    col = (m * here + h) * HD
                    rot[pl.ds(at, strip), col : col + HD] = clip_tile(v).astype(jnp.bfloat16)
            return carry

        lax.fori_loop(0, span // strip, turn, 0)

    depth = w_ref.shape[0] // steps
    for i in range(steps):
        part = jnp.dot(
            rot[:, i * depth : (i + 1) * depth],
            w_ref[i * depth : (i + 1) * depth, :],
            preferred_element_type=jnp.float32,
        )
        if i == 0:
            acc[...] = part
        else:
            acc[...] += part

    b = acc[...]
    t = t_ref[chunk * rows : (chunk + 1) * rows, :].astype(jnp.float32)
    b_ref[...] = b
    sums = [jnp.sum(v, axis=-1, keepdims=True) for v in (b * b, b * t, t * t)]
    lane = lax.broadcasted_iota(jnp.int32, (rows, 128), 1)
    wide = jnp.where(lane == 0, sums[0], jnp.where(lane == 1, sums[1], sums[2]))
    s_ref[...] = jnp.transpose(wide)[:8]


def project_out(flips, blocks, w_out, teacher, chunk):
    parts = len(blocks)
    counts = [len(b) for b in blocks]
    rows, width = blocks[0][0].shape
    depth, cols = w_out.shape
    steps = 4
    flat = [p for b in blocks for p in b]
    return pl.pallas_call(
        functools.partial(out_kernel, counts, steps, chunk),
        in_specs=[IN_SMEM] + [IN_VMEM] * (len(flat) + 2),
        out_specs=[IN_VMEM, IN_VMEM],
        out_shape=[
            jax.ShapeDtypeStruct((rows, cols), jnp.float32),
            jax.ShapeDtypeStruct((8, rows), jnp.float32),
        ],
        scratch_shapes=[
            pltpu.VMEM((parts * width // HD, 16, HD), jnp.float32),
            pltpu.VMEM((rows, depth), jnp.bfloat16),
            pltpu.VMEM((rows, cols), jnp.float32),
        ],
        compiler_params=params(OUT_MIB),
        cost_estimate=cost(2 * rows * depth * cols, 2 * depth * (rows + cols) + 6 * rows * cols),
        name="project_out",
    )(flips, teacher, *flat, w_out)


def final_kernel(features, chunks, parts, *refs):
    branches, stats = refs[:chunks], refs[chunks : chunks + parts]
    student_ref, loss_ref = refs[chunks + parts :]
    total = stats[0][...]
    for at in range(1, parts):
        total = total + stats[at][...]
    inverse = lax.rsqrt(total[0:1] * (1.0 / features) + EPS_OUT)
    loss = inverse * inverse * total[0:1] - 2.0 * inverse * total[1:2] + total[2:3]
    loss_ref[...] = jnp.maximum(loss, 0.0) * (1.0 / features)
    column = jnp.transpose(jnp.broadcast_to(inverse, total.shape))[:, :1]
    rows = branches[0].shape[0]
    for at in range(chunks):
        scale = column[at * rows : (at + 1) * rows]
        student_ref[at * rows : (at + 1) * rows, :] = (branches[at][...] * scale).astype(
            jnp.bfloat16
        )


def final(features, branches, stats):
    chunks, parts = len(branches), len(stats)
    part_rows, cols = branches[0].shape
    rows = part_rows * chunks
    return pl.pallas_call(
        functools.partial(final_kernel, features, chunks, parts),
        grid=(1,),
        in_specs=[whole((part_rows, cols))] * chunks + [whole((8, rows))] * parts,
        out_specs=[whole((rows, cols)), whole((1, rows))],
        out_shape=[
            jax.ShapeDtypeStruct((rows, cols), jnp.bfloat16),
            jax.ShapeDtypeStruct((1, rows), jnp.float32),
        ],
        compiler_params=params(16),
        cost_estimate=cost(2 * rows * cols, 6 * rows * cols),
        name="final",
    )(*branches, *stats)


def swap(x, mask):
    count = lax.axis_size("tp")
    return lax.ppermute(x, "tp", [(i, i ^ mask) for i in range(count)])


def send_up(x, distance, first=0):
    count = lax.axis_size("ctx")
    return lax.ppermute(x, "ctx", [(i, i + distance) for i in range(first, count - distance)])


def after(x, *others):
    return lax.optimization_barrier((x,) + others)[0]


def gather(own, core_after=None, beside=None):
    count = lax.axis_size("tp")
    got, direct = {0: [own]}, []
    masks = [1 << b for b in range(1, count.bit_length() - 1)]
    if len(masks) >= 2:
        a, b = masks[0], masks[1]
        half = own.shape[0] // (2 * EXTRA) * EXTRA
        got[a] = [swap(own, a)]
        got[b] = [swap(own, b)]
        direct = via_a, via_b = got[a][0], got[b][0]
        got[1] = [swap(own, 1)]
        if beside is not None:
            first = beside(got[1][0])
            via_a, via_b = after(via_a, first), after(via_b, first)
        got[a | b] = [swap(via_a[:half], b), swap(via_b[half:], a)]
        first = got[a | b][0]
        got[a], got[b] = [after(got[a][0], first)], [after(got[b][0], first)]
        masks = masks[2:]
    if core_after is not None:
        for m in got:
            if m > 1:
                got[m] = [after(p, core_after) for p in got[m]]
    if count > 1:
        for m in list(got):
            if m | 1 not in got:
                got[m | 1] = [swap(p, 1) for p in got[m]]
    for mask in masks:
        for m in list(got):
            got[m | mask] = [swap(p, mask) for p in got[m]]
    return [got[m] for m in range(count)], direct


def body(hidden_in, norm_gain, w_query, w_key, w_value, sign_bits, w_out, teacher):
    rows = hidden_in.shape[0]
    half = rows // HALVES
    tp_count = lax.axis_size("tp")
    ctx_count = lax.axis_size("ctx")
    features = hidden_in.shape[1] * tp_count
    tp_at = lax.axis_index("tp")
    ctx_at = jnp.reshape(lax.axis_index("ctx"), (1,)).astype(jnp.int32)
    masks = jnp.arange(tp_count, dtype=jnp.int32)
    order = tp_at ^ masks
    shared = tp_at & masks
    parity = jnp.zeros_like(shared)
    for bit in range(tp_count.bit_length()):
        parity = parity ^ (shared >> bit & 1)
    flips = (1 - 2 * parity).astype(jnp.float32)
    signs = (2 * sign_bits - 1).astype(jnp.float32)
    gain = norm_gain.reshape(-1, GROUP)

    gain, order, ctx_at, flips, signs = lax.optimization_barrier(
        (gain, order, ctx_at, flips, signs)
    )
    clipped = pre(hidden_in, gain)
    squares = None

    kv_cols = w_key.shape[1]
    sharing = HD // kv_cols if kv_cols < HD else 1
    kv_heads = kv_cols * sharing // HD
    queries, kvs = [], []
    for at in range(HALVES):
        own = clipped[at]
        if at:
            own = after(own, *neighbours, loaded[1])
        if at:
            blocks, neighbours = gather(own, core_after=queries[-1])
        else:
            loaded = []

            def bring(token):
                first = after(w_query, token, order, ctx_at, flips, signs)
                loaded.extend(load(first, w_key, w_value, w_out))
                return loaded[1]

            blocks, neighbours = gather(own, beside=bring)
            if not loaded:
                bring(own)
        part = squares
        q, kv, *rest = proj(order, blocks, at, half, part, *loaded[:3])
        if rest:
            squares = rest[0]
        if sharing > 1:
            k, v = kv[:, :kv_cols], kv[:, kv_cols:]
            for bit in range(sharing.bit_length() - 1):
                upper = tp_at >> bit & 1 == 1
                k2, v2 = swap(k, 1 << bit), swap(v, 1 << bit)
                k, v = (
                    jnp.where(
                        upper,
                        jnp.concatenate([far, near], axis=1),
                        jnp.concatenate([near, far], axis=1),
                    )
                    for near, far in ((k, k2), (v, v2))
                )
            kv = jnp.concatenate([k, v], axis=1)
        queries.append(q)
        kvs.append([kv])
        for hop in range(1, ctx_count):
            if at == HALVES - 1:
                kvs[at].append(send_up(kv, hop))
            elif hop < 2:
                kvs[at].append(send_up(kvs[at][-1], 1, hop - 1))
        for near in kvs[:at]:
            for hop in range(len(near), ctx_count):
                near.append(send_up(after(near[-1], q), 1, hop - 1))

    states = []
    for at in range(HALVES):
        near = [(p * half, kvs[p][0]) for p in range(at + 1)]
        far = [(hop, kvs[p][hop]) for p in range(HALVES - 1) for hop in range(1, ctx_count)]
        states.append(
            attend(ctx_at, queries[at], at * half, kv_heads, near, far, None, None)
        )
    branches, stats = [], []
    for at in range(HALVES):
        far = [(hop, kvs[HALVES - 1][hop]) for hop in range(1, ctx_count)]
        signed = attend(
            ctx_at, queries[at], at * half, kv_heads, [], far, states[at], signs
        )
        if at:
            signed = after(signed, *neighbours)
        blocks, neighbours = gather(signed, branches[-1] if at else None)
        b, s = project_out(flips, blocks, loaded[3], teacher, at)
        branches.append(b)
        stats.append(s)
    stat = jnp.concatenate(stats, axis=1)
    for bit in range(tp_count.bit_length() - 1):
        stat = stat + swap(stat, 1 << bit)
    student, loss = final(features, branches, [stat])
    return student, loss.reshape(rows)


def solution(mesh):
    in_specs = (
        P("ctx", "tp"),
        P("tp"),
        P(None, "tp"),
        P(None, "tp"),
        P(None, "tp"),
        P("tp", None),
        P(None, "tp"),
        P("ctx", "tp"),
    )
    out_specs = (P("ctx", "tp"), P("ctx"))
    return jax.shard_map(body, mesh=mesh, in_specs=in_specs, out_specs=out_specs, check_vma=False)
```

```python
import functools
import math

import jax
import jax.numpy as jnp
from jax import lax
from jax.experimental import pallas as pl
from jax.experimental.pallas import tpu as pltpu
from jax.sharding import PartitionSpec as P

HD = 128
GROUP = 128
EPS_IN = 1e-05
EPS_OUT = 1e-06
CLIP_RATIO = 0.9
FAR_BELOW = -1e30
LOG2E = math.log2(math.e)
HALVES = 2
EXTRA = 16
LOAD_PARTS = 4
LOAD_MIB = 38
PROJ_MIB = 14
ATT_MIB = 12
OUT_MIB = 12
MIB = 1024 * 1024


def params(mib, **kw):
    return pltpu.CompilerParams(vmem_limit_bytes=mib * MIB, **kw)


def whole(shape):
    zeros = (0,) * len(shape)
    return pl.BlockSpec(shape, lambda *_: zeros)


IN_SMEM = pl.BlockSpec(memory_space=pltpu.SMEM)
IN_VMEM = pl.BlockSpec(memory_space=pltpu.VMEM)
ANYWHERE = pl.BlockSpec(memory_space=pl.ANY)
IN_HBM = pl.BlockSpec(memory_space=pltpu.HBM)


def cost(flops, moved, trans=0):
    return pl.CostEstimate(flops=int(flops), bytes_accessed=int(moved), transcendentals=int(trans))


def clip_tile(v):
    limit = CLIP_RATIO * jnp.max(jnp.abs(v), axis=-1, keepdims=True)
    return jnp.clip(v, -limit, limit)


def pre_kernel(h_hbm, g_hbm, *refs):
    c_ref, h_all, g_ref, sem = refs
    rows, width = h_all.shape
    steps = sem.shape[0] - 1
    part = rows // steps
    copies = [pltpu.make_async_copy(g_hbm, g_ref, sem.at[steps])]
    for i in range(steps):
        at = slice(i * part, (i + 1) * part)
        copies.append(pltpu.make_async_copy(h_hbm.at[at], h_all.at[at], sem.at[i]))
    for copy in copies:
        copy.start()
    copies[0].wait()
    for i in range(steps):
        copies[i + 1].wait()
        total = jnp.zeros((part, GROUP), jnp.float32)
        row = i * part
        for at in range(0, width, GROUP):
            h = h_all[i * part : (i + 1) * part, at : at + GROUP].astype(jnp.float32)
            total = total + h * h
            v = h * g_ref[at // GROUP : at // GROUP + 1, :].astype(jnp.float32)
            c_ref[row : row + part, at : at + GROUP] = clip_tile(v).astype(jnp.bfloat16)
        sums = jnp.sum(total, axis=-1, keepdims=True)
        sums = jnp.transpose(jnp.broadcast_to(sums, (part, 128)))[:EXTRA]
        row = lax.broadcasted_iota(jnp.int32, sums.shape, 0)
        left = sums
        for place in range(3):
            piece = left.astype(jnp.bfloat16).astype(jnp.float32)
            left = left - piece
            sums = jnp.where(row == place, piece, sums)
        c_ref[rows:, i * part : (i + 1) * part] = sums.astype(jnp.bfloat16)


def pre(hidden, gain):
    rows, width = hidden.shape
    steps = 4
    return pl.pallas_call(
        pre_kernel,
        in_specs=[IN_HBM] * 2,
        out_specs=IN_VMEM,
        out_shape=pltpu.VMEM((rows + EXTRA, width), jnp.bfloat16),
        scratch_shapes=[
            pltpu.VMEM((rows, width), jnp.bfloat16),
            pltpu.VMEM(gain.shape, jnp.bfloat16),
            pltpu.SemaphoreType.DMA((steps + 1,)),
        ],
        compiler_params=params(62),
        cost_estimate=cost(8 * rows * width, 4 * rows * width),
        name="pre",
    )(hidden, gain)


def load_kernel(count, *refs):
    sources, goals, sem = refs[:count], refs[count : 2 * count], refs[-1]
    copies = []
    for i in range(count):
        depth = sources[i].shape[0] // LOAD_PARTS
        for p in range(LOAD_PARTS):
            at = slice(p * depth, (p + 1) * depth)
            copies.append(
                pltpu.make_async_copy(sources[i].at[at], goals[i].at[at], sem.at[i, p])
            )
    for copy in copies:
        copy.start()
    for copy in copies:
        copy.wait()


def load(*weights):
    count = len(weights)
    return pl.pallas_call(
        functools.partial(load_kernel, count),
        in_specs=[IN_HBM] * count,
        out_specs=[IN_VMEM] * count,
        out_shape=[pltpu.VMEM(w.shape, w.dtype) for w in weights],
        scratch_shapes=[pltpu.SemaphoreType.DMA((count, LOAD_PARTS))],
        compiler_params=params(LOAD_MIB),
        cost_estimate=cost(0, 2 * sum(w.size * 2 for w in weights)),
        name="load",
    )(*weights)


def proj_kernel(counts, masks, begins, ends, order_ref, *refs):
    depth = len(counts)
    blocks, refs = refs[: sum(counts)], refs[sum(counts) :]
    wq_ref, wk_ref, wv_ref, *refs = refs
    if not begins:
        *before, ss_in = refs[:4]
        refs = refs[4:]
        squares = ss_in[0:1, :]
    else:
        before = [None] * 3
        squares = jnp.zeros((1, ss_rows(blocks)), jnp.float32)
    if ends:
        q_ref, kv_ref, *accs = refs
    else:
        *accs, ss_ref = refs
    nk = wk_ref.shape[1]
    k_rows = blocks[0].shape[1]
    at_block = 0
    for k in range(depth):
        at = pl.ds(pl.multiple_of(order_ref[masks[k]] * k_rows, k_rows), k_rows)
        mine = [b[...] for b in blocks[at_block : at_block + counts[k]]]
        at_block += counts[k]
        body_rows = mine[-1].shape[0] - EXTRA
        tail = mine[-1][body_rows:, : squares.shape[1]].astype(jnp.float32)
        squares = squares + (tail[0:1] + tail[1:2] + tail[2:3])
        mine[-1] = mine[-1][:body_rows]
        left = mine[0] if len(mine) == 1 else jnp.concatenate(mine, axis=0)
        wq, wk, wv = wq_ref[at, :], wk_ref[at, :], wv_ref[at, :]
        if nk % 128 == 0:
            both = jnp.dot(
                left, jnp.concatenate([wk, wv], axis=1), preferred_element_type=jnp.float32
            )
            parts = (both[:, :nk], both[:, nk:])
        else:
            parts = [jnp.dot(left, w, preferred_element_type=jnp.float32) for w in (wk, wv)]
        first = jnp.dot(left, wq, preferred_element_type=jnp.float32)
        for part, acc, old in zip((first, *parts), accs, before):
            if k:
                acc[...] += part
            elif not begins:
                acc[...] = old[...] + part
            else:
                acc[...] = part

    if not ends:
        ss_ref[...] = jnp.broadcast_to(squares, ss_ref.shape)
    else:
        accq, acck, accv = accs
        features = wq_ref.shape[0]
        squares = jnp.broadcast_to(squares, (8, squares.shape[1]))
        inverse = lax.rsqrt(squares * (1.0 / features) + EPS_IN)
        scale = jnp.transpose(inverse)[:, :1]
        q_ref[...] = (accq[...] * scale).astype(jnp.bfloat16)
        kv_ref[:, :nk] = (acck[...] * scale).astype(jnp.bfloat16)
        kv_ref[:, nk:] = (accv[...] * scale).astype(jnp.bfloat16)


def ss_rows(blocks):
    return blocks[0].shape[0] - EXTRA


def proj(order, blocks, rows, state, ends, wq, wk, wv):
    masks = sorted(blocks)
    blocks = [blocks[m] for m in masks]
    depth = len(blocks)
    counts = [len(b) for b in blocks]
    part_cols = blocks[0][0].shape[1]
    sizes = wq.shape[1], wk.shape[1], wv.shape[1]
    n = sum(sizes)
    flat = [p for b in blocks for p in b]
    args = [order, *flat, wq, wk, wv, *state]
    if ends:
        out_shape = [
            jax.ShapeDtypeStruct((rows, sizes[0]), jnp.bfloat16),
            jax.ShapeDtypeStruct((rows, sizes[1] + sizes[2]), jnp.bfloat16),
        ]
        scratch = [pltpu.VMEM((rows, m), jnp.float32) for m in sizes]
    else:
        out_shape = [pltpu.VMEM((rows, m), jnp.float32) for m in sizes]
        out_shape.append(jax.ShapeDtypeStruct((8, rows), jnp.float32))
        scratch = []
    return pl.pallas_call(
        functools.partial(proj_kernel, counts, masks, not state, ends),
        in_specs=[IN_SMEM] + [IN_VMEM] * (len(args) - 1),
        out_specs=[IN_VMEM] * len(out_shape),
        out_shape=out_shape,
        scratch_shapes=scratch,
        compiler_params=params(PROJ_MIB),
        cost_estimate=cost(
            2 * rows * part_cols * depth * n, 2 * part_cols * depth * (rows + n)
        ),
        name="proj",
    )(*args)


def att_kernel(first, kv_heads, near, far, begins, ends, me_ref, q_ref, *refs):
    count = near + len(far)
    kvs, refs = refs[:count], refs[count:]
    if not begins:
        high_in, total_in, accum_in, *refs = refs
    if ends:
        sign_ref, o_ref, high, total, accum = refs
    else:
        high, total, accum = refs
    rows = accum.shape[2]
    heads = q_ref.shape[1] // HD
    part = rows
    group = heads // kv_heads
    scale = HD ** (-0.5) * LOG2E

    if not begins:
        high[...] = high_in[...]
        total[...] = total_in[...]
        accum[...] = accum_in[...]

    def visit(kv_ref, sub, start, fresh):
        keys = slice(sub * part, (sub + 1) * part)
        masked = start is not None and start + part > first
        scores, turned = [], []
        for kv in range(kv_heads):
            at = (kv_heads + kv) * HD
            turned.append(jnp.transpose(kv_ref[keys, at : at + HD]))
        for head in range(heads):
            kv = head // group
            q = q_ref[first : first + rows, head * HD : (head + 1) * HD]
            k = kv_ref[keys, kv * HD : (kv + 1) * HD]
            s = lax.dot_general(
                k, q, (((1,), (1,)), ((), ())), preferred_element_type=jnp.float32
            )
            if masked:
                kpos = start + lax.broadcasted_iota(jnp.int32, s.shape, 0)
                qpos = first + lax.broadcasted_iota(jnp.int32, s.shape, 1)
                s = jnp.where(kpos <= qpos, s, FAR_BELOW)
            scores.append(s)
        for head in range(heads):
            s = scores[head]
            best = jnp.max(s, axis=0, keepdims=True)
            if not fresh:
                before = high[head : head + 1]
                best = jnp.maximum(best, before)
            w = jnp.exp2((s - best) * scale)
            sums = jnp.sum(w, axis=0, keepdims=True)
            mixed = jnp.dot(
                turned[head // group], w.astype(jnp.bfloat16), preferred_element_type=jnp.float32
            )
            if fresh:
                total[head : head + 1] = sums
                accum[head] = mixed
            else:
                decay = jnp.exp2((before - best) * scale)
                total[head : head + 1] = total[head : head + 1] * decay + sums
                accum[head] = accum[head] * decay + mixed
            high[head : head + 1] = best

    for at in range(near):
        for sub in range((first + rows) // part):
            visit(kvs[at], sub, sub * part, begins and at == 0 and sub == 0)
    for at, hop in enumerate(far):

        @pl.when(me_ref[0] >= hop)
        def _():
            for sub in range(kvs[near + at].shape[0] // part):
                visit(kvs[near + at], sub, None, False)

    if ends:
        for head in range(heads):
            att = jnp.transpose(accum[head] / total[head : head + 1])
            att = att.astype(jnp.bfloat16).astype(jnp.float32)
            o_ref[:, head * HD : (head + 1) * HD] = (att * sign_ref[head : head + 1, :]).astype(
                jnp.bfloat16
            )


def attend(me, q, first, rows, kv_heads, near, far, state, signs):
    heads = q.shape[1] // HD
    kvs = near + [kv for _, kv in far]
    keys = sum(kv.shape[0] for kv in kvs)
    shapes = [(max(heads, 8), rows), (max(heads, 8), rows), (heads, HD, rows)]
    args = [me, q, *kvs]
    if state is not None:
        args += list(state)
    if signs is None:
        out_shape = [jax.ShapeDtypeStruct(shape, jnp.float32) for shape in shapes]
        scratch = []
    else:
        args.append(signs)
        out_shape = jax.ShapeDtypeStruct((rows, heads * HD), jnp.bfloat16)
        scratch = [pltpu.VMEM(shape, jnp.float32) for shape in shapes]
    far_at = [n for n, _ in far]
    kernel = functools.partial(
        att_kernel, first, kv_heads, len(near), far_at, state is None, signs is not None
    )
    return pl.pallas_call(
        kernel,
        in_specs=[IN_SMEM] + [IN_VMEM] * (len(args) - 1),
        out_specs=IN_VMEM if signs is not None else [IN_VMEM] * 3,
        out_shape=out_shape,
        scratch_shapes=scratch,
        compiler_params=params(ATT_MIB),
        cost_estimate=cost(4 * rows * keys * heads * HD, 4 * keys * HD, rows * keys * heads),
        name="attend",
    )(*args)


def butterfly(tiles):
    count = len(tiles)
    span = 1
    while span < count:
        out = list(tiles)
        for at in range(count):
            if not at & span:
                a, b = tiles[at], tiles[at | span]
                out[at], out[at | span] = a + b, a - b
        tiles = out
        span *= 2
    return tiles


def out_kernel(counts, steps, chunk, sign_ref, t_ref, *refs):
    parts = len(counts)
    blocks, at_block = [], 0
    for n in counts:
        blocks.append(refs[at_block : at_block + n])
        at_block += n
    w_ref, b_ref, s_ref, mid, rot, acc = refs[at_block:]
    rows = b_ref.shape[0]
    width = blocks[0][0].shape[1]
    here = width // HD
    heads = here * parts
    factor = heads ** (-0.5)

    strip = 16
    most = max(counts)
    span = rows // most
    for section in range(most):

        def turn(i, carry):
            at = pl.multiple_of(section * span + i * strip, strip)
            for m in range(parts):
                if len(blocks[m]) == 1:
                    ref, start = blocks[m][0], at
                else:
                    ref, start = blocks[m][section], pl.multiple_of(i * strip, strip)
                tiles = [
                    ref[pl.ds(start, strip), h * HD : (h + 1) * HD].astype(jnp.float32)
                    for h in range(here)
                ]
                for h, v in enumerate(butterfly(tiles)):
                    mid[m * here + h] = v
            for h in range(here):
                tiles = butterfly([mid[m * here + h] for m in range(parts)])
                for m in range(parts):
                    v = tiles[m] * (factor * sign_ref[m])
                    col = (m * here + h) * HD
                    rot[pl.ds(at, strip), col : col + HD] = clip_tile(v).astype(jnp.bfloat16)
            return carry

        lax.fori_loop(0, span // strip, turn, 0)

    depth = w_ref.shape[0] // steps
    for i in range(steps):
        part = jnp.dot(
            rot[:, i * depth : (i + 1) * depth],
            w_ref[i * depth : (i + 1) * depth, :],
            preferred_element_type=jnp.float32,
        )
        if i == 0:
            acc[...] = part
        else:
            acc[...] += part

    b = acc[...]
    t = t_ref[chunk * rows : (chunk + 1) * rows, :].astype(jnp.float32)
    b_ref[...] = b
    sums = [jnp.sum(v, axis=-1, keepdims=True) for v in (b * b, b * t, t * t)]
    lane = lax.broadcasted_iota(jnp.int32, (rows, 128), 1)
    wide = jnp.where(lane == 0, sums[0], jnp.where(lane == 1, sums[1], sums[2]))
    s_ref[...] = jnp.transpose(wide)[:8]


def project_out(flips, blocks, w_out, teacher, chunk):
    parts = len(blocks)
    counts = [len(b) for b in blocks]
    rows, width = blocks[0][0].shape
    depth, cols = w_out.shape
    steps = 4
    flat = [p for b in blocks for p in b]
    return pl.pallas_call(
        functools.partial(out_kernel, counts, steps, chunk),
        in_specs=[IN_SMEM] + [IN_VMEM] * (len(flat) + 2),
        out_specs=[IN_VMEM, IN_VMEM],
        out_shape=[
            jax.ShapeDtypeStruct((rows, cols), jnp.float32),
            jax.ShapeDtypeStruct((8, rows), jnp.float32),
        ],
        scratch_shapes=[
            pltpu.VMEM((parts * width // HD, 16, HD), jnp.float32),
            pltpu.VMEM((rows, depth), jnp.bfloat16),
            pltpu.VMEM((rows, cols), jnp.float32),
        ],
        compiler_params=params(OUT_MIB),
        cost_estimate=cost(2 * rows * depth * cols, 2 * depth * (rows + cols) + 6 * rows * cols),
        name="project_out",
    )(flips, teacher, *flat, w_out)


def final_kernel(features, chunks, parts, *refs):
    branches, stats = refs[:chunks], refs[chunks : chunks + parts]
    student_ref, loss_ref = refs[chunks + parts :]
    total = stats[0][...]
    for at in range(1, parts):
        total = total + stats[at][...]
    inverse = lax.rsqrt(total[0:1] * (1.0 / features) + EPS_OUT)
    loss = inverse * inverse * total[0:1] - 2.0 * inverse * total[1:2] + total[2:3]
    loss_ref[...] = jnp.maximum(loss, 0.0) * (1.0 / features)
    column = jnp.transpose(jnp.broadcast_to(inverse, total.shape))[:, :1]
    rows = branches[0].shape[0]
    for at in range(chunks):
        scale = column[at * rows : (at + 1) * rows]
        student_ref[at * rows : (at + 1) * rows, :] = (branches[at][...] * scale).astype(
            jnp.bfloat16
        )


def final(features, branches, stats):
    chunks, parts = len(branches), len(stats)
    part_rows, cols = branches[0].shape
    rows = part_rows * chunks
    return pl.pallas_call(
        functools.partial(final_kernel, features, chunks, parts),
        grid=(1,),
        in_specs=[whole((part_rows, cols))] * chunks + [whole((8, rows))] * parts,
        out_specs=[whole((rows, cols)), whole((1, rows))],
        out_shape=[
            jax.ShapeDtypeStruct((rows, cols), jnp.bfloat16),
            jax.ShapeDtypeStruct((1, rows), jnp.float32),
        ],
        compiler_params=params(16),
        cost_estimate=cost(2 * rows * cols, 6 * rows * cols),
        name="final",
    )(*branches, *stats)


def swap(x, mask):
    count = lax.axis_size("tp")
    return lax.ppermute(x, "tp", [(i, i ^ mask) for i in range(count)])


def send_up(x, first):
    count = lax.axis_size("ctx")
    return lax.ppermute(x, "ctx", [(i, i + 1) for i in range(first, count - 1)])


def after(x, *others):
    return lax.optimization_barrier((x,) + others)[0]


def gather(own, core_after=None, beside=None, middle=None):
    count = lax.axis_size("tp")
    got = {0: [own]}
    masks = [1 << b for b in range(1, count.bit_length() - 1)]
    if len(masks) >= 2:
        a, b = masks[0], masks[1]
        half = own.shape[0] // (2 * EXTRA) * EXTRA
        via_a, via_b = swap(own, a), swap(own, b)
        got[1] = [swap(own, 1)]
        if beside is not None:
            token = beside(got[1][0])
            via_a, via_b = after(via_a, token), after(via_b, token)
        got[a], got[b] = [via_a], [via_b]
        diagonal = [swap(via_a[:half], b), swap(via_b[half:], a)]
        if core_after is not None:
            diagonal = [after(p, core_after) for p in diagonal]
            via_a, via_b = after(via_a, core_after), after(via_b, core_after)
        got[a | 1], got[b | 1] = [swap(via_a, 1)], [swap(via_b, 1)]
        got[a | b] = diagonal
        if middle is not None:
            token = middle(got)
            diagonal = [after(p, token) for p in diagonal]
        got[a | b | 1] = [swap(p, 1) for p in diagonal]
        masks = masks[2:]
    elif count > 1:
        got[1] = [swap(own, 1)]
    for mask in masks:
        for m in list(got):
            got[m | mask] = [swap(p, mask) for p in got[m]]
    return [got[m] for m in range(count)]


def body(hidden_in, norm_gain, w_query, w_key, w_value, sign_bits, w_out, teacher):
    rows = hidden_in.shape[0]
    half = rows // HALVES
    tp_count = lax.axis_size("tp")
    ctx_count = lax.axis_size("ctx")
    features = hidden_in.shape[1] * tp_count
    tp_at = lax.axis_index("tp")
    ctx_at = jnp.reshape(lax.axis_index("ctx"), (1,)).astype(jnp.int32)
    masks = jnp.arange(tp_count, dtype=jnp.int32)
    order = tp_at ^ masks
    shared = tp_at & masks
    parity = jnp.zeros_like(shared)
    for bit in range(tp_count.bit_length()):
        parity = parity ^ (shared >> bit & 1)
    flips = (1 - 2 * parity).astype(jnp.float32)
    signs = (2 * sign_bits - 1).astype(jnp.float32)
    gain = norm_gain.reshape(-1, GROUP)

    gain, order, ctx_at, flips, signs = lax.optimization_barrier(
        (gain, order, ctx_at, flips, signs)
    )
    clipped = pre(hidden_in, gain)

    kv_cols = w_key.shape[1]
    sharing = HD // kv_cols if kv_cols < HD else 1
    kv_heads = kv_cols * sharing // HD
    loaded = []

    def bring(token):
        first = after(w_query, token, order, ctx_at, flips, signs)
        loaded.extend(load(first, w_key, w_value, w_out))
        return loaded[1]

    early, state = [], []

    def begin(got):
        early.extend(sorted(got)[:-1])
        part = {m: got[m] for m in early}
        state.extend(proj(order, part, rows, (), False, *loaded[:3]))
        return state[-1]

    blocks = gather(clipped, beside=bring, middle=begin)
    if not loaded:
        bring(clipped)
    late = {m: block for m, block in enumerate(blocks) if m not in early}
    q, kv = proj(order, late, rows, state, True, *loaded[:3])
    if sharing > 1:
        k, v = kv[:, :kv_cols], kv[:, kv_cols:]
        for bit in range(sharing.bit_length() - 1):
            upper = tp_at >> bit & 1 == 1
            k2, v2 = swap(k, 1 << bit), swap(v, 1 << bit)
            k, v = (
                jnp.where(
                    upper,
                    jnp.concatenate([far, near], axis=1),
                    jnp.concatenate([near, far], axis=1),
                )
                for near, far in ((k, k2), (v, v2))
            )
        kv = jnp.concatenate([k, v], axis=1)
    kvs = [kv]
    for hop in range(1, ctx_count):
        kvs.append(send_up(kvs[-1], hop - 1))
    far = list(enumerate(kvs))[1:]

    states = [
        attend(ctx_at, q, at * half, half, kv_heads, [kv], far[:-1], None, None)
        for at in range(HALVES)
    ]
    branches, stats = [], []
    for at in range(HALVES):
        signed = attend(
            ctx_at, q, at * half, half, kv_heads, [], far[-1:], states[at], signs
        )
        if at:
            signed = after(signed, *[b[0] for b in blocks[2:6:2]])
        blocks = gather(signed, branches[-1] if at else None)
        b, s = project_out(flips, blocks, loaded[3], teacher, at)
        branches.append(b)
        stats.append(s)
    stat = jnp.concatenate(stats, axis=1)
    for bit in range(tp_count.bit_length() - 1):
        stat = stat + swap(stat, 1 << bit)
    student, loss = final(features, branches, [stat])
    return student, loss.reshape(rows)


def solution(mesh):
    in_specs = (
        P("ctx", "tp"),
        P("tp"),
        P(None, "tp"),
        P(None, "tp"),
        P(None, "tp"),
        P("tp", None),
        P(None, "tp"),
        P("ctx", "tp"),
    )
    out_specs = (P("ctx", "tp"), P("ctx"))
    return jax.shard_map(body, mesh=mesh, in_specs=in_specs, out_specs=out_specs, check_vma=False)
```

```python
import functools
import math

import jax
import jax.numpy as jnp
from jax import lax
from jax.experimental import pallas as pl
from jax.experimental.pallas import tpu as pltpu
from jax.sharding import PartitionSpec as P

HD = 128
GROUP = 128
EPS_IN = 1e-05
EPS_OUT = 1e-06
CLIP_RATIO = 0.9
FAR_BELOW = -1e30
LOG2E = math.log2(math.e)
HALVES = 2
EXTRA = 16
LOAD_PARTS = 4
LOAD_MIB = 38
PROJ_MIB = 14
ATT_MIB = 12
OUT_MIB = 12
MIB = 1024 * 1024


def params(mib, **kw):
    return pltpu.CompilerParams(vmem_limit_bytes=mib * MIB, **kw)


def whole(shape):
    zeros = (0,) * len(shape)
    return pl.BlockSpec(shape, lambda *_: zeros)


IN_SMEM = pl.BlockSpec(memory_space=pltpu.SMEM)
IN_VMEM = pl.BlockSpec(memory_space=pltpu.VMEM)
ANYWHERE = pl.BlockSpec(memory_space=pl.ANY)
IN_HBM = pl.BlockSpec(memory_space=pltpu.HBM)


def cost(flops, moved, trans=0):
    return pl.CostEstimate(flops=int(flops), bytes_accessed=int(moved), transcendentals=int(trans))


def clip_tile(v):
    limit = CLIP_RATIO * jnp.max(jnp.abs(v), axis=-1, keepdims=True)
    return jnp.clip(v, -limit, limit)


def pre_kernel(h_hbm, g_hbm, *refs):
    c_ref, h_all, g_ref, sem = refs
    rows, width = h_all.shape
    steps = sem.shape[0] - 1
    part = rows // steps
    copies = [pltpu.make_async_copy(g_hbm, g_ref, sem.at[steps])]
    for i in range(steps):
        at = slice(i * part, (i + 1) * part)
        copies.append(pltpu.make_async_copy(h_hbm.at[at], h_all.at[at], sem.at[i]))
    for copy in copies:
        copy.start()
    copies[0].wait()
    for i in range(steps):
        copies[i + 1].wait()
        total = jnp.zeros((part, GROUP), jnp.float32)
        row = i * part
        for at in range(0, width, GROUP):
            h = h_all[i * part : (i + 1) * part, at : at + GROUP].astype(jnp.float32)
            total = total + h * h
            v = h * g_ref[at // GROUP : at // GROUP + 1, :].astype(jnp.float32)
            c_ref[row : row + part, at : at + GROUP] = clip_tile(v).astype(jnp.bfloat16)
        sums = jnp.sum(total, axis=-1, keepdims=True)
        sums = jnp.transpose(jnp.broadcast_to(sums, (part, 128)))[:EXTRA]
        row = lax.broadcasted_iota(jnp.int32, sums.shape, 0)
        left = sums
        for place in range(3):
            piece = left.astype(jnp.bfloat16).astype(jnp.float32)
            left = left - piece
            sums = jnp.where(row == place, piece, sums)
        c_ref[rows:, i * part : (i + 1) * part] = sums.astype(jnp.bfloat16)


def pre(hidden, gain):
    rows, width = hidden.shape
    steps = 4
    return pl.pallas_call(
        pre_kernel,
        in_specs=[IN_HBM] * 2,
        out_specs=IN_VMEM,
        out_shape=pltpu.VMEM((rows + EXTRA, width), jnp.bfloat16),
        scratch_shapes=[
            pltpu.VMEM((rows, width), jnp.bfloat16),
            pltpu.VMEM(gain.shape, jnp.bfloat16),
            pltpu.SemaphoreType.DMA((steps + 1,)),
        ],
        compiler_params=params(62),
        cost_estimate=cost(8 * rows * width, 4 * rows * width),
        name="pre",
    )(hidden, gain)


def load_kernel(count, *refs):
    sources, goals, sem = refs[:count], refs[count : 2 * count], refs[-1]
    copies = []
    for i in range(count):
        depth = sources[i].shape[0] // LOAD_PARTS
        for p in range(LOAD_PARTS):
            at = slice(p * depth, (p + 1) * depth)
            copies.append(
                pltpu.make_async_copy(sources[i].at[at], goals[i].at[at], sem.at[i, p])
            )
    for copy in copies:
        copy.start()
    for copy in copies:
        copy.wait()


def load(*weights):
    count = len(weights)
    return pl.pallas_call(
        functools.partial(load_kernel, count),
        in_specs=[IN_HBM] * count,
        out_specs=[IN_VMEM] * count,
        out_shape=[pltpu.VMEM(w.shape, w.dtype) for w in weights],
        scratch_shapes=[pltpu.SemaphoreType.DMA((count, LOAD_PARTS))],
        compiler_params=params(LOAD_MIB),
        cost_estimate=cost(0, 2 * sum(w.size * 2 for w in weights)),
        name="load",
    )(*weights)


def proj_kernel(counts, masks, begins, ends, order_ref, *refs):
    depth = len(counts)
    blocks, refs = refs[: sum(counts)], refs[sum(counts) :]
    wq_ref, wk_ref, wv_ref, *refs = refs
    if not begins:
        *before, ss_in = refs[:4]
        refs = refs[4:]
        squares = ss_in[0:1, :]
    else:
        before = [None] * 3
        squares = jnp.zeros((1, ss_rows(blocks)), jnp.float32)
    if ends:
        q_ref, *kv_refs = refs[: 1 + HALVES]
        accs = refs[1 + HALVES :]
    else:
        *accs, ss_ref = refs
    nk = wk_ref.shape[1]
    k_rows = blocks[0].shape[1]
    at_block = 0
    for k in range(depth):
        at = pl.ds(pl.multiple_of(order_ref[masks[k]] * k_rows, k_rows), k_rows)
        mine = [b[...] for b in blocks[at_block : at_block + counts[k]]]
        at_block += counts[k]
        body_rows = mine[-1].shape[0] - EXTRA
        tail = mine[-1][body_rows:, : squares.shape[1]].astype(jnp.float32)
        squares = squares + (tail[0:1] + tail[1:2] + tail[2:3])
        mine[-1] = mine[-1][:body_rows]
        left = mine[0] if len(mine) == 1 else jnp.concatenate(mine, axis=0)
        wq, wk, wv = wq_ref[at, :], wk_ref[at, :], wv_ref[at, :]
        if nk % 128 == 0:
            both = jnp.dot(
                left, jnp.concatenate([wk, wv], axis=1), preferred_element_type=jnp.float32
            )
            parts = (both[:, :nk], both[:, nk:])
        else:
            parts = [jnp.dot(left, w, preferred_element_type=jnp.float32) for w in (wk, wv)]
        first = jnp.dot(left, wq, preferred_element_type=jnp.float32)
        for part, acc, old in zip((first, *parts), accs, before):
            if k:
                acc[...] += part
            elif not begins:
                acc[...] = old[...] + part
            else:
                acc[...] = part

    if not ends:
        ss_ref[...] = jnp.broadcast_to(squares, ss_ref.shape)
    else:
        accq, acck, accv = accs
        features = wq_ref.shape[0]
        squares = jnp.broadcast_to(squares, (8, squares.shape[1]))
        inverse = lax.rsqrt(squares * (1.0 / features) + EPS_IN)
        scale = jnp.transpose(inverse)[:, :1]
        q_ref[...] = (accq[...] * scale).astype(jnp.bfloat16)
        rows = kv_refs[0].shape[0]
        for i, kv_ref in enumerate(kv_refs):
            at = slice(i * rows, (i + 1) * rows)
            kv_ref[:, :nk] = (acck[at, :] * scale[at]).astype(jnp.bfloat16)
            kv_ref[:, nk:] = (accv[at, :] * scale[at]).astype(jnp.bfloat16)


def ss_rows(blocks):
    return blocks[0].shape[0] - EXTRA


def proj(order, blocks, rows, state, ends, wq, wk, wv):
    masks = sorted(blocks)
    blocks = [blocks[m] for m in masks]
    depth = len(blocks)
    counts = [len(b) for b in blocks]
    part_cols = blocks[0][0].shape[1]
    sizes = wq.shape[1], wk.shape[1], wv.shape[1]
    n = sum(sizes)
    flat = [p for b in blocks for p in b]
    args = [order, *flat, wq, wk, wv, *state]
    if ends:
        out_shape = [
            jax.ShapeDtypeStruct((rows, sizes[0]), jnp.bfloat16),
        ] + [
            jax.ShapeDtypeStruct((rows // HALVES, sizes[1] + sizes[2]), jnp.bfloat16)
            for _ in range(HALVES)
        ]
        scratch = [pltpu.VMEM((rows, m), jnp.float32) for m in sizes]
    else:
        out_shape = [pltpu.VMEM((rows, m), jnp.float32) for m in sizes]
        out_shape.append(jax.ShapeDtypeStruct((8, rows), jnp.float32))
        scratch = []
    return pl.pallas_call(
        functools.partial(proj_kernel, counts, masks, not state, ends),
        in_specs=[IN_SMEM] + [IN_VMEM] * (len(args) - 1),
        out_specs=[IN_VMEM] * len(out_shape),
        out_shape=out_shape,
        scratch_shapes=scratch,
        compiler_params=params(PROJ_MIB),
        cost_estimate=cost(
            2 * rows * part_cols * depth * n, 2 * part_cols * depth * (rows + n)
        ),
        name="proj",
    )(*args)


def att_kernel(first, kv_heads, near, far, begins, ends, me_ref, q_ref, *refs):
    count = near + len(far)
    kvs, refs = refs[:count], refs[count:]
    if not begins:
        high_in, total_in, accum_in, *refs = refs
    if ends:
        sign_ref, o_ref, high, total, accum = refs
    else:
        high, total, accum = refs
    rows = accum.shape[2]
    heads = q_ref.shape[1] // HD
    part = kvs[0].shape[0]
    group = heads // kv_heads
    scale = HD ** (-0.5) * LOG2E

    if not begins:
        high[...] = high_in[...]
        total[...] = total_in[...]
        accum[...] = accum_in[...]

    def visit(kv_ref, sub, start, fresh):
        keys = slice(sub * part, (sub + 1) * part)
        masked = start is not None and start + part > first
        scores, turned = [], []
        for kv in range(kv_heads):
            at = (kv_heads + kv) * HD
            turned.append(jnp.transpose(kv_ref[keys, at : at + HD]))
        for head in range(heads):
            kv = head // group
            q = q_ref[first : first + rows, head * HD : (head + 1) * HD]
            k = kv_ref[keys, kv * HD : (kv + 1) * HD]
            s = lax.dot_general(
                k, q, (((1,), (1,)), ((), ())), preferred_element_type=jnp.float32
            )
            if masked:
                kpos = start + lax.broadcasted_iota(jnp.int32, s.shape, 0)
                qpos = first + lax.broadcasted_iota(jnp.int32, s.shape, 1)
                s = jnp.where(kpos <= qpos, s, FAR_BELOW)
            scores.append(s)
        for head in range(heads):
            s = scores[head]
            best = jnp.max(s, axis=0, keepdims=True)
            if not fresh:
                before = high[head : head + 1]
                best = jnp.maximum(best, before)
            w = jnp.exp2((s - best) * scale)
            sums = jnp.sum(w, axis=0, keepdims=True)
            mixed = jnp.dot(
                turned[head // group], w.astype(jnp.bfloat16), preferred_element_type=jnp.float32
            )
            if fresh:
                total[head : head + 1] = sums
                accum[head] = mixed
            else:
                decay = jnp.exp2((before - best) * scale)
                total[head : head + 1] = total[head : head + 1] * decay + sums
                accum[head] = accum[head] * decay + mixed
            high[head : head + 1] = best

    for at in range(near):
        visit(kvs[at], 0, at * part, begins and at == 0)
    for at, hop in enumerate(far):

        @pl.when(me_ref[0] >= hop)
        def _():
            visit(kvs[near + at], 0, None, False)

    if ends:
        for head in range(heads):
            att = jnp.transpose(accum[head] / total[head : head + 1])
            att = att.astype(jnp.bfloat16).astype(jnp.float32)
            o_ref[:, head * HD : (head + 1) * HD] = (att * sign_ref[head : head + 1, :]).astype(
                jnp.bfloat16
            )


def attend(me, q, first, rows, kv_heads, near, far, state, signs):
    heads = q.shape[1] // HD
    kvs = near + [kv for _, kv in far]
    keys = sum(kv.shape[0] for kv in kvs)
    shapes = [(max(heads, 8), rows), (max(heads, 8), rows), (heads, HD, rows)]
    args = [me, q, *kvs]
    if state is not None:
        args += list(state)
    if signs is None:
        out_shape = [jax.ShapeDtypeStruct(shape, jnp.float32) for shape in shapes]
        scratch = []
    else:
        args.append(signs)
        out_shape = jax.ShapeDtypeStruct((rows, heads * HD), jnp.bfloat16)
        scratch = [pltpu.VMEM(shape, jnp.float32) for shape in shapes]
    far_at = [n for n, _ in far]
    kernel = functools.partial(
        att_kernel, first, kv_heads, len(near), far_at, state is None, signs is not None
    )
    return pl.pallas_call(
        kernel,
        in_specs=[IN_SMEM] + [IN_VMEM] * (len(args) - 1),
        out_specs=IN_VMEM if signs is not None else [IN_VMEM] * 3,
        out_shape=out_shape,
        scratch_shapes=scratch,
        compiler_params=params(ATT_MIB),
        cost_estimate=cost(4 * rows * keys * heads * HD, 4 * keys * HD, rows * keys * heads),
        name="attend",
    )(*args)


def butterfly(tiles):
    count = len(tiles)
    span = 1
    while span < count:
        out = list(tiles)
        for at in range(count):
            if not at & span:
                a, b = tiles[at], tiles[at | span]
                out[at], out[at | span] = a + b, a - b
        tiles = out
        span *= 2
    return tiles


def out_kernel(counts, steps, chunk, sign_ref, t_ref, *refs):
    parts = len(counts)
    blocks, at_block = [], 0
    for n in counts:
        blocks.append(refs[at_block : at_block + n])
        at_block += n
    w_ref, b_ref, s_ref, mid, rot, acc = refs[at_block:]
    rows = b_ref.shape[0]
    width = blocks[0][0].shape[1]
    here = width // HD
    heads = here * parts
    factor = heads ** (-0.5)

    strip = 16
    most = max(counts)
    span = rows // most
    for section in range(most):

        def turn(i, carry):
            at = pl.multiple_of(section * span + i * strip, strip)
            for m in range(parts):
                if len(blocks[m]) == 1:
                    ref, start = blocks[m][0], at
                else:
                    ref, start = blocks[m][section], pl.multiple_of(i * strip, strip)
                tiles = [
                    ref[pl.ds(start, strip), h * HD : (h + 1) * HD].astype(jnp.float32)
                    for h in range(here)
                ]
                for h, v in enumerate(butterfly(tiles)):
                    mid[m * here + h] = v
            for h in range(here):
                tiles = butterfly([mid[m * here + h] for m in range(parts)])
                for m in range(parts):
                    v = tiles[m] * (factor * sign_ref[m])
                    col = (m * here + h) * HD
                    rot[pl.ds(at, strip), col : col + HD] = clip_tile(v).astype(jnp.bfloat16)
            return carry

        lax.fori_loop(0, span // strip, turn, 0)

    depth = w_ref.shape[0] // steps
    for i in range(steps):
        part = jnp.dot(
            rot[:, i * depth : (i + 1) * depth],
            w_ref[i * depth : (i + 1) * depth, :],
            preferred_element_type=jnp.float32,
        )
        if i == 0:
            acc[...] = part
        else:
            acc[...] += part

    b = acc[...]
    t = t_ref[chunk * rows : (chunk + 1) * rows, :].astype(jnp.float32)
    b_ref[...] = b
    sums = [jnp.sum(v, axis=-1, keepdims=True) for v in (b * b, b * t, t * t)]
    lane = lax.broadcasted_iota(jnp.int32, (rows, 128), 1)
    wide = jnp.where(lane == 0, sums[0], jnp.where(lane == 1, sums[1], sums[2]))
    s_ref[...] = jnp.transpose(wide)[:8]


def project_out(flips, blocks, w_out, teacher, chunk):
    parts = len(blocks)
    counts = [len(b) for b in blocks]
    rows, width = blocks[0][0].shape
    depth, cols = w_out.shape
    steps = 4
    flat = [p for b in blocks for p in b]
    return pl.pallas_call(
        functools.partial(out_kernel, counts, steps, chunk),
        in_specs=[IN_SMEM] + [IN_VMEM] * (len(flat) + 2),
        out_specs=[IN_VMEM, IN_VMEM],
        out_shape=[
            jax.ShapeDtypeStruct((rows, cols), jnp.float32),
            jax.ShapeDtypeStruct((8, rows), jnp.float32),
        ],
        scratch_shapes=[
            pltpu.VMEM((parts * width // HD, 16, HD), jnp.float32),
            pltpu.VMEM((rows, depth), jnp.bfloat16),
            pltpu.VMEM((rows, cols), jnp.float32),
        ],
        compiler_params=params(OUT_MIB),
        cost_estimate=cost(2 * rows * depth * cols, 2 * depth * (rows + cols) + 6 * rows * cols),
        name="project_out",
    )(flips, teacher, *flat, w_out)


def final_kernel(features, chunks, parts, *refs):
    branches, stats = refs[:chunks], refs[chunks : chunks + parts]
    student_ref, loss_ref = refs[chunks + parts :]
    sums = [stat[...] for stat in stats]
    while len(sums) > 1:
        sums = [x + y for x, y in zip(sums[::2], sums[1::2])]
    total = sums[0]
    inverse = lax.rsqrt(total[0:1] * (1.0 / features) + EPS_OUT)
    loss = inverse * inverse * total[0:1] - 2.0 * inverse * total[1:2] + total[2:3]
    loss_ref[...] = jnp.maximum(loss, 0.0) * (1.0 / features)
    column = jnp.transpose(jnp.broadcast_to(inverse, total.shape))[:, :1]
    rows = branches[0].shape[0]
    for at in range(chunks):
        scale = column[at * rows : (at + 1) * rows]
        student_ref[at * rows : (at + 1) * rows, :] = (branches[at][...] * scale).astype(
            jnp.bfloat16
        )


def final(features, branches, stats):
    chunks, parts = len(branches), len(stats)
    part_rows, cols = branches[0].shape
    rows = part_rows * chunks
    return pl.pallas_call(
        functools.partial(final_kernel, features, chunks, parts),
        grid=(1,),
        in_specs=[whole((part_rows, cols))] * chunks + [whole((8, rows))] * parts,
        out_specs=[whole((rows, cols)), whole((1, rows))],
        out_shape=[
            jax.ShapeDtypeStruct((rows, cols), jnp.bfloat16),
            jax.ShapeDtypeStruct((1, rows), jnp.float32),
        ],
        compiler_params=params(16),
        cost_estimate=cost(2 * rows * cols, 6 * rows * cols),
        name="final",
    )(*branches, *stats)


def swap(x, mask):
    count = lax.axis_size("tp")
    return lax.ppermute(x, "tp", [(i, i ^ mask) for i in range(count)])


def send_up(x, first):
    count = lax.axis_size("ctx")
    return lax.ppermute(x, "ctx", [(i, i + 1) for i in range(first, count - 1)])


def after(x, *others):
    return lax.optimization_barrier((x,) + others)[0]


def gather(own, core_after=None, beside=None, middle=None):
    count = lax.axis_size("tp")
    got = {0: [own]}
    masks = [1 << b for b in range(1, count.bit_length() - 1)]
    if len(masks) >= 2:
        a, b = masks[0], masks[1]
        half = own.shape[0] // (2 * EXTRA) * EXTRA
        via_a, via_b = swap(own, a), swap(own, b)
        got[1] = [swap(own, 1)]
        if beside is not None:
            token = beside(got[1][0])
            via_a, via_b = after(via_a, token), after(via_b, token)
        got[a], got[b] = [via_a], [via_b]
        diagonal = [swap(via_a[:half], b), swap(via_b[half:], a)]
        if core_after is not None:
            diagonal = [after(p, core_after) for p in diagonal]
            via_a, via_b = after(via_a, core_after), after(via_b, core_after)
        got[a | 1], got[b | 1] = [swap(via_a, 1)], [swap(via_b, 1)]
        got[a | b] = diagonal
        if middle is not None:
            token = middle(got)
            diagonal = [after(p, token) for p in diagonal]
        got[a | b | 1] = [swap(p, 1) for p in diagonal]
        masks = masks[2:]
    elif count > 1:
        got[1] = [swap(own, 1)]
    for mask in masks:
        for m in list(got):
            got[m | mask] = [swap(p, mask) for p in got[m]]
    return [got[m] for m in range(count)]


def body(hidden_in, norm_gain, w_query, w_key, w_value, sign_bits, w_out, teacher):
    rows = hidden_in.shape[0]
    half = rows // HALVES
    tp_count = lax.axis_size("tp")
    ctx_count = lax.axis_size("ctx")
    features = hidden_in.shape[1] * tp_count
    tp_at = lax.axis_index("tp")
    ctx_at = jnp.reshape(lax.axis_index("ctx"), (1,)).astype(jnp.int32)
    masks = jnp.arange(tp_count, dtype=jnp.int32)
    order = tp_at ^ masks
    shared = tp_at & masks
    parity = jnp.zeros_like(shared)
    for bit in range(tp_count.bit_length()):
        parity = parity ^ (shared >> bit & 1)
    flips = (1 - 2 * parity).astype(jnp.float32)
    signs = (2 * sign_bits - 1).astype(jnp.float32)
    gain = norm_gain.reshape(-1, GROUP)

    gain, order, ctx_at, flips, signs = lax.optimization_barrier(
        (gain, order, ctx_at, flips, signs)
    )
    clipped = pre(hidden_in, gain)

    kv_cols = w_key.shape[1]
    sharing = HD // kv_cols if kv_cols < HD else 1
    kv_heads = kv_cols * sharing // HD
    loaded = []

    def bring(token):
        first = after(w_query, token, order, ctx_at, flips, signs)
        loaded.extend(load(first, w_key, w_value, w_out))
        return loaded[1]

    early, state = [], []

    def begin(got):
        early.extend(sorted(got)[:-1])
        part = {m: got[m] for m in early}
        state.extend(proj(order, part, rows, (), False, *loaded[:3]))
        return state[-1]

    blocks = gather(clipped, beside=bring, middle=begin)
    if not loaded:
        bring(clipped)
    late = {m: block for m, block in enumerate(blocks) if m not in early}
    q, *kvs = proj(order, late, rows, state, True, *loaded[:3])
    for i, kv in enumerate(kvs):
        if sharing > 1:
            k, v = kv[:, :kv_cols], kv[:, kv_cols:]
            for bit in range(sharing.bit_length() - 1):
                upper = tp_at >> bit & 1 == 1
                k2, v2 = swap(k, 1 << bit), swap(v, 1 << bit)
                k, v = (
                    jnp.where(
                        upper,
                        jnp.concatenate([far, near], axis=1),
                        jnp.concatenate([near, far], axis=1),
                    )
                    for near, far in ((k, k2), (v, v2))
                )
            kv = jnp.concatenate([k, v], axis=1)
        kvs[i] = kv
    far, sent = [], kvs
    for hop in range(1, ctx_count):
        sent = [send_up(kv, hop - 1) for kv in sent]
        far += [(hop, kv) for kv in sent]

    states = [
        attend(ctx_at, q, at * half, half, kv_heads, kvs[: at + 1], far[:-HALVES], None, None)
        for at in range(HALVES)
    ]
    branches, stats = [], []
    for at in range(HALVES):
        signed = attend(
            ctx_at, q, at * half, half, kv_heads, [], far[-HALVES:], states[at], signs
        )
        if at:
            signed = after(signed, *[b[0] for b in blocks[2:6:2]])
        blocks = gather(signed, branches[-1] if at else None)
        b, s = project_out(flips, blocks, loaded[3], teacher, at)
        branches.append(b)
        stats.append(s)
    stat = jnp.concatenate(stats, axis=1)
    if tp_count > 1:
        stat = stat + swap(stat, 1)
    totals = [stat] + [swap(stat, m) for m in range(2, tp_count, 2)]
    student, loss = final(features, branches, totals)
    return student, loss.reshape(rows)


def solution(mesh):
    in_specs = (
        P("ctx", "tp"),
        P("tp"),
        P(None, "tp"),
        P(None, "tp"),
        P(None, "tp"),
        P("tp", None),
        P(None, "tp"),
        P("ctx", "tp"),
    )
    out_specs = (P("ctx", "tp"), P("ctx"))
    return jax.shard_map(body, mesh=mesh, in_specs=in_specs, out_specs=out_specs, check_vma=False)
```

```python
import functools
import math

import jax
import jax.numpy as jnp
from jax import lax
from jax.experimental import pallas as pl
from jax.experimental.pallas import tpu as pltpu
from jax.sharding import PartitionSpec as P

HD = 128
GROUP = 128
EPS_IN = 1e-05
EPS_OUT = 1e-06
CLIP_RATIO = 0.9
FAR_BELOW = -1e30
LOG2E = math.log2(math.e)
HALVES = 2
EXTRA = 16
LOAD_PARTS = 4
LOAD_MIB = 38
PROJ_MIB = 14
ATT_MIB = 12
OUT_MIB = 12
MIB = 1024 * 1024


def params(mib, **kw):
    return pltpu.CompilerParams(vmem_limit_bytes=mib * MIB, **kw)


def whole(shape):
    zeros = (0,) * len(shape)
    return pl.BlockSpec(shape, lambda *_: zeros)


IN_SMEM = pl.BlockSpec(memory_space=pltpu.SMEM)
IN_VMEM = pl.BlockSpec(memory_space=pltpu.VMEM)
ANYWHERE = pl.BlockSpec(memory_space=pl.ANY)
IN_HBM = pl.BlockSpec(memory_space=pltpu.HBM)


def cost(flops, moved, trans=0):
    return pl.CostEstimate(flops=int(flops), bytes_accessed=int(moved), transcendentals=int(trans))


def clip_tile(v):
    limit = CLIP_RATIO * jnp.max(jnp.abs(v), axis=-1, keepdims=True)
    return jnp.clip(v, -limit, limit)


def pre_kernel(h_hbm, g_hbm, *refs):
    c_ref, h_all, g_ref, sem = refs
    rows, width = h_all.shape
    steps = sem.shape[0] - 1
    part = rows // steps
    copies = [pltpu.make_async_copy(g_hbm, g_ref, sem.at[steps])]
    for i in range(steps):
        at = slice(i * part, (i + 1) * part)
        copies.append(pltpu.make_async_copy(h_hbm.at[at], h_all.at[at], sem.at[i]))
    for copy in copies:
        copy.start()
    copies[0].wait()
    for i in range(steps):
        copies[i + 1].wait()
        total = jnp.zeros((part, GROUP), jnp.float32)
        row = i * part
        for at in range(0, width, GROUP):
            h = h_all[i * part : (i + 1) * part, at : at + GROUP].astype(jnp.float32)
            total = total + h * h
            v = h * g_ref[at // GROUP : at // GROUP + 1, :].astype(jnp.float32)
            c_ref[row : row + part, at : at + GROUP] = clip_tile(v).astype(jnp.bfloat16)
        sums = jnp.sum(total, axis=-1, keepdims=True)
        sums = jnp.transpose(jnp.broadcast_to(sums, (part, 128)))[:EXTRA]
        row = lax.broadcasted_iota(jnp.int32, sums.shape, 0)
        left = sums
        for place in range(3):
            piece = left.astype(jnp.bfloat16).astype(jnp.float32)
            left = left - piece
            sums = jnp.where(row == place, piece, sums)
        c_ref[rows:, i * part : (i + 1) * part] = sums.astype(jnp.bfloat16)


def pre(hidden, gain):
    rows, width = hidden.shape
    steps = 4
    return pl.pallas_call(
        pre_kernel,
        in_specs=[IN_HBM] * 2,
        out_specs=IN_VMEM,
        out_shape=pltpu.VMEM((rows + EXTRA, width), jnp.bfloat16),
        scratch_shapes=[
            pltpu.VMEM((rows, width), jnp.bfloat16),
            pltpu.VMEM(gain.shape, jnp.bfloat16),
            pltpu.SemaphoreType.DMA((steps + 1,)),
        ],
        compiler_params=params(62),
        cost_estimate=cost(8 * rows * width, 4 * rows * width),
        name="pre",
    )(hidden, gain)


def load_kernel(count, *refs):
    sources, goals, sem = refs[:count], refs[count : 2 * count], refs[-1]
    copies = []
    for i in range(count):
        depth = sources[i].shape[0] // LOAD_PARTS
        for p in range(LOAD_PARTS):
            at = slice(p * depth, (p + 1) * depth)
            copies.append(
                pltpu.make_async_copy(sources[i].at[at], goals[i].at[at], sem.at[i, p])
            )
    for copy in copies:
        copy.start()
    for copy in copies:
        copy.wait()


def load(*weights):
    count = len(weights)
    return pl.pallas_call(
        functools.partial(load_kernel, count),
        in_specs=[IN_HBM] * count,
        out_specs=[IN_VMEM] * count,
        out_shape=[pltpu.VMEM(w.shape, w.dtype) for w in weights],
        scratch_shapes=[pltpu.SemaphoreType.DMA((count, LOAD_PARTS))],
        compiler_params=params(LOAD_MIB),
        cost_estimate=cost(0, 2 * sum(w.size * 2 for w in weights)),
        name="load",
    )(*weights)


def proj_kernel(counts, masks, begins, ends, order_ref, *refs):
    depth = len(counts)
    blocks, refs = refs[: sum(counts)], refs[sum(counts) :]
    wq_ref, wk_ref, wv_ref, *refs = refs
    if not begins:
        *before, ss_in = refs[:4]
        refs = refs[4:]
        squares = ss_in[0:1, :]
    else:
        before = [None] * 3
        squares = jnp.zeros((1, ss_rows(blocks)), jnp.float32)
    if ends:
        q_ref, *kv_refs = refs[: 1 + HALVES]
        accs = refs[1 + HALVES :]
    else:
        *accs, ss_ref = refs
    nk = wk_ref.shape[1]
    k_rows = blocks[0].shape[1]
    at_block = 0
    for k in range(depth):
        at = pl.ds(pl.multiple_of(order_ref[masks[k]] * k_rows, k_rows), k_rows)
        mine = [b[...] for b in blocks[at_block : at_block + counts[k]]]
        at_block += counts[k]
        body_rows = mine[-1].shape[0] - EXTRA
        tail = mine[-1][body_rows:, : squares.shape[1]].astype(jnp.float32)
        squares = squares + (tail[0:1] + tail[1:2] + tail[2:3])
        mine[-1] = mine[-1][:body_rows]
        left = mine[0] if len(mine) == 1 else jnp.concatenate(mine, axis=0)
        wq, wk, wv = wq_ref[at, :], wk_ref[at, :], wv_ref[at, :]
        if nk % 128 == 0:
            both = jnp.dot(
                left, jnp.concatenate([wk, wv], axis=1), preferred_element_type=jnp.float32
            )
            parts = (both[:, :nk], both[:, nk:])
        else:
            parts = [jnp.dot(left, w, preferred_element_type=jnp.float32) for w in (wk, wv)]
        first = jnp.dot(left, wq, preferred_element_type=jnp.float32)
        for part, acc, old in zip((first, *parts), accs, before):
            if k:
                acc[...] += part
            elif not begins:
                acc[...] = old[...] + part
            else:
                acc[...] = part

    if not ends:
        ss_ref[...] = jnp.broadcast_to(squares, ss_ref.shape)
    else:
        accq, acck, accv = accs
        features = wq_ref.shape[0]
        squares = jnp.broadcast_to(squares, (8, squares.shape[1]))
        inverse = lax.rsqrt(squares * (1.0 / features) + EPS_IN)
        scale = jnp.transpose(inverse)[:, :1]
        q_ref[...] = (accq[...] * scale).astype(jnp.bfloat16)
        rows = kv_refs[0].shape[0]
        for i, kv_ref in enumerate(kv_refs):
            at = slice(i * rows, (i + 1) * rows)
            kv_ref[:, :nk] = (acck[at, :] * scale[at]).astype(jnp.bfloat16)
            kv_ref[:, nk:] = (accv[at, :] * scale[at]).astype(jnp.bfloat16)


def ss_rows(blocks):
    return blocks[0].shape[0] - EXTRA


def proj(order, blocks, rows, state, ends, wq, wk, wv):
    masks = sorted(blocks)
    blocks = [blocks[m] for m in masks]
    depth = len(blocks)
    counts = [len(b) for b in blocks]
    part_cols = blocks[0][0].shape[1]
    sizes = wq.shape[1], wk.shape[1], wv.shape[1]
    n = sum(sizes)
    flat = [p for b in blocks for p in b]
    args = [order, *flat, wq, wk, wv, *state]
    if ends:
        out_shape = [
            jax.ShapeDtypeStruct((rows, sizes[0]), jnp.bfloat16),
        ] + [
            jax.ShapeDtypeStruct((rows // HALVES, sizes[1] + sizes[2]), jnp.bfloat16)
            for _ in range(HALVES)
        ]
        scratch = [pltpu.VMEM((rows, m), jnp.float32) for m in sizes]
    else:
        out_shape = [pltpu.VMEM((rows, m), jnp.float32) for m in sizes]
        out_shape.append(jax.ShapeDtypeStruct((8, rows), jnp.float32))
        scratch = []
    return pl.pallas_call(
        functools.partial(proj_kernel, counts, masks, not state, ends),
        in_specs=[IN_SMEM] + [IN_VMEM] * (len(args) - 1),
        out_specs=[IN_VMEM] * len(out_shape),
        out_shape=out_shape,
        scratch_shapes=scratch,
        compiler_params=params(PROJ_MIB),
        cost_estimate=cost(
            2 * rows * part_cols * depth * n, 2 * part_cols * depth * (rows + n)
        ),
        name="proj",
    )(*args)


def att_kernel(first, kv_heads, near, far, begins, ends, me_ref, q_ref, *refs):
    count = near + len(far)
    kvs, refs = refs[:count], refs[count:]
    if not begins:
        high_in, total_in, accum_in, *refs = refs
    if ends:
        sign_ref, o_ref, high, total, accum = refs
    else:
        high, total, accum = refs
    rows = accum.shape[2]
    heads = q_ref.shape[1] // HD
    part = kvs[0].shape[0]
    group = heads // kv_heads
    scale = HD ** (-0.5) * LOG2E

    if not begins:
        high[...] = high_in[...]
        total[...] = total_in[...]
        accum[...] = accum_in[...]

    def visit(kv_ref, sub, start, fresh):
        keys = slice(sub * part, (sub + 1) * part)
        masked = start is not None and start + part > first
        scores, turned = [], []
        for kv in range(kv_heads):
            at = (kv_heads + kv) * HD
            turned.append(jnp.transpose(kv_ref[keys, at : at + HD]))
        for head in range(heads):
            kv = head // group
            q = q_ref[first : first + rows, head * HD : (head + 1) * HD]
            k = kv_ref[keys, kv * HD : (kv + 1) * HD]
            s = lax.dot_general(
                k, q, (((1,), (1,)), ((), ())), preferred_element_type=jnp.float32
            )
            if masked:
                kpos = start + lax.broadcasted_iota(jnp.int32, s.shape, 0)
                qpos = first + lax.broadcasted_iota(jnp.int32, s.shape, 1)
                s = jnp.where(kpos <= qpos, s, FAR_BELOW)
            scores.append(s)
        for head in range(heads):
            s = scores[head]
            best = jnp.max(s, axis=0, keepdims=True)
            if not fresh:
                before = high[head : head + 1]
                best = jnp.maximum(best, before)
            w = jnp.exp2((s - best) * scale)
            sums = jnp.sum(w, axis=0, keepdims=True)
            mixed = jnp.dot(
                turned[head // group], w.astype(jnp.bfloat16), preferred_element_type=jnp.float32
            )
            if fresh:
                total[head : head + 1] = sums
                accum[head] = mixed
            else:
                decay = jnp.exp2((before - best) * scale)
                total[head : head + 1] = total[head : head + 1] * decay + sums
                accum[head] = accum[head] * decay + mixed
            high[head : head + 1] = best

    for at in range(near):
        visit(kvs[at], 0, at * part, begins and at == 0)
    for at, hop in enumerate(far):

        @pl.when(me_ref[0] >= hop)
        def _():
            visit(kvs[near + at], 0, None, False)

    if ends:
        for head in range(heads):
            att = jnp.transpose(accum[head] / total[head : head + 1])
            att = att.astype(jnp.bfloat16).astype(jnp.float32)
            o_ref[:, head * HD : (head + 1) * HD] = (att * sign_ref[head : head + 1, :]).astype(
                jnp.bfloat16
            )


def attend(me, q, first, rows, kv_heads, near, far, state, signs):
    heads = q.shape[1] // HD
    kvs = near + [kv for _, kv in far]
    keys = sum(kv.shape[0] for kv in kvs)
    shapes = [(max(heads, 8), rows), (max(heads, 8), rows), (heads, HD, rows)]
    args = [me, q, *kvs]
    if state is not None:
        args += list(state)
    if signs is None:
        out_shape = [jax.ShapeDtypeStruct(shape, jnp.float32) for shape in shapes]
        scratch = []
    else:
        args.append(signs)
        out_shape = jax.ShapeDtypeStruct((rows, heads * HD), jnp.bfloat16)
        scratch = [pltpu.VMEM(shape, jnp.float32) for shape in shapes]
    far_at = [n for n, _ in far]
    kernel = functools.partial(
        att_kernel, first, kv_heads, len(near), far_at, state is None, signs is not None
    )
    return pl.pallas_call(
        kernel,
        in_specs=[IN_SMEM] + [IN_VMEM] * (len(args) - 1),
        out_specs=IN_VMEM if signs is not None else [IN_VMEM] * 3,
        out_shape=out_shape,
        scratch_shapes=scratch,
        compiler_params=params(ATT_MIB),
        cost_estimate=cost(4 * rows * keys * heads * HD, 4 * keys * HD, rows * keys * heads),
        name="attend",
    )(*args)


def butterfly(tiles):
    count = len(tiles)
    span = 1
    while span < count:
        out = list(tiles)
        for at in range(count):
            if not at & span:
                a, b = tiles[at], tiles[at | span]
                out[at], out[at | span] = a + b, a - b
        tiles = out
        span *= 2
    return tiles


def out_kernel(counts, steps, chunk, sign_ref, t_ref, *refs):
    parts = len(counts)
    blocks, at_block = [], 0
    for n in counts:
        blocks.append(refs[at_block : at_block + n])
        at_block += n
    w_ref, b_ref, s_ref, mid, rot, acc = refs[at_block:]
    rows = b_ref.shape[0]
    width = blocks[0][0].shape[1]
    here = width // HD
    heads = here * parts
    factor = heads ** (-0.5)

    strip = 16
    most = max(counts)
    span = rows // most
    for section in range(most):

        def turn(i, carry):
            at = pl.multiple_of(section * span + i * strip, strip)
            for m in range(parts):
                if len(blocks[m]) == 1:
                    ref, start = blocks[m][0], at
                else:
                    ref, start = blocks[m][section], pl.multiple_of(i * strip, strip)
                tiles = [
                    ref[pl.ds(start, strip), h * HD : (h + 1) * HD].astype(jnp.float32)
                    for h in range(here)
                ]
                for h, v in enumerate(butterfly(tiles)):
                    mid[m * here + h] = v
            for h in range(here):
                tiles = butterfly([mid[m * here + h] for m in range(parts)])
                for m in range(parts):
                    v = tiles[m] * (factor * sign_ref[m])
                    col = (m * here + h) * HD
                    rot[pl.ds(at, strip), col : col + HD] = clip_tile(v).astype(jnp.bfloat16)
            return carry

        lax.fori_loop(0, span // strip, turn, 0)

    depth = w_ref.shape[0] // steps
    for i in range(steps):
        part = jnp.dot(
            rot[:, i * depth : (i + 1) * depth],
            w_ref[i * depth : (i + 1) * depth, :],
            preferred_element_type=jnp.float32,
        )
        if i == 0:
            acc[...] = part
        else:
            acc[...] += part

    b = acc[...]
    t = t_ref[chunk * rows : (chunk + 1) * rows, :].astype(jnp.float32)
    b_ref[...] = b
    sums = [jnp.sum(v, axis=-1, keepdims=True) for v in (b * b, b * t, t * t)]
    lane = lax.broadcasted_iota(jnp.int32, (rows, 128), 1)
    wide = jnp.where(lane == 0, sums[0], jnp.where(lane == 1, sums[1], sums[2]))
    s_ref[...] = jnp.transpose(wide)[:8]


def project_out(flips, blocks, w_out, teacher, chunk):
    parts = len(blocks)
    counts = [len(b) for b in blocks]
    rows, width = blocks[0][0].shape
    depth, cols = w_out.shape
    steps = 4
    flat = [p for b in blocks for p in b]
    return pl.pallas_call(
        functools.partial(out_kernel, counts, steps, chunk),
        in_specs=[IN_SMEM] + [IN_VMEM] * (len(flat) + 2),
        out_specs=[IN_VMEM, IN_VMEM],
        out_shape=[
            jax.ShapeDtypeStruct((rows, cols), jnp.float32),
            jax.ShapeDtypeStruct((8, rows), jnp.float32),
        ],
        scratch_shapes=[
            pltpu.VMEM((parts * width // HD, 16, HD), jnp.float32),
            pltpu.VMEM((rows, depth), jnp.bfloat16),
            pltpu.VMEM((rows, cols), jnp.float32),
        ],
        compiler_params=params(OUT_MIB),
        cost_estimate=cost(2 * rows * depth * cols, 2 * depth * (rows + cols) + 6 * rows * cols),
        name="project_out",
    )(flips, teacher, *flat, w_out)


def final_kernel(features, chunks, parts, *refs):
    branches, stats = refs[:chunks], refs[chunks : chunks + parts]
    student_ref, loss_ref = refs[chunks + parts :]
    sums = [stat[...] for stat in stats]
    while len(sums) > 1:
        sums = [x + y for x, y in zip(sums[::2], sums[1::2])]
    total = sums[0]
    inverse = lax.rsqrt(total[0:1] * (1.0 / features) + EPS_OUT)
    loss = inverse * inverse * total[0:1] - 2.0 * inverse * total[1:2] + total[2:3]
    loss_ref[...] = jnp.maximum(loss, 0.0) * (1.0 / features)
    column = jnp.transpose(jnp.broadcast_to(inverse, total.shape))[:, :1]
    rows = branches[0].shape[0]
    for at in range(chunks):
        scale = column[at * rows : (at + 1) * rows]
        student_ref[at * rows : (at + 1) * rows, :] = (branches[at][...] * scale).astype(
            jnp.bfloat16
        )


def final(features, branches, stats):
    chunks, parts = len(branches), len(stats)
    part_rows, cols = branches[0].shape
    rows = part_rows * chunks
    return pl.pallas_call(
        functools.partial(final_kernel, features, chunks, parts),
        grid=(1,),
        in_specs=[whole((part_rows, cols))] * chunks + [whole((8, rows))] * parts,
        out_specs=[whole((rows, cols)), whole((1, rows))],
        out_shape=[
            jax.ShapeDtypeStruct((rows, cols), jnp.bfloat16),
            jax.ShapeDtypeStruct((1, rows), jnp.float32),
        ],
        compiler_params=params(16),
        cost_estimate=cost(2 * rows * cols, 6 * rows * cols),
        name="final",
    )(*branches, *stats)


def swap(x, mask):
    count = lax.axis_size("tp")
    return lax.ppermute(x, "tp", [(i, i ^ mask) for i in range(count)])


def send_up(x, first):
    count = lax.axis_size("ctx")
    return lax.ppermute(x, "ctx", [(i, i + 1) for i in range(first, count - 1)])


def after(x, *others):
    return lax.optimization_barrier((x,) + others)[0]


def gather(own, core_after=None, beside=None, middle=None):
    count = lax.axis_size("tp")
    got = {0: [own]}
    masks = [1 << b for b in range(1, count.bit_length() - 1)]
    if len(masks) >= 2:
        a, b = masks[0], masks[1]
        half = own.shape[0] // (2 * EXTRA) * EXTRA
        via_a, via_b = swap(own, a), swap(own, b)
        got[1] = [swap(own, 1)]
        if beside is not None:
            token = beside(got[1][0])
            via_a, via_b = after(via_a, token), after(via_b, token)
        got[a], got[b] = [via_a], [via_b]
        diagonal = [swap(via_a[:half], b), swap(via_b[half:], a)]
        if core_after is not None:
            diagonal = [after(p, core_after) for p in diagonal]
        got[a | 1], got[b | 1] = [swap(via_a, 1)], [swap(via_b, 1)]
        got[a | b] = diagonal
        if middle is not None:
            token = middle(got)
            diagonal = [after(p, token) for p in diagonal]
        got[a | b | 1] = [swap(p, 1) for p in diagonal]
        masks = masks[2:]
    elif count > 1:
        got[1] = [swap(own, 1)]
    for mask in masks:
        for m in list(got):
            got[m | mask] = [swap(p, mask) for p in got[m]]
    return [got[m] for m in range(count)]


def body(hidden_in, norm_gain, w_query, w_key, w_value, sign_bits, w_out, teacher):
    rows = hidden_in.shape[0]
    half = rows // HALVES
    tp_count = lax.axis_size("tp")
    ctx_count = lax.axis_size("ctx")
    features = hidden_in.shape[1] * tp_count
    tp_at = lax.axis_index("tp")
    ctx_at = jnp.reshape(lax.axis_index("ctx"), (1,)).astype(jnp.int32)
    masks = jnp.arange(tp_count, dtype=jnp.int32)
    order = tp_at ^ masks
    shared = tp_at & masks
    parity = jnp.zeros_like(shared)
    for bit in range(tp_count.bit_length()):
        parity = parity ^ (shared >> bit & 1)
    flips = (1 - 2 * parity).astype(jnp.float32)
    signs = (2 * sign_bits - 1).astype(jnp.float32)
    gain = norm_gain.reshape(-1, GROUP)

    gain, order, ctx_at, flips, signs = lax.optimization_barrier(
        (gain, order, ctx_at, flips, signs)
    )
    clipped = pre(hidden_in, gain)

    kv_cols = w_key.shape[1]
    sharing = HD // kv_cols if kv_cols < HD else 1
    kv_heads = kv_cols * sharing // HD
    loaded = []

    def bring(token):
        first = after(w_query, token, order, ctx_at, flips, signs)
        loaded.extend(load(first, w_key, w_value, w_out))
        return loaded[1]

    early, state = [], []

    def begin(got):
        early.extend(sorted(got)[:-1])
        part = {m: got[m] for m in early}
        state.extend(proj(order, part, rows, (), False, *loaded[:3]))
        return state[-1]

    blocks = gather(clipped, beside=bring, middle=begin)
    if not loaded:
        bring(clipped)
    late = {m: block for m, block in enumerate(blocks) if m not in early}
    q, *kvs = proj(order, late, rows, state, True, *loaded[:3])
    for i, kv in enumerate(kvs):
        if sharing > 1:
            k, v = kv[:, :kv_cols], kv[:, kv_cols:]
            for bit in range(sharing.bit_length() - 1):
                upper = tp_at >> bit & 1 == 1
                k2, v2 = swap(k, 1 << bit), swap(v, 1 << bit)
                k, v = (
                    jnp.where(
                        upper,
                        jnp.concatenate([far, near], axis=1),
                        jnp.concatenate([near, far], axis=1),
                    )
                    for near, far in ((k, k2), (v, v2))
                )
            kv = jnp.concatenate([k, v], axis=1)
        kvs[i] = kv
    far, sent = [], kvs
    for hop in range(1, ctx_count):
        sent = [send_up(kv, hop - 1) for kv in sent]
        far += [(hop, kv) for kv in sent]

    states = [
        attend(ctx_at, q, at * half, half, kv_heads, kvs[: at + 1], far[:-HALVES], None, None)
        for at in range(HALVES)
    ]
    q = after(q, *[state[0] for state in states])
    branches, stats = [], []
    for at in range(HALVES):
        signed = attend(
            ctx_at, q, at * half, half, kv_heads, [], far[-HALVES:], states[at], signs
        )
        blocks = gather(signed, branches[-1] if at else None)
        b, s = project_out(flips, blocks, loaded[3], teacher, at)
        branches.append(b)
        stats.append(s)
    stat = jnp.concatenate(stats, axis=1)
    if tp_count > 1:
        stat = stat + swap(stat, 1)
    totals = [stat] + [swap(stat, m) for m in range(2, tp_count, 2)]
    student, loss = final(features, branches, totals)
    return student, loss.reshape(rows)


def solution(mesh):
    in_specs = (
        P("ctx", "tp"),
        P("tp"),
        P(None, "tp"),
        P(None, "tp"),
        P(None, "tp"),
        P("tp", None),
        P(None, "tp"),
        P("ctx", "tp"),
    )
    out_specs = (P("ctx", "tp"), P("ctx"))
    return jax.shard_map(body, mesh=mesh, in_specs=in_specs, out_specs=out_specs, check_vma=False)
```

```python
import functools
import math

import jax
import jax.numpy as jnp
from jax import lax
from jax.experimental import pallas as pl
from jax.experimental.pallas import tpu as pltpu
from jax.sharding import PartitionSpec as P

HD = 128
GROUP = 128
EPS_IN = 1e-05
EPS_OUT = 1e-06
CLIP_RATIO = 0.9
FAR_BELOW = -1e30
LOG2E = math.log2(math.e)
HALVES = 2
EXTRA = 16
LOAD_PARTS = 4
LOAD_MIB = 38
PROJ_MIB = 14
ATT_MIB = 12
OUT_MIB = 12
MIB = 1024 * 1024


def params(mib, **kw):
    return pltpu.CompilerParams(vmem_limit_bytes=mib * MIB, **kw)


def whole(shape):
    zeros = (0,) * len(shape)
    return pl.BlockSpec(shape, lambda *_: zeros)


IN_SMEM = pl.BlockSpec(memory_space=pltpu.SMEM)
IN_VMEM = pl.BlockSpec(memory_space=pltpu.VMEM)
ANYWHERE = pl.BlockSpec(memory_space=pl.ANY)
IN_HBM = pl.BlockSpec(memory_space=pltpu.HBM)


def cost(flops, moved, trans=0):
    return pl.CostEstimate(flops=int(flops), bytes_accessed=int(moved), transcendentals=int(trans))


def clip_tile(v):
    limit = CLIP_RATIO * jnp.max(jnp.abs(v), axis=-1, keepdims=True)
    return jnp.clip(v, -limit, limit)


def pre_kernel(h_hbm, g_hbm, *refs):
    c_ref, h_all, g_ref, sem = refs
    rows, width = h_all.shape
    steps = sem.shape[0] - 1
    part = rows // steps
    copies = [pltpu.make_async_copy(g_hbm, g_ref, sem.at[steps])]
    for i in range(steps):
        at = slice(i * part, (i + 1) * part)
        copies.append(pltpu.make_async_copy(h_hbm.at[at], h_all.at[at], sem.at[i]))
    for copy in copies:
        copy.start()
    copies[0].wait()
    for i in range(steps):
        copies[i + 1].wait()
        total = jnp.zeros((part, GROUP), jnp.float32)
        row = i * part
        for at in range(0, width, GROUP):
            h = h_all[i * part : (i + 1) * part, at : at + GROUP].astype(jnp.float32)
            total = total + h * h
            v = h * g_ref[at // GROUP : at // GROUP + 1, :].astype(jnp.float32)
            c_ref[row : row + part, at : at + GROUP] = clip_tile(v).astype(jnp.bfloat16)
        sums = jnp.sum(total, axis=-1, keepdims=True)
        sums = jnp.transpose(jnp.broadcast_to(sums, (part, 128)))[:EXTRA]
        row = lax.broadcasted_iota(jnp.int32, sums.shape, 0)
        left = sums
        for place in range(3):
            piece = left.astype(jnp.bfloat16).astype(jnp.float32)
            left = left - piece
            sums = jnp.where(row == place, piece, sums)
        c_ref[rows:, i * part : (i + 1) * part] = sums.astype(jnp.bfloat16)


def pre(hidden, gain):
    rows, width = hidden.shape
    steps = 4
    return pl.pallas_call(
        pre_kernel,
        in_specs=[IN_HBM] * 2,
        out_specs=IN_VMEM,
        out_shape=pltpu.VMEM((rows + EXTRA, width), jnp.bfloat16),
        scratch_shapes=[
            pltpu.VMEM((rows, width), jnp.bfloat16),
            pltpu.VMEM(gain.shape, jnp.bfloat16),
            pltpu.SemaphoreType.DMA((steps + 1,)),
        ],
        compiler_params=params(62),
        cost_estimate=cost(8 * rows * width, 4 * rows * width),
        name="pre",
    )(hidden, gain)


def load_kernel(count, *refs):
    sources, goals, sem = refs[:count], refs[count : 2 * count], refs[-1]
    copies = []
    for i in range(count):
        depth = sources[i].shape[0] // LOAD_PARTS
        for p in range(LOAD_PARTS):
            at = slice(p * depth, (p + 1) * depth)
            copies.append(
                pltpu.make_async_copy(sources[i].at[at], goals[i].at[at], sem.at[i, p])
            )
    for copy in copies:
        copy.start()
    for copy in copies:
        copy.wait()


def load(*weights):
    count = len(weights)
    return pl.pallas_call(
        functools.partial(load_kernel, count),
        in_specs=[IN_HBM] * count,
        out_specs=[IN_VMEM] * count,
        out_shape=[pltpu.VMEM(w.shape, w.dtype) for w in weights],
        scratch_shapes=[pltpu.SemaphoreType.DMA((count, LOAD_PARTS))],
        compiler_params=params(LOAD_MIB),
        cost_estimate=cost(0, 2 * sum(w.size * 2 for w in weights)),
        name="load",
    )(*weights)


def proj_kernel(counts, masks, begins, ends, order_ref, *refs):
    depth = len(counts)
    blocks, refs = refs[: sum(counts)], refs[sum(counts) :]
    wq_ref, wk_ref, wv_ref, *refs = refs
    if not begins:
        *before, ss_in = refs[:4]
        refs = refs[4:]
        squares = ss_in[0:1, :]
    else:
        before = [None] * 3
        squares = jnp.zeros((1, ss_rows(blocks)), jnp.float32)
    if ends:
        q_ref, *kv_refs = refs[: 1 + HALVES]
        accs = refs[1 + HALVES :]
    else:
        *accs, ss_ref = refs
    nk = wk_ref.shape[1]
    k_rows = blocks[0].shape[1]
    at_block = 0
    for k in range(depth):
        at = pl.ds(pl.multiple_of(order_ref[masks[k]] * k_rows, k_rows), k_rows)
        mine = [b[...] for b in blocks[at_block : at_block + counts[k]]]
        at_block += counts[k]
        body_rows = mine[-1].shape[0] - EXTRA
        tail = mine[-1][body_rows:, : squares.shape[1]].astype(jnp.float32)
        squares = squares + (tail[0:1] + tail[1:2] + tail[2:3])
        mine[-1] = mine[-1][:body_rows]
        left = mine[0] if len(mine) == 1 else jnp.concatenate(mine, axis=0)
        wq, wk, wv = wq_ref[at, :], wk_ref[at, :], wv_ref[at, :]
        if nk % 128 == 0:
            both = jnp.dot(
                left, jnp.concatenate([wk, wv], axis=1), preferred_element_type=jnp.float32
            )
            parts = (both[:, :nk], both[:, nk:])
        else:
            parts = [jnp.dot(left, w, preferred_element_type=jnp.float32) for w in (wk, wv)]
        first = jnp.dot(left, wq, preferred_element_type=jnp.float32)
        for part, acc, old in zip((first, *parts), accs, before):
            if k:
                acc[...] += part
            elif not begins:
                acc[...] = old[...] + part
            else:
                acc[...] = part

    if not ends:
        ss_ref[...] = jnp.broadcast_to(squares, ss_ref.shape)
    else:
        accq, acck, accv = accs
        features = wq_ref.shape[0]
        squares = jnp.broadcast_to(squares, (8, squares.shape[1]))
        inverse = lax.rsqrt(squares * (1.0 / features) + EPS_IN)
        scale = jnp.transpose(inverse)[:, :1]
        q_ref[...] = (accq[...] * scale).astype(jnp.bfloat16)
        rows = kv_refs[0].shape[0]
        for i, kv_ref in enumerate(kv_refs):
            at = slice(i * rows, (i + 1) * rows)
            kv_ref[:, :nk] = (acck[at, :] * scale[at]).astype(jnp.bfloat16)
            kv_ref[:, nk:] = (accv[at, :] * scale[at]).astype(jnp.bfloat16)


def ss_rows(blocks):
    return blocks[0].shape[0] - EXTRA


def proj(order, blocks, rows, state, ends, wq, wk, wv):
    masks = sorted(blocks)
    blocks = [blocks[m] for m in masks]
    depth = len(blocks)
    counts = [len(b) for b in blocks]
    part_cols = blocks[0][0].shape[1]
    sizes = wq.shape[1], wk.shape[1], wv.shape[1]
    n = sum(sizes)
    flat = [p for b in blocks for p in b]
    args = [order, *flat, wq, wk, wv, *state]
    if ends:
        out_shape = [
            jax.ShapeDtypeStruct((rows, sizes[0]), jnp.bfloat16),
        ] + [
            jax.ShapeDtypeStruct((rows // HALVES, sizes[1] + sizes[2]), jnp.bfloat16)
            for _ in range(HALVES)
        ]
        scratch = [pltpu.VMEM((rows, m), jnp.float32) for m in sizes]
    else:
        out_shape = [pltpu.VMEM((rows, m), jnp.float32) for m in sizes]
        out_shape.append(jax.ShapeDtypeStruct((8, rows), jnp.float32))
        scratch = []
    return pl.pallas_call(
        functools.partial(proj_kernel, counts, masks, not state, ends),
        in_specs=[IN_SMEM] + [IN_VMEM] * (len(args) - 1),
        out_specs=[IN_VMEM] * len(out_shape),
        out_shape=out_shape,
        scratch_shapes=scratch,
        compiler_params=params(PROJ_MIB),
        cost_estimate=cost(
            2 * rows * part_cols * depth * n, 2 * part_cols * depth * (rows + n)
        ),
        name="proj",
    )(*args)


def att_kernel(first, kv_heads, near, far, begins, ends, me_ref, q_ref, *refs):
    count = near + len(far)
    kvs, refs = refs[:count], refs[count:]
    if not begins:
        high_in, total_in, accum_in, *refs = refs
    if ends:
        sign_ref, o_ref, high, total, accum = refs
    else:
        high, total, accum = refs
    rows = accum.shape[2]
    heads = q_ref.shape[1] // HD
    part = kvs[0].shape[0]
    group = heads // kv_heads
    scale = HD ** (-0.5) * LOG2E

    if not begins:
        high[...] = high_in[...]
        total[...] = total_in[...]
        accum[...] = accum_in[...]

    def visit(kv_ref, sub, start, fresh):
        keys = slice(sub * part, (sub + 1) * part)
        masked = start is not None and start + part > first
        scores, turned = [], []
        for kv in range(kv_heads):
            at = (kv_heads + kv) * HD
            turned.append(jnp.transpose(kv_ref[keys, at : at + HD]))
        for head in range(heads):
            kv = head // group
            q = q_ref[first : first + rows, head * HD : (head + 1) * HD]
            k = kv_ref[keys, kv * HD : (kv + 1) * HD]
            s = lax.dot_general(
                k, q, (((1,), (1,)), ((), ())), preferred_element_type=jnp.float32
            )
            if masked:
                kpos = start + lax.broadcasted_iota(jnp.int32, s.shape, 0)
                qpos = first + lax.broadcasted_iota(jnp.int32, s.shape, 1)
                s = jnp.where(kpos <= qpos, s, FAR_BELOW)
            scores.append(s)
        for head in range(heads):
            s = scores[head]
            best = jnp.max(s, axis=0, keepdims=True)
            if not fresh:
                before = high[head : head + 1]
                best = jnp.maximum(best, before)
            w = jnp.exp2((s - best) * scale)
            sums = jnp.sum(w, axis=0, keepdims=True)
            mixed = jnp.dot(
                turned[head // group], w.astype(jnp.bfloat16), preferred_element_type=jnp.float32
            )
            if fresh:
                total[head : head + 1] = sums
                accum[head] = mixed
            else:
                decay = jnp.exp2((before - best) * scale)
                total[head : head + 1] = total[head : head + 1] * decay + sums
                accum[head] = accum[head] * decay + mixed
            high[head : head + 1] = best

    for at in range(near):
        visit(kvs[at], 0, at * part, begins and at == 0)
    for at, hop in enumerate(far):

        @pl.when(me_ref[0] >= hop)
        def _():
            visit(kvs[near + at], 0, None, False)

    if ends:
        for head in range(heads):
            att = jnp.transpose(accum[head] / total[head : head + 1])
            att = att.astype(jnp.bfloat16).astype(jnp.float32)
            o_ref[:, head * HD : (head + 1) * HD] = (att * sign_ref[head : head + 1, :]).astype(
                jnp.bfloat16
            )


def attend(me, q, first, rows, kv_heads, near, far, state, signs):
    heads = q.shape[1] // HD
    kvs = near + [kv for _, kv in far]
    keys = sum(kv.shape[0] for kv in kvs)
    shapes = [(max(heads, 8), rows), (max(heads, 8), rows), (heads, HD, rows)]
    args = [me, q, *kvs]
    if state is not None:
        args += list(state)
    if signs is None:
        out_shape = [jax.ShapeDtypeStruct(shape, jnp.float32) for shape in shapes]
        scratch = []
    else:
        args.append(signs)
        out_shape = jax.ShapeDtypeStruct((rows, heads * HD), jnp.bfloat16)
        scratch = [pltpu.VMEM(shape, jnp.float32) for shape in shapes]
    far_at = [n for n, _ in far]
    kernel = functools.partial(
        att_kernel, first, kv_heads, len(near), far_at, state is None, signs is not None
    )
    return pl.pallas_call(
        kernel,
        in_specs=[IN_SMEM] + [IN_VMEM] * (len(args) - 1),
        out_specs=IN_VMEM if signs is not None else [IN_VMEM] * 3,
        out_shape=out_shape,
        scratch_shapes=scratch,
        compiler_params=params(ATT_MIB),
        cost_estimate=cost(4 * rows * keys * heads * HD, 4 * keys * HD, rows * keys * heads),
        name="attend",
    )(*args)


def butterfly(tiles):
    count = len(tiles)
    span = 1
    while span < count:
        out = list(tiles)
        for at in range(count):
            if not at & span:
                a, b = tiles[at], tiles[at | span]
                out[at], out[at | span] = a + b, a - b
        tiles = out
        span *= 2
    return tiles


def out_kernel(counts, steps, chunk, sign_ref, t_ref, *refs):
    parts = len(counts)
    blocks, at_block = [], 0
    for n in counts:
        blocks.append(refs[at_block : at_block + n])
        at_block += n
    w_ref, b_ref, s_ref, mid, rot, acc = refs[at_block:]
    rows = b_ref.shape[0]
    width = blocks[0][0].shape[1]
    here = width // HD
    heads = here * parts
    factor = heads ** (-0.5)

    strip = 16
    most = max(counts)
    span = rows // most
    for section in range(most):

        def turn(i, carry):
            at = pl.multiple_of(section * span + i * strip, strip)
            for m in range(parts):
                if len(blocks[m]) == 1:
                    ref, start = blocks[m][0], at
                else:
                    ref, start = blocks[m][section], pl.multiple_of(i * strip, strip)
                tiles = [
                    ref[pl.ds(start, strip), h * HD : (h + 1) * HD].astype(jnp.float32)
                    for h in range(here)
                ]
                for h, v in enumerate(butterfly(tiles)):
                    mid[m * here + h] = v
            for h in range(here):
                tiles = butterfly([mid[m * here + h] for m in range(parts)])
                for m in range(parts):
                    v = tiles[m] * (factor * sign_ref[m])
                    col = (m * here + h) * HD
                    rot[pl.ds(at, strip), col : col + HD] = clip_tile(v).astype(jnp.bfloat16)
            return carry

        lax.fori_loop(0, span // strip, turn, 0)

    depth = w_ref.shape[0] // steps
    for i in range(steps):
        part = jnp.dot(
            rot[:, i * depth : (i + 1) * depth],
            w_ref[i * depth : (i + 1) * depth, :],
            preferred_element_type=jnp.float32,
        )
        if i == 0:
            acc[...] = part
        else:
            acc[...] += part

    b = acc[...]
    t = t_ref[chunk * rows : (chunk + 1) * rows, :].astype(jnp.float32)
    b_ref[...] = b
    sums = [jnp.sum(v, axis=-1, keepdims=True) for v in (b * b, b * t, t * t)]
    lane = lax.broadcasted_iota(jnp.int32, (rows, 128), 1)
    wide = jnp.where(lane == 0, sums[0], jnp.where(lane == 1, sums[1], sums[2]))
    s_ref[...] = jnp.transpose(wide)[:8]


def project_out(flips, blocks, w_out, teacher, chunk):
    parts = len(blocks)
    counts = [len(b) for b in blocks]
    rows, width = blocks[0][0].shape
    depth, cols = w_out.shape
    steps = 4
    flat = [p for b in blocks for p in b]
    return pl.pallas_call(
        functools.partial(out_kernel, counts, steps, chunk),
        in_specs=[IN_SMEM] + [IN_VMEM] * (len(flat) + 2),
        out_specs=[IN_VMEM, IN_VMEM],
        out_shape=[
            jax.ShapeDtypeStruct((rows, cols), jnp.float32),
            jax.ShapeDtypeStruct((8, rows), jnp.float32),
        ],
        scratch_shapes=[
            pltpu.VMEM((parts * width // HD, 16, HD), jnp.float32),
            pltpu.VMEM((rows, depth), jnp.bfloat16),
            pltpu.VMEM((rows, cols), jnp.float32),
        ],
        compiler_params=params(OUT_MIB),
        cost_estimate=cost(2 * rows * depth * cols, 2 * depth * (rows + cols) + 6 * rows * cols),
        name="project_out",
    )(flips, teacher, *flat, w_out)


def final_kernel(features, chunks, parts, *refs):
    branches, stats = refs[:chunks], refs[chunks : chunks + parts]
    student_ref, loss_ref = refs[chunks + parts :]
    sums = [stat[...] for stat in stats]
    while len(sums) > 1:
        sums = [x + y for x, y in zip(sums[::2], sums[1::2])]
    total = sums[0]
    inverse = lax.rsqrt(total[0:1] * (1.0 / features) + EPS_OUT)
    loss = inverse * inverse * total[0:1] - 2.0 * inverse * total[1:2] + total[2:3]
    loss_ref[...] = jnp.maximum(loss, 0.0) * (1.0 / features)
    column = jnp.transpose(jnp.broadcast_to(inverse, total.shape))[:, :1]
    rows = branches[0].shape[0]
    for at in range(chunks):
        scale = column[at * rows : (at + 1) * rows]
        student_ref[at * rows : (at + 1) * rows, :] = (branches[at][...] * scale).astype(
            jnp.bfloat16
        )


def final(features, branches, stats):
    chunks, parts = len(branches), len(stats)
    part_rows, cols = branches[0].shape
    rows = part_rows * chunks
    return pl.pallas_call(
        functools.partial(final_kernel, features, chunks, parts),
        grid=(1,),
        in_specs=[whole((part_rows, cols))] * chunks + [whole((8, rows))] * parts,
        out_specs=[whole((rows, cols)), whole((1, rows))],
        out_shape=[
            jax.ShapeDtypeStruct((rows, cols), jnp.bfloat16),
            jax.ShapeDtypeStruct((1, rows), jnp.float32),
        ],
        compiler_params=params(16),
        cost_estimate=cost(2 * rows * cols, 6 * rows * cols),
        name="final",
    )(*branches, *stats)


def swap(x, mask):
    count = lax.axis_size("tp")
    return lax.ppermute(x, "tp", [(i, i ^ mask) for i in range(count)])


def send_up(x, first):
    count = lax.axis_size("ctx")
    return lax.ppermute(x, "ctx", [(i, i + 1) for i in range(first, count - 1)])


def after(x, *others):
    return lax.optimization_barrier((x,) + others)[0]


def gather(own, core_after=None, beside=None, middle=None):
    count = lax.axis_size("tp")
    got = {0: [own]}
    masks = [1 << b for b in range(1, count.bit_length() - 1)]
    if len(masks) >= 2:
        a, b = masks[0], masks[1]
        half = own.shape[0] // (2 * EXTRA) * EXTRA
        via_a, via_b = swap(own, a), swap(own, b)
        got[1] = [swap(own, 1)]
        if beside is not None:
            token = beside(got[1][0])
            via_a, via_b = after(via_a, token), after(via_b, token)
        got[a], got[b] = [via_a], [via_b]
        diagonal = [swap(via_a[:half], b), swap(via_b[half:], a)]
        if core_after is not None:
            diagonal = [after(p, core_after) for p in diagonal]
        got[a | 1], got[b | 1] = [swap(via_a, 1)], [swap(via_b, 1)]
        got[a | b] = diagonal
        if middle is not None:
            token = middle(got)
            diagonal = [after(p, token) for p in diagonal]
        got[a | b | 1] = [swap(p, 1) for p in diagonal]
        masks = masks[2:]
    elif count > 1:
        got[1] = [swap(own, 1)]
    for mask in masks:
        for m in list(got):
            got[m | mask] = [swap(p, mask) for p in got[m]]
    return [got[m] for m in range(count)]


def body(hidden_in, norm_gain, w_query, w_key, w_value, sign_bits, w_out, teacher):
    rows = hidden_in.shape[0]
    half = rows // HALVES
    tp_count = lax.axis_size("tp")
    ctx_count = lax.axis_size("ctx")
    features = hidden_in.shape[1] * tp_count
    tp_at = lax.axis_index("tp")
    ctx_at = jnp.reshape(lax.axis_index("ctx"), (1,)).astype(jnp.int32)
    masks = jnp.arange(tp_count, dtype=jnp.int32)
    order = tp_at ^ masks
    shared = tp_at & masks
    parity = jnp.zeros_like(shared)
    for bit in range(tp_count.bit_length()):
        parity = parity ^ (shared >> bit & 1)
    flips = (1 - 2 * parity).astype(jnp.float32)
    signs = (2 * sign_bits - 1).astype(jnp.float32)
    gain = norm_gain.reshape(-1, GROUP)

    clipped = pre(hidden_in, gain)

    kv_cols = w_key.shape[1]
    sharing = HD // kv_cols if kv_cols < HD else 1
    kv_heads = kv_cols * sharing // HD
    loaded = []

    def bring(token):
        first = after(w_query, token, order, ctx_at, flips, signs)
        loaded.extend(load(first, w_key, w_value, w_out))
        return loaded[1]

    early, state = [], []

    def begin(got):
        early.extend(sorted(got)[:-1])
        part = {m: got[m] for m in early}
        state.extend(proj(order, part, rows, (), False, *loaded[:3]))
        return state[-1]

    blocks = gather(clipped, beside=bring, middle=begin)
    if not loaded:
        bring(clipped)
    late = {m: block for m, block in enumerate(blocks) if m not in early}
    q, *kvs = proj(order, late, rows, state, True, *loaded[:3])
    for i, kv in enumerate(kvs):
        if sharing > 1:
            k, v = kv[:, :kv_cols], kv[:, kv_cols:]
            for bit in range(sharing.bit_length() - 1):
                upper = tp_at >> bit & 1 == 1
                k2, v2 = swap(k, 1 << bit), swap(v, 1 << bit)
                k, v = (
                    jnp.where(
                        upper,
                        jnp.concatenate([far, near], axis=1),
                        jnp.concatenate([near, far], axis=1),
                    )
                    for near, far in ((k, k2), (v, v2))
                )
            kv = jnp.concatenate([k, v], axis=1)
        kvs[i] = kv
    far, sent, states = [], kvs, []
    for hop in range(1, ctx_count):
        if hop == 3:
            sent = [after(kv, *[state[0] for state in states]) for kv in sent]
        sent = [send_up(kv, hop - 1) for kv in sent]
        far += [(hop, kv) for kv in sent]
        begun = far if ctx_count > 2 else []
        if hop == 1:
            states = [
                attend(ctx_at, q, at * half, half, kv_heads, kvs[: at + 1], begun, None, None)
                for at in range(HALVES)
            ]
    middle = far[HALVES:-HALVES]
    if middle:
        states = [
            attend(ctx_at, q, at * half, half, kv_heads, [], middle, states[at], None)
            for at in range(HALVES)
        ]
    q = after(q, *[state[0] for state in states])
    branches, stats = [], []
    for at in range(HALVES):
        signed = attend(
            ctx_at, q, at * half, half, kv_heads, [], far[-HALVES:], states[at], signs
        )
        blocks = gather(signed, branches[-1] if at else None)
        b, s = project_out(flips, blocks, loaded[3], teacher, at)
        branches.append(b)
        stats.append(s)
    stat = jnp.concatenate(stats, axis=1)
    if tp_count > 1:
        stat = stat + swap(stat, 1)
    totals = [stat] + [swap(stat, m) for m in range(2, tp_count, 2)]
    student, loss = final(features, branches, totals)
    return student, loss.reshape(rows)


def solution(mesh):
    in_specs = (
        P("ctx", "tp"),
        P("tp"),
        P(None, "tp"),
        P(None, "tp"),
        P(None, "tp"),
        P("tp", None),
        P(None, "tp"),
        P("ctx", "tp"),
    )
    out_specs = (P("ctx", "tp"), P("ctx"))
    return jax.shard_map(body, mesh=mesh, in_specs=in_specs, out_specs=out_specs, check_vma=False)
```

```python
import functools
import math

import jax
import jax.numpy as jnp
from jax import lax
from jax.experimental import pallas as pl
from jax.experimental.pallas import tpu as pltpu
from jax.sharding import PartitionSpec as P

HD = 128
GROUP = 128
EPS_IN = 1e-05
EPS_OUT = 1e-06
CLIP_RATIO = 0.9
FAR_BELOW = -1e30
LOG2E = math.log2(math.e)
HALVES = 2
EXTRA = 16
LOAD_PARTS = 4
LOAD_MIB = 37
PROJ_MIB = 14
ATT_MIB = 12
OUT_MIB = 12
MIB = 1024 * 1024


def params(mib, **kw):
    return pltpu.CompilerParams(vmem_limit_bytes=mib * MIB, **kw)


def whole(shape):
    zeros = (0,) * len(shape)
    return pl.BlockSpec(shape, lambda *_: zeros)


IN_SMEM = pl.BlockSpec(memory_space=pltpu.SMEM)
IN_VMEM = pl.BlockSpec(memory_space=pltpu.VMEM)
ANYWHERE = pl.BlockSpec(memory_space=pl.ANY)
IN_HBM = pl.BlockSpec(memory_space=pltpu.HBM)


def cost(flops, moved, trans=0):
    return pl.CostEstimate(flops=int(flops), bytes_accessed=int(moved), transcendentals=int(trans))


def clip_tile(v):
    limit = CLIP_RATIO * jnp.max(jnp.abs(v), axis=-1, keepdims=True)
    return jnp.clip(v, -limit, limit)


def pre_kernel(h_hbm, g_hbm, *refs):
    c_ref, h_all, g_ref, sem = refs
    rows, width = h_all.shape
    steps = sem.shape[0] - 1
    part = rows // steps
    copies = [pltpu.make_async_copy(g_hbm, g_ref, sem.at[steps])]
    for i in range(steps):
        at = slice(i * part, (i + 1) * part)
        copies.append(pltpu.make_async_copy(h_hbm.at[at], h_all.at[at], sem.at[i]))
    for copy in copies:
        copy.start()
    copies[0].wait()
    for i in range(steps):
        copies[i + 1].wait()
        total = jnp.zeros((part, GROUP), jnp.float32)
        row = i * part
        for at in range(0, width, GROUP):
            h = h_all[i * part : (i + 1) * part, at : at + GROUP].astype(jnp.float32)
            total = total + h * h
            v = h * g_ref[at // GROUP : at // GROUP + 1, :].astype(jnp.float32)
            c_ref[row : row + part, at : at + GROUP] = clip_tile(v).astype(jnp.bfloat16)
        sums = jnp.sum(total, axis=-1, keepdims=True)
        sums = jnp.transpose(jnp.broadcast_to(sums, (part, 128)))[:EXTRA]
        row = lax.broadcasted_iota(jnp.int32, sums.shape, 0)
        left = sums
        for place in range(3):
            piece = left.astype(jnp.bfloat16).astype(jnp.float32)
            left = left - piece
            sums = jnp.where(row == place, piece, sums)
        c_ref[rows:, i * part : (i + 1) * part] = sums.astype(jnp.bfloat16)


def pre(hidden, gain):
    rows, width = hidden.shape
    steps = 4
    return pl.pallas_call(
        pre_kernel,
        in_specs=[IN_HBM] * 2,
        out_specs=IN_VMEM,
        out_shape=pltpu.VMEM((rows + EXTRA, width), jnp.bfloat16),
        scratch_shapes=[
            pltpu.VMEM((rows, width), jnp.bfloat16),
            pltpu.VMEM(gain.shape, jnp.bfloat16),
            pltpu.SemaphoreType.DMA((steps + 1,)),
        ],
        compiler_params=params(62),
        cost_estimate=cost(8 * rows * width, 4 * rows * width),
        name="pre",
    )(hidden, gain)


def load_kernel(count, *refs):
    sources, goals, sem = refs[:count], refs[count : 2 * count], refs[-1]
    copies = []
    for i in range(count):
        depth = sources[i].shape[0] // LOAD_PARTS
        for p in range(LOAD_PARTS):
            at = slice(p * depth, (p + 1) * depth)
            copies.append(
                pltpu.make_async_copy(sources[i].at[at], goals[i].at[at], sem.at[i, p])
            )
    for copy in copies:
        copy.start()
    for copy in copies:
        copy.wait()


def load(*weights):
    count = len(weights)
    return pl.pallas_call(
        functools.partial(load_kernel, count),
        in_specs=[IN_HBM] * count,
        out_specs=[IN_VMEM] * count,
        out_shape=[pltpu.VMEM(w.shape, w.dtype) for w in weights],
        scratch_shapes=[pltpu.SemaphoreType.DMA((count, LOAD_PARTS))],
        compiler_params=params(LOAD_MIB),
        cost_estimate=cost(0, 2 * sum(w.size * 2 for w in weights)),
        name="load",
    )(*weights)


def proj_kernel(counts, masks, begins, ends, order_ref, *refs):
    depth = len(counts)
    blocks, refs = refs[: sum(counts)], refs[sum(counts) :]
    wq_ref, wk_ref, wv_ref, *refs = refs
    if not begins:
        *before, ss_in = refs[:4]
        refs = refs[4:]
        squares = ss_in[0:1, :]
    else:
        before = [None] * 3
        squares = jnp.zeros((1, ss_rows(blocks)), jnp.float32)
    if ends:
        q_ref, *kv_refs = refs[: 1 + HALVES]
        accs = refs[1 + HALVES :]
    else:
        *accs, ss_ref = refs
    nk = wk_ref.shape[1]
    k_rows = blocks[0].shape[1]
    at_block = 0
    for k in range(depth):
        at = pl.ds(pl.multiple_of(order_ref[masks[k]] * k_rows, k_rows), k_rows)
        mine = [b[...] for b in blocks[at_block : at_block + counts[k]]]
        at_block += counts[k]
        body_rows = mine[-1].shape[0] - EXTRA
        tail = mine[-1][body_rows:, : squares.shape[1]].astype(jnp.float32)
        squares = squares + (tail[0:1] + tail[1:2] + tail[2:3])
        mine[-1] = mine[-1][:body_rows]
        left = mine[0] if len(mine) == 1 else jnp.concatenate(mine, axis=0)
        wq, wk, wv = wq_ref[at, :], wk_ref[at, :], wv_ref[at, :]
        if nk % 128 == 0:
            both = jnp.dot(
                left, jnp.concatenate([wk, wv], axis=1), preferred_element_type=jnp.float32
            )
            parts = (both[:, :nk], both[:, nk:])
        else:
            parts = [jnp.dot(left, w, preferred_element_type=jnp.float32) for w in (wk, wv)]
        first = jnp.dot(left, wq, preferred_element_type=jnp.float32)
        for part, acc, old in zip((first, *parts), accs, before):
            if k:
                acc[...] += part
            elif not begins:
                acc[...] = old[...] + part
            else:
                acc[...] = part

    if not ends:
        ss_ref[...] = jnp.broadcast_to(squares, ss_ref.shape)
    else:
        accq, acck, accv = accs
        features = wq_ref.shape[0]
        squares = jnp.broadcast_to(squares, (8, squares.shape[1]))
        inverse = lax.rsqrt(squares * (1.0 / features) + EPS_IN)
        scale = jnp.transpose(inverse)[:, :1]
        q_ref[...] = (accq[...] * scale).astype(jnp.bfloat16)
        rows = kv_refs[0].shape[0]
        for i, kv_ref in enumerate(kv_refs):
            at = slice(i * rows, (i + 1) * rows)
            kv_ref[:, :nk] = (acck[at, :] * scale[at]).astype(jnp.bfloat16)
            kv_ref[:, nk:] = (accv[at, :] * scale[at]).astype(jnp.bfloat16)


def ss_rows(blocks):
    return blocks[0].shape[0] - EXTRA


def proj(order, blocks, rows, state, ends, wq, wk, wv):
    masks = sorted(blocks)
    blocks = [blocks[m] for m in masks]
    depth = len(blocks)
    counts = [len(b) for b in blocks]
    part_cols = blocks[0][0].shape[1]
    sizes = wq.shape[1], wk.shape[1], wv.shape[1]
    n = sum(sizes)
    flat = [p for b in blocks for p in b]
    args = [order, *flat, wq, wk, wv, *state]
    if ends:
        out_shape = [
            jax.ShapeDtypeStruct((rows, sizes[0]), jnp.bfloat16),
        ] + [
            jax.ShapeDtypeStruct((rows // HALVES, sizes[1] + sizes[2]), jnp.bfloat16)
            for _ in range(HALVES)
        ]
        scratch = [pltpu.VMEM((rows, m), jnp.float32) for m in sizes]
    else:
        out_shape = [pltpu.VMEM((rows, m), jnp.float32) for m in sizes]
        out_shape.append(jax.ShapeDtypeStruct((8, rows), jnp.float32))
        scratch = []
    return pl.pallas_call(
        functools.partial(proj_kernel, counts, masks, not state, ends),
        in_specs=[IN_SMEM] + [IN_VMEM] * (len(args) - 1),
        out_specs=[IN_VMEM] * len(out_shape),
        out_shape=out_shape,
        scratch_shapes=scratch,
        compiler_params=params(PROJ_MIB),
        cost_estimate=cost(
            2 * rows * part_cols * depth * n, 2 * part_cols * depth * (rows + n)
        ),
        name="proj",
    )(*args)


def att_kernel(first, kv_heads, near, far, begins, ends, me_ref, q_ref, *refs):
    count = near + len(far)
    kvs, refs = refs[:count], refs[count:]
    if not begins:
        high_in, total_in, accum_in, *refs = refs
    if ends:
        sign_ref, o_ref, high, total, accum = refs
    else:
        high, total, accum = refs
    rows = accum.shape[2]
    heads = q_ref.shape[1] // HD
    part = kvs[0].shape[0]
    group = heads // kv_heads
    scale = HD ** (-0.5) * LOG2E

    if not begins:
        high[...] = high_in[...]
        total[...] = total_in[...]
        accum[...] = accum_in[...]

    def visit(kv_ref, sub, start, fresh):
        keys = slice(sub * part, (sub + 1) * part)
        masked = start is not None and start + part > first
        scores, turned = [], []
        for kv in range(kv_heads):
            at = (kv_heads + kv) * HD
            turned.append(jnp.transpose(kv_ref[keys, at : at + HD]))
        for head in range(heads):
            kv = head // group
            q = q_ref[first : first + rows, head * HD : (head + 1) * HD]
            k = kv_ref[keys, kv * HD : (kv + 1) * HD]
            s = lax.dot_general(
                k, q, (((1,), (1,)), ((), ())), preferred_element_type=jnp.float32
            )
            if masked:
                kpos = start + lax.broadcasted_iota(jnp.int32, s.shape, 0)
                qpos = first + lax.broadcasted_iota(jnp.int32, s.shape, 1)
                s = jnp.where(kpos <= qpos, s, FAR_BELOW)
            scores.append(s)
        for head in range(heads):
            s = scores[head]
            best = jnp.max(s, axis=0, keepdims=True)
            if not fresh:
                before = high[head : head + 1]
                best = jnp.maximum(best, before)
            w = jnp.exp2((s - best) * scale)
            sums = jnp.sum(w, axis=0, keepdims=True)
            mixed = jnp.dot(
                turned[head // group], w.astype(jnp.bfloat16), preferred_element_type=jnp.float32
            )
            if fresh:
                total[head : head + 1] = sums
                accum[head] = mixed
            else:
                decay = jnp.exp2((before - best) * scale)
                total[head : head + 1] = total[head : head + 1] * decay + sums
                accum[head] = accum[head] * decay + mixed
            high[head : head + 1] = best

    for at in range(near):
        visit(kvs[at], 0, at * part, begins and at == 0)
    for at, hop in enumerate(far):

        @pl.when(me_ref[0] >= hop)
        def _():
            visit(kvs[near + at], 0, None, False)

    if ends:
        for head in range(heads):
            att = jnp.transpose(accum[head] / total[head : head + 1])
            att = att.astype(jnp.bfloat16).astype(jnp.float32)
            o_ref[:, head * HD : (head + 1) * HD] = (att * sign_ref[head : head + 1, :]).astype(
                jnp.bfloat16
            )


def attend(me, q, first, rows, kv_heads, near, far, state, signs):
    heads = q.shape[1] // HD
    kvs = near + [kv for _, kv in far]
    keys = sum(kv.shape[0] for kv in kvs)
    shapes = [(max(heads, 8), rows), (max(heads, 8), rows), (heads, HD, rows)]
    args = [me, q, *kvs]
    if state is not None:
        args += list(state)
    if signs is None:
        out_shape = [jax.ShapeDtypeStruct(shape, jnp.float32) for shape in shapes]
        scratch = []
    else:
        args.append(signs)
        out_shape = jax.ShapeDtypeStruct((rows, heads * HD), jnp.bfloat16)
        scratch = [pltpu.VMEM(shape, jnp.float32) for shape in shapes]
    far_at = [n for n, _ in far]
    kernel = functools.partial(
        att_kernel, first, kv_heads, len(near), far_at, state is None, signs is not None
    )
    return pl.pallas_call(
        kernel,
        in_specs=[IN_SMEM] + [IN_VMEM] * (len(args) - 1),
        out_specs=IN_VMEM if signs is not None else [IN_VMEM] * 3,
        out_shape=out_shape,
        scratch_shapes=scratch,
        compiler_params=params(ATT_MIB),
        cost_estimate=cost(4 * rows * keys * heads * HD, 4 * keys * HD, rows * keys * heads),
        name="attend",
    )(*args)


def butterfly(tiles):
    count = len(tiles)
    span = 1
    while span < count:
        out = list(tiles)
        for at in range(count):
            if not at & span:
                a, b = tiles[at], tiles[at | span]
                out[at], out[at | span] = a + b, a - b
        tiles = out
        span *= 2
    return tiles


def out_kernel(counts, steps, chunk, sign_ref, t_ref, *refs):
    parts = len(counts)
    blocks, at_block = [], 0
    for n in counts:
        blocks.append(refs[at_block : at_block + n])
        at_block += n
    w_ref, b_ref, s_ref, mid, rot, acc = refs[at_block:]
    rows = b_ref.shape[0]
    width = blocks[0][0].shape[1]
    here = width // HD
    heads = here * parts
    factor = heads ** (-0.5)

    strip = 16
    most = max(counts)
    span = rows // most
    for section in range(most):

        def turn(i, carry):
            at = pl.multiple_of(section * span + i * strip, strip)
            for m in range(parts):
                if len(blocks[m]) == 1:
                    ref, start = blocks[m][0], at
                else:
                    ref, start = blocks[m][section], pl.multiple_of(i * strip, strip)
                tiles = [
                    ref[pl.ds(start, strip), h * HD : (h + 1) * HD].astype(jnp.float32)
                    for h in range(here)
                ]
                for h, v in enumerate(butterfly(tiles)):
                    mid[m * here + h] = v
            for h in range(here):
                tiles = butterfly([mid[m * here + h] for m in range(parts)])
                for m in range(parts):
                    v = tiles[m] * (factor * sign_ref[m])
                    col = (m * here + h) * HD
                    rot[pl.ds(at, strip), col : col + HD] = clip_tile(v).astype(jnp.bfloat16)
            return carry

        lax.fori_loop(0, span // strip, turn, 0)

    depth = w_ref.shape[0] // steps
    for i in range(steps):
        part = jnp.dot(
            rot[:, i * depth : (i + 1) * depth],
            w_ref[i * depth : (i + 1) * depth, :],
            preferred_element_type=jnp.float32,
        )
        if i == 0:
            acc[...] = part
        else:
            acc[...] += part

    b = acc[...]
    t = t_ref[chunk * rows : (chunk + 1) * rows, :].astype(jnp.float32)
    b_ref[...] = b
    sums = [jnp.sum(v, axis=-1, keepdims=True) for v in (b * b, b * t, t * t)]
    lane = lax.broadcasted_iota(jnp.int32, (rows, 128), 1)
    wide = jnp.where(lane == 0, sums[0], jnp.where(lane == 1, sums[1], sums[2]))
    s_ref[...] = jnp.transpose(wide)[:8]


def project_out(flips, blocks, w_out, teacher, chunk):
    parts = len(blocks)
    counts = [len(b) for b in blocks]
    rows, width = blocks[0][0].shape
    depth, cols = w_out.shape
    steps = 4
    flat = [p for b in blocks for p in b]
    return pl.pallas_call(
        functools.partial(out_kernel, counts, steps, chunk),
        in_specs=[IN_SMEM] + [IN_VMEM] * (len(flat) + 2),
        out_specs=[IN_VMEM, IN_VMEM],
        out_shape=[
            jax.ShapeDtypeStruct((rows, cols), jnp.float32),
            jax.ShapeDtypeStruct((8, rows), jnp.float32),
        ],
        scratch_shapes=[
            pltpu.VMEM((parts * width // HD, 16, HD), jnp.float32),
            pltpu.VMEM((rows, depth), jnp.bfloat16),
            pltpu.VMEM((rows, cols), jnp.float32),
        ],
        compiler_params=params(OUT_MIB),
        cost_estimate=cost(2 * rows * depth * cols, 2 * depth * (rows + cols) + 6 * rows * cols),
        name="project_out",
    )(flips, teacher, *flat, w_out)


def final_kernel(features, chunks, parts, *refs):
    branches, stats = refs[:chunks], refs[chunks : chunks + parts]
    student_ref, loss_ref = refs[chunks + parts :]
    sums = [stat[...] for stat in stats]
    while len(sums) > 1:
        sums = [x + y for x, y in zip(sums[::2], sums[1::2])]
    total = sums[0]
    inverse = lax.rsqrt(total[0:1] * (1.0 / features) + EPS_OUT)
    loss = inverse * inverse * total[0:1] - 2.0 * inverse * total[1:2] + total[2:3]
    loss_ref[...] = jnp.maximum(loss, 0.0) * (1.0 / features)
    column = jnp.transpose(jnp.broadcast_to(inverse, total.shape))[:, :1]
    rows = branches[0].shape[0]
    for at in range(chunks):
        scale = column[at * rows : (at + 1) * rows]
        student_ref[at * rows : (at + 1) * rows, :] = (branches[at][...] * scale).astype(
            jnp.bfloat16
        )


def final(features, branches, stats):
    chunks, parts = len(branches), len(stats)
    part_rows, cols = branches[0].shape
    rows = part_rows * chunks
    return pl.pallas_call(
        functools.partial(final_kernel, features, chunks, parts),
        grid=(1,),
        in_specs=[whole((part_rows, cols))] * chunks + [whole((8, rows))] * parts,
        out_specs=[whole((rows, cols)), whole((1, rows))],
        out_shape=[
            jax.ShapeDtypeStruct((rows, cols), jnp.bfloat16),
            jax.ShapeDtypeStruct((1, rows), jnp.float32),
        ],
        compiler_params=params(16),
        cost_estimate=cost(2 * rows * cols, 6 * rows * cols),
        name="final",
    )(*branches, *stats)


def swap(x, mask):
    count = lax.axis_size("tp")
    return lax.ppermute(x, "tp", [(i, i ^ mask) for i in range(count)])


def send_up(x, first):
    count = lax.axis_size("ctx")
    return lax.ppermute(x, "ctx", [(i, i + 1) for i in range(first, count - 1)])


def after(x, *others):
    return lax.optimization_barrier((x,) + others)[0]


def gather(own, core_after=None, beside=None, middle=None):
    count = lax.axis_size("tp")
    got = {0: [own]}
    masks = [1 << b for b in range(1, count.bit_length() - 1)]
    if len(masks) >= 2:
        a, b = masks[0], masks[1]
        half = own.shape[0] // (2 * EXTRA) * EXTRA
        via_a, via_b = swap(own, a), swap(own, b)
        got[1] = [swap(own, 1)]
        if beside is not None:
            token = beside(got[1][0])
            via_a, via_b = after(via_a, token), after(via_b, token)
        got[a], got[b] = [via_a], [via_b]
        diagonal = [swap(via_a[:half], b), swap(via_b[half:], a)]
        if core_after is not None:
            diagonal = [after(p, core_after) for p in diagonal]
        got[a | 1], got[b | 1] = [swap(via_a, 1)], [swap(via_b, 1)]
        got[a | b] = diagonal
        if middle is not None:
            token = middle(got)
            diagonal = [after(p, token) for p in diagonal]
        got[a | b | 1] = [swap(p, 1) for p in diagonal]
        masks = masks[2:]
    elif count > 1:
        got[1] = [swap(own, 1)]
    for mask in masks:
        for m in list(got):
            got[m | mask] = [swap(p, mask) for p in got[m]]
    return [got[m] for m in range(count)]


def body(hidden_in, norm_gain, w_query, w_key, w_value, sign_bits, w_out, teacher):
    rows = hidden_in.shape[0]
    half = rows // HALVES
    tp_count = lax.axis_size("tp")
    ctx_count = lax.axis_size("ctx")
    features = hidden_in.shape[1] * tp_count
    tp_at = lax.axis_index("tp")
    ctx_at = jnp.reshape(lax.axis_index("ctx"), (1,)).astype(jnp.int32)
    masks = jnp.arange(tp_count, dtype=jnp.int32)
    order = tp_at ^ masks
    shared = tp_at & masks
    parity = jnp.zeros_like(shared)
    for bit in range(tp_count.bit_length()):
        parity = parity ^ (shared >> bit & 1)
    flips = (1 - 2 * parity).astype(jnp.float32)
    signs = (2 * sign_bits - 1).astype(jnp.float32)
    gain = norm_gain.reshape(-1, GROUP)

    clipped = pre(hidden_in, gain)

    kv_cols = w_key.shape[1]
    sharing = HD // kv_cols if kv_cols < HD else 1
    kv_heads = kv_cols * sharing // HD
    loaded = []

    def bring(token):
        first = after(w_query, token, order, ctx_at, flips, signs)
        loaded.extend(load(first, w_key, w_value, w_out))
        return loaded[1]

    early, state = [], []

    def begin(got):
        early.extend(sorted(got)[:-1])
        part = {m: got[m] for m in early}
        state.extend(proj(order, part, rows, (), False, *loaded[:3]))
        return state[-1]

    blocks = gather(clipped, beside=bring, middle=begin)
    if not loaded:
        bring(clipped)
    late = {m: block for m, block in enumerate(blocks) if m not in early}
    q, *kvs = proj(order, late, rows, state, True, *loaded[:3])
    for i, kv in enumerate(kvs):
        if sharing > 1:
            k, v = kv[:, :kv_cols], kv[:, kv_cols:]
            for bit in range(sharing.bit_length() - 1):
                upper = tp_at >> bit & 1 == 1
                k2, v2 = swap(k, 1 << bit), swap(v, 1 << bit)
                k, v = (
                    jnp.where(
                        upper,
                        jnp.concatenate([far, near], axis=1),
                        jnp.concatenate([near, far], axis=1),
                    )
                    for near, far in ((k, k2), (v, v2))
                )
            kv = jnp.concatenate([k, v], axis=1)
        kvs[i] = kv
    far, sent, states = [], kvs, []
    for hop in range(1, ctx_count):
        if hop == 3:
            sent = [after(kv, *[state[0] for state in states]) for kv in sent]
        sent = [send_up(kv, hop - 1) for kv in sent]
        far += [(hop, kv) for kv in sent]
        begun = far if ctx_count > 2 else []
        if hop == 1:
            states = [
                attend(ctx_at, q, at * half, half, kv_heads, kvs[: at + 1], begun, None, None)
                for at in range(HALVES)
            ]
    middle = far[HALVES:-HALVES]
    if middle:
        states = [
            attend(ctx_at, q, at * half, half, kv_heads, [], middle, states[at], None)
            for at in range(HALVES)
        ]
    q = after(q, *[state[0] for state in states])
    branches, stats = [], []
    for at in range(HALVES):
        signed = attend(
            ctx_at, q, at * half, half, kv_heads, [], far[-HALVES:], states[at], signs
        )
        blocks = gather(signed, branches[-1] if at else None)
        b, s = project_out(flips, blocks, loaded[3], teacher, at)
        branches.append(b)
        stats.append(s)
    stat = jnp.concatenate(stats, axis=1)
    if tp_count > 1:
        stat = stat + swap(stat, 1)
    totals = [stat] + [swap(stat, m) for m in range(2, tp_count, 2)]
    student, loss = final(features, branches, totals)
    return student, loss.reshape(rows)


def solution(mesh):
    in_specs = (
        P("ctx", "tp"),
        P("tp"),
        P(None, "tp"),
        P(None, "tp"),
        P(None, "tp"),
        P("tp", None),
        P(None, "tp"),
        P("ctx", "tp"),
    )
    out_specs = (P("ctx", "tp"), P("ctx"))
    return jax.shard_map(body, mesh=mesh, in_specs=in_specs, out_specs=out_specs, check_vma=False)
```

```python
import functools
import math

import jax
import jax.numpy as jnp
from jax import lax
from jax.experimental import pallas as pl
from jax.experimental.pallas import tpu as pltpu
from jax.sharding import PartitionSpec as P

HD = 128
GROUP = 128
EPS_IN = 1e-05
EPS_OUT = 1e-06
CLIP_RATIO = 0.9
FAR_BELOW = -1e30
LOG2E = math.log2(math.e)
HALVES = 2
EXTRA = 16
LOAD_PARTS = 4
LOAD_MIB = 34
PROJ_MIB = 14
ATT_MIB = 12
OUT_MIB = 12
MIB = 1024 * 1024


def params(mib, **kw):
    return pltpu.CompilerParams(vmem_limit_bytes=mib * MIB, **kw)


def whole(shape):
    zeros = (0,) * len(shape)
    return pl.BlockSpec(shape, lambda *_: zeros)


IN_SMEM = pl.BlockSpec(memory_space=pltpu.SMEM)
IN_VMEM = pl.BlockSpec(memory_space=pltpu.VMEM)
ANYWHERE = pl.BlockSpec(memory_space=pl.ANY)
IN_HBM = pl.BlockSpec(memory_space=pltpu.HBM)


def cost(flops, moved, trans=0):
    return pl.CostEstimate(flops=int(flops), bytes_accessed=int(moved), transcendentals=int(trans))


def clip_tile(v):
    limit = CLIP_RATIO * jnp.max(jnp.abs(v), axis=-1, keepdims=True)
    return jnp.clip(v, -limit, limit)


def pre_kernel(h_hbm, g_hbm, *refs):
    c_ref, h_all, g_ref, sem = refs
    rows, width = h_all.shape
    steps = sem.shape[0] - 1
    part = rows // steps
    copies = [pltpu.make_async_copy(g_hbm, g_ref, sem.at[steps])]
    for i in range(steps):
        at = slice(i * part, (i + 1) * part)
        copies.append(pltpu.make_async_copy(h_hbm.at[at], h_all.at[at], sem.at[i]))
    for copy in copies:
        copy.start()
    copies[0].wait()
    for i in range(steps):
        copies[i + 1].wait()
        total = jnp.zeros((part, GROUP), jnp.float32)
        row = i * part
        for at in range(0, width, GROUP):
            h = h_all[i * part : (i + 1) * part, at : at + GROUP].astype(jnp.float32)
            total = total + h * h
            v = h * g_ref[at // GROUP : at // GROUP + 1, :].astype(jnp.float32)
            c_ref[row : row + part, at : at + GROUP] = clip_tile(v).astype(jnp.bfloat16)
        sums = jnp.sum(total, axis=-1, keepdims=True)
        sums = jnp.transpose(jnp.broadcast_to(sums, (part, 128)))[:EXTRA]
        row = lax.broadcasted_iota(jnp.int32, sums.shape, 0)
        left = sums
        for place in range(3):
            piece = left.astype(jnp.bfloat16).astype(jnp.float32)
            left = left - piece
            sums = jnp.where(row == place, piece, sums)
        c_ref[rows:, i * part : (i + 1) * part] = sums.astype(jnp.bfloat16)


def pre(hidden, gain):
    rows, width = hidden.shape
    steps = 4
    return pl.pallas_call(
        pre_kernel,
        in_specs=[IN_HBM] * 2,
        out_specs=IN_VMEM,
        out_shape=pltpu.VMEM((rows + EXTRA, width), jnp.bfloat16),
        scratch_shapes=[
            pltpu.VMEM((rows, width), jnp.bfloat16),
            pltpu.VMEM(gain.shape, jnp.bfloat16),
            pltpu.SemaphoreType.DMA((steps + 1,)),
        ],
        compiler_params=params(62),
        cost_estimate=cost(8 * rows * width, 4 * rows * width),
        name="pre",
    )(hidden, gain)


def load_kernel(count, *refs):
    sources, goals, sem = refs[:count], refs[count : 2 * count], refs[-1]
    copies = []
    for i in range(count):
        depth = sources[i].shape[0] // LOAD_PARTS
        for p in range(LOAD_PARTS):
            at = slice(p * depth, (p + 1) * depth)
            copies.append(
                pltpu.make_async_copy(sources[i].at[at], goals[i].at[at], sem.at[i, p])
            )
    for copy in copies:
        copy.start()
    for copy in copies:
        copy.wait()


def load(*weights):
    count = len(weights)
    return pl.pallas_call(
        functools.partial(load_kernel, count),
        in_specs=[IN_HBM] * count,
        out_specs=[IN_VMEM] * count,
        out_shape=[pltpu.VMEM(w.shape, w.dtype) for w in weights],
        scratch_shapes=[pltpu.SemaphoreType.DMA((count, LOAD_PARTS))],
        compiler_params=params(LOAD_MIB),
        cost_estimate=cost(0, 2 * sum(w.size * 2 for w in weights)),
        name="load",
    )(*weights)


def proj_kernel(counts, masks, begins, ends, order_ref, *refs):
    depth = len(counts)
    blocks, refs = refs[: sum(counts)], refs[sum(counts) :]
    wq_ref, wk_ref, wv_ref, *refs = refs
    if not begins:
        *before, ss_in = refs[:4]
        refs = refs[4:]
        squares = ss_in[0:1, :]
    else:
        before = [None] * 3
        squares = jnp.zeros((1, ss_rows(blocks)), jnp.float32)
    if ends:
        q_ref, *kv_refs = refs[: 1 + HALVES]
        accs = refs[1 + HALVES :]
    else:
        *accs, ss_ref = refs
    nk = wk_ref.shape[1]
    k_rows = blocks[0].shape[1]
    at_block = 0
    for k in range(depth):
        at = pl.ds(pl.multiple_of(order_ref[masks[k]] * k_rows, k_rows), k_rows)
        mine = [b[...] for b in blocks[at_block : at_block + counts[k]]]
        at_block += counts[k]
        body_rows = mine[-1].shape[0] - EXTRA
        tail = mine[-1][body_rows:, : squares.shape[1]].astype(jnp.float32)
        squares = squares + (tail[0:1] + tail[1:2] + tail[2:3])
        mine[-1] = mine[-1][:body_rows]
        left = mine[0] if len(mine) == 1 else jnp.concatenate(mine, axis=0)
        wq, wk, wv = wq_ref[at, :], wk_ref[at, :], wv_ref[at, :]
        if nk % 128 == 0:
            both = jnp.dot(
                left, jnp.concatenate([wk, wv], axis=1), preferred_element_type=jnp.float32
            )
            parts = (both[:, :nk], both[:, nk:])
        else:
            parts = [jnp.dot(left, w, preferred_element_type=jnp.float32) for w in (wk, wv)]
        first = jnp.dot(left, wq, preferred_element_type=jnp.float32)
        for part, acc, old in zip((first, *parts), accs, before):
            if k:
                acc[...] += part
            elif not begins:
                acc[...] = old[...] + part
            else:
                acc[...] = part

    if not ends:
        ss_ref[...] = jnp.broadcast_to(squares, ss_ref.shape)
    else:
        accq, acck, accv = accs
        features = wq_ref.shape[0]
        squares = jnp.broadcast_to(squares, (8, squares.shape[1]))
        inverse = lax.rsqrt(squares * (1.0 / features) + EPS_IN)
        scale = jnp.transpose(inverse)[:, :1]
        q_ref[...] = (accq[...] * scale).astype(jnp.bfloat16)
        rows = kv_refs[0].shape[0]
        for i, kv_ref in enumerate(kv_refs):
            at = slice(i * rows, (i + 1) * rows)
            kv_ref[:, :nk] = (acck[at, :] * scale[at]).astype(jnp.bfloat16)
            kv_ref[:, nk:] = (accv[at, :] * scale[at]).astype(jnp.bfloat16)


def ss_rows(blocks):
    return blocks[0].shape[0] - EXTRA


def proj(order, blocks, rows, state, ends, wq, wk, wv):
    masks = sorted(blocks)
    blocks = [blocks[m] for m in masks]
    depth = len(blocks)
    counts = [len(b) for b in blocks]
    part_cols = blocks[0][0].shape[1]
    sizes = wq.shape[1], wk.shape[1], wv.shape[1]
    n = sum(sizes)
    flat = [p for b in blocks for p in b]
    args = [order, *flat, wq, wk, wv, *state]
    if ends:
        out_shape = [
            jax.ShapeDtypeStruct((rows, sizes[0]), jnp.bfloat16),
        ] + [
            jax.ShapeDtypeStruct((rows // HALVES, sizes[1] + sizes[2]), jnp.bfloat16)
            for _ in range(HALVES)
        ]
        scratch = [pltpu.VMEM((rows, m), jnp.float32) for m in sizes]
    else:
        out_shape = [pltpu.VMEM((rows, m), jnp.float32) for m in sizes]
        out_shape.append(jax.ShapeDtypeStruct((8, rows), jnp.float32))
        scratch = []
    return pl.pallas_call(
        functools.partial(proj_kernel, counts, masks, not state, ends),
        in_specs=[IN_SMEM] + [IN_VMEM] * (len(args) - 1),
        out_specs=[IN_VMEM] * len(out_shape),
        out_shape=out_shape,
        scratch_shapes=scratch,
        compiler_params=params(PROJ_MIB),
        cost_estimate=cost(
            2 * rows * part_cols * depth * n, 2 * part_cols * depth * (rows + n)
        ),
        name="proj",
    )(*args)


def att_kernel(first, kv_heads, near, far, begins, ends, me_ref, q_ref, *refs):
    count = near + len(far)
    kvs, refs = refs[:count], refs[count:]
    if not begins:
        high_in, total_in, accum_in, *refs = refs
    if ends:
        sign_ref, o_ref, high, total, accum = refs
    else:
        high, total, accum = refs
    rows = accum.shape[2]
    heads = q_ref.shape[1] // HD
    part = kvs[0].shape[0]
    group = heads // kv_heads
    scale = HD ** (-0.5) * LOG2E

    if not begins:
        high[...] = high_in[...]
        total[...] = total_in[...]
        accum[...] = accum_in[...]

    def visit(kv_ref, sub, start, fresh):
        keys = slice(sub * part, (sub + 1) * part)
        masked = start is not None and start + part > first
        scores, turned = [], []
        for kv in range(kv_heads):
            at = (kv_heads + kv) * HD
            turned.append(jnp.transpose(kv_ref[keys, at : at + HD]))
        for head in range(heads):
            kv = head // group
            q = q_ref[first : first + rows, head * HD : (head + 1) * HD]
            k = kv_ref[keys, kv * HD : (kv + 1) * HD]
            s = lax.dot_general(
                k, q, (((1,), (1,)), ((), ())), preferred_element_type=jnp.float32
            )
            if masked:
                kpos = start + lax.broadcasted_iota(jnp.int32, s.shape, 0)
                qpos = first + lax.broadcasted_iota(jnp.int32, s.shape, 1)
                s = jnp.where(kpos <= qpos, s, FAR_BELOW)
            scores.append(s)
        for head in range(heads):
            s = scores[head]
            best = jnp.max(s, axis=0, keepdims=True)
            if not fresh:
                before = high[head : head + 1]
                best = jnp.maximum(best, before)
            w = jnp.exp2((s - best) * scale)
            sums = jnp.sum(w, axis=0, keepdims=True)
            mixed = jnp.dot(
                turned[head // group], w.astype(jnp.bfloat16), preferred_element_type=jnp.float32
            )
            if fresh:
                total[head : head + 1] = sums
                accum[head] = mixed
            else:
                decay = jnp.exp2((before - best) * scale)
                total[head : head + 1] = total[head : head + 1] * decay + sums
                accum[head] = accum[head] * decay + mixed
            high[head : head + 1] = best

    for at in range(near):
        visit(kvs[at], 0, at * part, begins and at == 0)
    for at, hop in enumerate(far):

        @pl.when(me_ref[0] >= hop)
        def _():
            visit(kvs[near + at], 0, None, False)

    if ends:
        for head in range(heads):
            att = jnp.transpose(accum[head] / total[head : head + 1])
            att = att.astype(jnp.bfloat16).astype(jnp.float32)
            o_ref[:, head * HD : (head + 1) * HD] = (att * sign_ref[head : head + 1, :]).astype(
                jnp.bfloat16
            )


def attend(me, q, first, rows, kv_heads, near, far, state, signs):
    heads = q.shape[1] // HD
    kvs = near + [kv for _, kv in far]
    keys = sum(kv.shape[0] for kv in kvs)
    shapes = [(max(heads, 8), rows), (max(heads, 8), rows), (heads, HD, rows)]
    args = [me, q, *kvs]
    if state is not None:
        args += list(state)
    if signs is None:
        out_shape = [jax.ShapeDtypeStruct(shape, jnp.float32) for shape in shapes]
        scratch = []
    else:
        args.append(signs)
        out_shape = jax.ShapeDtypeStruct((rows, heads * HD), jnp.bfloat16)
        scratch = [pltpu.VMEM(shape, jnp.float32) for shape in shapes]
    far_at = [n for n, _ in far]
    kernel = functools.partial(
        att_kernel, first, kv_heads, len(near), far_at, state is None, signs is not None
    )
    return pl.pallas_call(
        kernel,
        in_specs=[IN_SMEM] + [IN_VMEM] * (len(args) - 1),
        out_specs=IN_VMEM if signs is not None else [IN_VMEM] * 3,
        out_shape=out_shape,
        scratch_shapes=scratch,
        compiler_params=params(ATT_MIB),
        cost_estimate=cost(4 * rows * keys * heads * HD, 4 * keys * HD, rows * keys * heads),
        name="attend",
    )(*args)


def butterfly(tiles):
    count = len(tiles)
    span = 1
    while span < count:
        out = list(tiles)
        for at in range(count):
            if not at & span:
                a, b = tiles[at], tiles[at | span]
                out[at], out[at | span] = a + b, a - b
        tiles = out
        span *= 2
    return tiles


def out_kernel(counts, steps, chunk, sign_ref, t_ref, *refs):
    parts = len(counts)
    blocks, at_block = [], 0
    for n in counts:
        blocks.append(refs[at_block : at_block + n])
        at_block += n
    w_ref, b_ref, s_ref, mid, rot, acc = refs[at_block:]
    rows = b_ref.shape[0]
    width = blocks[0][0].shape[1]
    here = width // HD
    heads = here * parts
    factor = heads ** (-0.5)

    strip = 16
    most = max(counts)
    span = rows // most
    for section in range(most):

        def turn(i, carry):
            at = pl.multiple_of(section * span + i * strip, strip)
            for m in range(parts):
                if len(blocks[m]) == 1:
                    ref, start = blocks[m][0], at
                else:
                    ref, start = blocks[m][section], pl.multiple_of(i * strip, strip)
                tiles = [
                    ref[pl.ds(start, strip), h * HD : (h + 1) * HD].astype(jnp.float32)
                    for h in range(here)
                ]
                for h, v in enumerate(butterfly(tiles)):
                    mid[m * here + h] = v
            for h in range(here):
                tiles = butterfly([mid[m * here + h] for m in range(parts)])
                for m in range(parts):
                    v = tiles[m] * (factor * sign_ref[m])
                    col = (m * here + h) * HD
                    rot[pl.ds(at, strip), col : col + HD] = clip_tile(v).astype(jnp.bfloat16)
            return carry

        lax.fori_loop(0, span // strip, turn, 0)

    depth = w_ref.shape[0] // steps
    for i in range(steps):
        part = jnp.dot(
            rot[:, i * depth : (i + 1) * depth],
            w_ref[i * depth : (i + 1) * depth, :],
            preferred_element_type=jnp.float32,
        )
        if i == 0:
            acc[...] = part
        else:
            acc[...] += part

    b = acc[...]
    t = t_ref[chunk * rows : (chunk + 1) * rows, :].astype(jnp.float32)
    b_ref[...] = b
    sums = [jnp.sum(v, axis=-1, keepdims=True) for v in (b * b, b * t, t * t)]
    lane = lax.broadcasted_iota(jnp.int32, (rows, 128), 1)
    wide = jnp.where(lane == 0, sums[0], jnp.where(lane == 1, sums[1], sums[2]))
    s_ref[...] = jnp.transpose(wide)[:8]


def project_out(flips, blocks, w_out, teacher, chunk):
    parts = len(blocks)
    counts = [len(b) for b in blocks]
    rows, width = blocks[0][0].shape
    depth, cols = w_out.shape
    steps = 4
    flat = [p for b in blocks for p in b]
    return pl.pallas_call(
        functools.partial(out_kernel, counts, steps, chunk),
        in_specs=[IN_SMEM] + [IN_VMEM] * (len(flat) + 2),
        out_specs=[IN_VMEM, IN_VMEM],
        out_shape=[
            jax.ShapeDtypeStruct((rows, cols), jnp.float32),
            jax.ShapeDtypeStruct((8, rows), jnp.float32),
        ],
        scratch_shapes=[
            pltpu.VMEM((parts * width // HD, 16, HD), jnp.float32),
            pltpu.VMEM((rows, depth), jnp.bfloat16),
            pltpu.VMEM((rows, cols), jnp.float32),
        ],
        compiler_params=params(OUT_MIB),
        cost_estimate=cost(2 * rows * depth * cols, 2 * depth * (rows + cols) + 6 * rows * cols),
        name="project_out",
    )(flips, teacher, *flat, w_out)


def final_kernel(features, chunks, parts, *refs):
    branches, stats = refs[:chunks], refs[chunks : chunks + parts]
    student_ref, loss_ref = refs[chunks + parts :]
    sums = [stat[...] for stat in stats]
    while len(sums) > 1:
        sums = [x + y for x, y in zip(sums[::2], sums[1::2])]
    total = sums[0]
    inverse = lax.rsqrt(total[0:1] * (1.0 / features) + EPS_OUT)
    loss = inverse * inverse * total[0:1] - 2.0 * inverse * total[1:2] + total[2:3]
    loss_ref[...] = jnp.maximum(loss, 0.0) * (1.0 / features)
    column = jnp.transpose(jnp.broadcast_to(inverse, total.shape))[:, :1]
    rows = branches[0].shape[0]
    for at in range(chunks):
        scale = column[at * rows : (at + 1) * rows]
        student_ref[at * rows : (at + 1) * rows, :] = (branches[at][...] * scale).astype(
            jnp.bfloat16
        )


def final(features, branches, stats):
    chunks, parts = len(branches), len(stats)
    part_rows, cols = branches[0].shape
    rows = part_rows * chunks
    return pl.pallas_call(
        functools.partial(final_kernel, features, chunks, parts),
        grid=(1,),
        in_specs=[whole((part_rows, cols))] * chunks + [whole((8, rows))] * parts,
        out_specs=[whole((rows, cols)), whole((1, rows))],
        out_shape=[
            jax.ShapeDtypeStruct((rows, cols), jnp.bfloat16),
            jax.ShapeDtypeStruct((1, rows), jnp.float32),
        ],
        compiler_params=params(16),
        cost_estimate=cost(2 * rows * cols, 6 * rows * cols),
        name="final",
    )(*branches, *stats)


def swap(x, mask):
    count = lax.axis_size("tp")
    return lax.ppermute(x, "tp", [(i, i ^ mask) for i in range(count)])


def send_up(x, first):
    count = lax.axis_size("ctx")
    return lax.ppermute(x, "ctx", [(i, i + 1) for i in range(first, count - 1)])


def after(x, *others):
    return lax.optimization_barrier((x,) + others)[0]


def gather(own, core_after=None, beside=None, middle=None):
    count = lax.axis_size("tp")
    got = {0: [own]}
    masks = [1 << b for b in range(1, count.bit_length() - 1)]
    if len(masks) >= 2:
        a, b = masks[0], masks[1]
        half = own.shape[0] // (2 * EXTRA) * EXTRA
        via_a, via_b = swap(own, a), swap(own, b)
        got[1] = [swap(own, 1)]
        if beside is not None:
            token = beside(got[1][0])
            via_a, via_b = after(via_a, token), after(via_b, token)
        got[a], got[b] = [via_a], [via_b]
        diagonal = [swap(via_a[:half], b), swap(via_b[half:], a)]
        if core_after is not None:
            diagonal = [after(p, core_after) for p in diagonal]
        got[a | 1], got[b | 1] = [swap(via_a, 1)], [swap(via_b, 1)]
        got[a | b] = diagonal
        if middle is not None:
            token = middle(got)
            diagonal = [after(p, token) for p in diagonal]
        got[a | b | 1] = [swap(p, 1) for p in diagonal]
        masks = masks[2:]
    elif count > 1:
        got[1] = [swap(own, 1)]
    for mask in masks:
        for m in list(got):
            got[m | mask] = [swap(p, mask) for p in got[m]]
    return [got[m] for m in range(count)]


def body(hidden_in, norm_gain, w_query, w_key, w_value, sign_bits, w_out, teacher):
    rows = hidden_in.shape[0]
    half = rows // HALVES
    tp_count = lax.axis_size("tp")
    ctx_count = lax.axis_size("ctx")
    features = hidden_in.shape[1] * tp_count
    tp_at = lax.axis_index("tp")
    ctx_at = jnp.reshape(lax.axis_index("ctx"), (1,)).astype(jnp.int32)
    masks = jnp.arange(tp_count, dtype=jnp.int32)
    order = tp_at ^ masks
    shared = tp_at & masks
    parity = jnp.zeros_like(shared)
    for bit in range(tp_count.bit_length()):
        parity = parity ^ (shared >> bit & 1)
    flips = (1 - 2 * parity).astype(jnp.float32)
    signs = (2 * sign_bits - 1).astype(jnp.float32)
    gain = norm_gain.reshape(-1, GROUP)

    clipped = pre(hidden_in, gain)

    kv_cols = w_key.shape[1]
    sharing = HD // kv_cols if kv_cols < HD else 1
    kv_heads = kv_cols * sharing // HD
    loaded = []

    def bring(token):
        first = after(w_query, token, order, ctx_at, flips, signs)
        loaded.extend(load(first, w_key, w_value, w_out))
        return loaded[1]

    early, state = [], []

    def begin(got):
        early.extend(sorted(got)[:-1])
        part = {m: got[m] for m in early}
        state.extend(proj(order, part, rows, (), False, *loaded[:3]))
        return state[-1]

    blocks = gather(clipped, beside=bring, middle=begin)
    if not loaded:
        bring(clipped)
    late = {m: block for m, block in enumerate(blocks) if m not in early}
    q, *kvs = proj(order, late, rows, state, True, *loaded[:3])
    for i, kv in enumerate(kvs):
        if sharing > 1:
            k, v = kv[:, :kv_cols], kv[:, kv_cols:]
            for bit in range(sharing.bit_length() - 1):
                upper = tp_at >> bit & 1 == 1
                k2, v2 = swap(k, 1 << bit), swap(v, 1 << bit)
                k, v = (
                    jnp.where(
                        upper,
                        jnp.concatenate([far, near], axis=1),
                        jnp.concatenate([near, far], axis=1),
                    )
                    for near, far in ((k, k2), (v, v2))
                )
            kv = jnp.concatenate([k, v], axis=1)
        kvs[i] = kv
    far, sent, states = [], kvs, []
    for hop in range(1, ctx_count):
        if hop == 3:
            sent = [after(kv, *[state[0] for state in states]) for kv in sent]
        sent = [send_up(kv, hop - 1) for kv in sent]
        far += [(hop, kv) for kv in sent]
        begun = far if ctx_count > 2 else []
        if hop == 1:
            states = [
                attend(ctx_at, q, at * half, half, kv_heads, kvs[: at + 1], begun, None, None)
                for at in range(HALVES)
            ]
    middle = far[HALVES:-HALVES]
    if middle:
        states = [
            attend(ctx_at, q, at * half, half, kv_heads, [], middle, states[at], None)
            for at in range(HALVES)
        ]
    q = after(q, *[state[0] for state in states])
    branches, stats = [], []
    for at in range(HALVES):
        signed = attend(
            ctx_at, q, at * half, half, kv_heads, [], far[-HALVES:], states[at], signs
        )
        blocks = gather(signed, branches[-1] if at else None)
        b, s = project_out(flips, blocks, loaded[3], teacher, at)
        branches.append(b)
        stats.append(s)
    stat = jnp.concatenate(stats, axis=1)
    if tp_count > 1:
        stat = stat + swap(stat, 1)
    totals = [stat] + [swap(stat, m) for m in range(2, tp_count, 2)]
    student, loss = final(features, branches, totals)
    return student, loss.reshape(rows)


def solution(mesh):
    in_specs = (
        P("ctx", "tp"),
        P("tp"),
        P(None, "tp"),
        P(None, "tp"),
        P(None, "tp"),
        P("tp", None),
        P(None, "tp"),
        P("ctx", "tp"),
    )
    out_specs = (P("ctx", "tp"), P("ctx"))
    return jax.shard_map(body, mesh=mesh, in_specs=in_specs, out_specs=out_specs, check_vma=False)
```

```python
import functools
import math

import jax
import jax.numpy as jnp
from jax import lax
from jax.experimental import pallas as pl
from jax.experimental.pallas import tpu as pltpu
from jax.sharding import PartitionSpec as P

HD = 128
GROUP = 128
EPS_IN = 1e-05
EPS_OUT = 1e-06
CLIP_RATIO = 0.9
FAR_BELOW = -1e30
LOG2E = math.log2(math.e)
HALVES = 2
EXTRA = 16
LOAD_PARTS = 4
LOAD_MIB = 38
PROJ_MIB = 14
ATT_MIB = 12
OUT_MIB = 12
MIB = 1024 * 1024


def params(mib, **kw):
    return pltpu.CompilerParams(vmem_limit_bytes=mib * MIB, **kw)


def whole(shape):
    zeros = (0,) * len(shape)
    return pl.BlockSpec(shape, lambda *_: zeros)


IN_SMEM = pl.BlockSpec(memory_space=pltpu.SMEM)
IN_VMEM = pl.BlockSpec(memory_space=pltpu.VMEM)
ANYWHERE = pl.BlockSpec(memory_space=pl.ANY)
IN_HBM = pl.BlockSpec(memory_space=pltpu.HBM)


def cost(flops, moved, trans=0):
    return pl.CostEstimate(flops=int(flops), bytes_accessed=int(moved), transcendentals=int(trans))


def clip_tile(v):
    limit = CLIP_RATIO * jnp.max(jnp.abs(v), axis=-1, keepdims=True)
    return jnp.clip(v, -limit, limit)


def pre_kernel(h_hbm, g_hbm, *refs):
    c_ref, h_all, g_ref, sem = refs
    rows, width = h_all.shape
    steps = sem.shape[0] - 1
    part = rows // steps
    copies = [pltpu.make_async_copy(g_hbm, g_ref, sem.at[steps])]
    for i in range(steps):
        at = slice(i * part, (i + 1) * part)
        copies.append(pltpu.make_async_copy(h_hbm.at[at], h_all.at[at], sem.at[i]))
    for copy in copies:
        copy.start()
    copies[0].wait()
    for i in range(steps):
        copies[i + 1].wait()
        total = jnp.zeros((part, GROUP), jnp.float32)
        row = i * part
        for at in range(0, width, GROUP):
            h = h_all[i * part : (i + 1) * part, at : at + GROUP].astype(jnp.float32)
            total = total + h * h
            v = h * g_ref[at // GROUP : at // GROUP + 1, :].astype(jnp.float32)
            c_ref[row : row + part, at : at + GROUP] = clip_tile(v).astype(jnp.bfloat16)
        sums = jnp.sum(total, axis=-1, keepdims=True)
        sums = jnp.transpose(jnp.broadcast_to(sums, (part, 128)))[:EXTRA]
        row = lax.broadcasted_iota(jnp.int32, sums.shape, 0)
        left = sums
        for place in range(3):
            piece = left.astype(jnp.bfloat16).astype(jnp.float32)
            left = left - piece
            sums = jnp.where(row == place, piece, sums)
        c_ref[rows:, i * part : (i + 1) * part] = sums.astype(jnp.bfloat16)


def pre(hidden, gain):
    rows, width = hidden.shape
    steps = 4
    return pl.pallas_call(
        pre_kernel,
        in_specs=[IN_HBM] * 2,
        out_specs=IN_VMEM,
        out_shape=pltpu.VMEM((rows + EXTRA, width), jnp.bfloat16),
        scratch_shapes=[
            pltpu.VMEM((rows, width), jnp.bfloat16),
            pltpu.VMEM(gain.shape, jnp.bfloat16),
            pltpu.SemaphoreType.DMA((steps + 1,)),
        ],
        compiler_params=params(62),
        cost_estimate=cost(8 * rows * width, 4 * rows * width),
        name="pre",
    )(hidden, gain)


def load_kernel(count, *refs):
    sources, goals, sem = refs[:count], refs[count : 2 * count], refs[-1]
    copies = []
    for i in range(count):
        depth = sources[i].shape[0] // LOAD_PARTS
        for p in range(LOAD_PARTS):
            at = slice(p * depth, (p + 1) * depth)
            copies.append(
                pltpu.make_async_copy(sources[i].at[at], goals[i].at[at], sem.at[i, p])
            )
    for copy in copies:
        copy.start()
    for copy in copies:
        copy.wait()


def load(*weights):
    count = len(weights)
    return pl.pallas_call(
        functools.partial(load_kernel, count),
        in_specs=[IN_HBM] * count,
        out_specs=[IN_VMEM] * count,
        out_shape=[pltpu.VMEM(w.shape, w.dtype) for w in weights],
        scratch_shapes=[pltpu.SemaphoreType.DMA((count, LOAD_PARTS))],
        compiler_params=params(LOAD_MIB),
        cost_estimate=cost(0, 2 * sum(w.size * 2 for w in weights)),
        name="load",
    )(*weights)


def proj_kernel(counts, masks, begins, ends, order_ref, *refs):
    depth = len(counts)
    blocks, refs = refs[: sum(counts)], refs[sum(counts) :]
    wq_ref, wk_ref, wv_ref, *refs = refs
    if not begins:
        *before, ss_in = refs[:4]
        refs = refs[4:]
        squares = ss_in[0:1, :]
    else:
        before = [None] * 3
        squares = jnp.zeros((1, ss_rows(blocks)), jnp.float32)
    if ends:
        q_ref, *kv_refs = refs[: 1 + HALVES]
        accs = refs[1 + HALVES :]
    else:
        *accs, ss_ref = refs
    nk = wk_ref.shape[1]
    k_rows = blocks[0].shape[1]
    at_block = 0
    for k in range(depth):
        at = pl.ds(pl.multiple_of(order_ref[masks[k]] * k_rows, k_rows), k_rows)
        mine = [b[...] for b in blocks[at_block : at_block + counts[k]]]
        at_block += counts[k]
        body_rows = mine[-1].shape[0] - EXTRA
        tail = mine[-1][body_rows:, : squares.shape[1]].astype(jnp.float32)
        squares = squares + (tail[0:1] + tail[1:2] + tail[2:3])
        mine[-1] = mine[-1][:body_rows]
        left = mine[0] if len(mine) == 1 else jnp.concatenate(mine, axis=0)
        wq, wk, wv = wq_ref[at, :], wk_ref[at, :], wv_ref[at, :]
        if nk % 128 == 0:
            both = jnp.dot(
                left, jnp.concatenate([wk, wv], axis=1), preferred_element_type=jnp.float32
            )
            parts = (both[:, :nk], both[:, nk:])
        else:
            parts = [jnp.dot(left, w, preferred_element_type=jnp.float32) for w in (wk, wv)]
        first = jnp.dot(left, wq, preferred_element_type=jnp.float32)
        for part, acc, old in zip((first, *parts), accs, before):
            if k:
                acc[...] += part
            elif not begins:
                acc[...] = old[...] + part
            else:
                acc[...] = part

    if not ends:
        ss_ref[...] = jnp.broadcast_to(squares, ss_ref.shape)
    else:
        accq, acck, accv = accs
        features = wq_ref.shape[0]
        squares = jnp.broadcast_to(squares, (8, squares.shape[1]))
        inverse = lax.rsqrt(squares * (1.0 / features) + EPS_IN)
        scale = jnp.transpose(inverse)[:, :1]
        q_ref[...] = (accq[...] * scale).astype(jnp.bfloat16)
        rows = kv_refs[0].shape[0]
        for i, kv_ref in enumerate(kv_refs):
            at = slice(i * rows, (i + 1) * rows)
            kv_ref[:, :nk] = (acck[at, :] * scale[at]).astype(jnp.bfloat16)
            kv_ref[:, nk:] = (accv[at, :] * scale[at]).astype(jnp.bfloat16)


def ss_rows(blocks):
    return blocks[0].shape[0] - EXTRA


def proj(order, blocks, rows, state, ends, wq, wk, wv):
    masks = sorted(blocks)
    blocks = [blocks[m] for m in masks]
    depth = len(blocks)
    counts = [len(b) for b in blocks]
    part_cols = blocks[0][0].shape[1]
    sizes = wq.shape[1], wk.shape[1], wv.shape[1]
    n = sum(sizes)
    flat = [p for b in blocks for p in b]
    args = [order, *flat, wq, wk, wv, *state]
    if ends:
        out_shape = [
            jax.ShapeDtypeStruct((rows, sizes[0]), jnp.bfloat16),
        ] + [
            jax.ShapeDtypeStruct((rows // HALVES, sizes[1] + sizes[2]), jnp.bfloat16)
            for _ in range(HALVES)
        ]
        scratch = [pltpu.VMEM((rows, m), jnp.float32) for m in sizes]
    else:
        out_shape = [pltpu.VMEM((rows, m), jnp.float32) for m in sizes]
        out_shape.append(jax.ShapeDtypeStruct((8, rows), jnp.float32))
        scratch = []
    return pl.pallas_call(
        functools.partial(proj_kernel, counts, masks, not state, ends),
        in_specs=[IN_SMEM] + [IN_VMEM] * (len(args) - 1),
        out_specs=[IN_VMEM] * len(out_shape),
        out_shape=out_shape,
        scratch_shapes=scratch,
        compiler_params=params(PROJ_MIB),
        cost_estimate=cost(
            2 * rows * part_cols * depth * n, 2 * part_cols * depth * (rows + n)
        ),
        name="proj",
    )(*args)


def att_kernel(first, kv_heads, near, far, begins, ends, me_ref, q_ref, *refs):
    count = near + len(far)
    kvs, refs = refs[:count], refs[count:]
    if not begins:
        high_in, total_in, accum_in, *refs = refs
    if ends:
        sign_ref, o_ref, high, total, accum = refs
    else:
        high, total, accum = refs
    rows = accum.shape[2]
    heads = q_ref.shape[1] // HD
    part = kvs[0].shape[0]
    group = heads // kv_heads
    scale = HD ** (-0.5) * LOG2E

    if not begins:
        high[...] = high_in[...]
        total[...] = total_in[...]
        accum[...] = accum_in[...]

    def visit(kv_ref, sub, start, fresh):
        keys = slice(sub * part, (sub + 1) * part)
        masked = start is not None and start + part > first
        scores, turned = [], []
        for kv in range(kv_heads):
            at = (kv_heads + kv) * HD
            turned.append(jnp.transpose(kv_ref[keys, at : at + HD]))
        for head in range(heads):
            kv = head // group
            q = q_ref[first : first + rows, head * HD : (head + 1) * HD]
            k = kv_ref[keys, kv * HD : (kv + 1) * HD]
            s = lax.dot_general(
                k, q, (((1,), (1,)), ((), ())), preferred_element_type=jnp.float32
            )
            if masked:
                kpos = start + lax.broadcasted_iota(jnp.int32, s.shape, 0)
                qpos = first + lax.broadcasted_iota(jnp.int32, s.shape, 1)
                s = jnp.where(kpos <= qpos, s, FAR_BELOW)
            scores.append(s)
        for head in range(heads):
            s = scores[head]
            best = jnp.max(s, axis=0, keepdims=True)
            if not fresh:
                before = high[head : head + 1]
                best = jnp.maximum(best, before)
            w = jnp.exp2((s - best) * scale)
            sums = jnp.sum(w, axis=0, keepdims=True)
            mixed = jnp.dot(
                turned[head // group], w.astype(jnp.bfloat16), preferred_element_type=jnp.float32
            )
            if fresh:
                total[head : head + 1] = sums
                accum[head] = mixed
            else:
                decay = jnp.exp2((before - best) * scale)
                total[head : head + 1] = total[head : head + 1] * decay + sums
                accum[head] = accum[head] * decay + mixed
            high[head : head + 1] = best

    for at in range(near):
        visit(kvs[at], 0, at * part, begins and at == 0)
    for at, hop in enumerate(far):

        @pl.when(me_ref[0] >= hop)
        def _():
            visit(kvs[near + at], 0, None, False)

    if ends:
        for head in range(heads):
            att = jnp.transpose(accum[head] / total[head : head + 1])
            att = att.astype(jnp.bfloat16).astype(jnp.float32)
            o_ref[:, head * HD : (head + 1) * HD] = (att * sign_ref[head : head + 1, :]).astype(
                jnp.bfloat16
            )


def attend(me, q, first, rows, kv_heads, near, far, state, signs):
    heads = q.shape[1] // HD
    kvs = near + [kv for _, kv in far]
    keys = sum(kv.shape[0] for kv in kvs)
    shapes = [(max(heads, 8), rows), (max(heads, 8), rows), (heads, HD, rows)]
    args = [me, q, *kvs]
    if state is not None:
        args += list(state)
    if signs is None:
        out_shape = [jax.ShapeDtypeStruct(shape, jnp.float32) for shape in shapes]
        scratch = []
    else:
        args.append(signs)
        out_shape = jax.ShapeDtypeStruct((rows, heads * HD), jnp.bfloat16)
        scratch = [pltpu.VMEM(shape, jnp.float32) for shape in shapes]
    far_at = [n for n, _ in far]
    kernel = functools.partial(
        att_kernel, first, kv_heads, len(near), far_at, state is None, signs is not None
    )
    return pl.pallas_call(
        kernel,
        in_specs=[IN_SMEM] + [IN_VMEM] * (len(args) - 1),
        out_specs=IN_VMEM if signs is not None else [IN_VMEM] * 3,
        out_shape=out_shape,
        scratch_shapes=scratch,
        compiler_params=params(ATT_MIB),
        cost_estimate=cost(4 * rows * keys * heads * HD, 4 * keys * HD, rows * keys * heads),
        name="attend",
    )(*args)


def butterfly(tiles):
    count = len(tiles)
    span = 1
    while span < count:
        out = list(tiles)
        for at in range(count):
            if not at & span:
                a, b = tiles[at], tiles[at | span]
                out[at], out[at | span] = a + b, a - b
        tiles = out
        span *= 2
    return tiles


def out_kernel(counts, steps, chunk, sign_ref, t_ref, *refs):
    parts = len(counts)
    blocks, at_block = [], 0
    for n in counts:
        blocks.append(refs[at_block : at_block + n])
        at_block += n
    w_ref, b_ref, s_ref, mid, rot, acc = refs[at_block:]
    rows = b_ref.shape[0]
    width = blocks[0][0].shape[1]
    here = width // HD
    heads = here * parts
    factor = heads ** (-0.5)

    strip = 16
    most = max(counts)
    span = rows // most
    for section in range(most):

        def turn(i, carry):
            at = pl.multiple_of(section * span + i * strip, strip)
            for m in range(parts):
                if len(blocks[m]) == 1:
                    ref, start = blocks[m][0], at
                else:
                    ref, start = blocks[m][section], pl.multiple_of(i * strip, strip)
                tiles = [
                    ref[pl.ds(start, strip), h * HD : (h + 1) * HD].astype(jnp.float32)
                    for h in range(here)
                ]
                for h, v in enumerate(butterfly(tiles)):
                    mid[m * here + h] = v
            for h in range(here):
                tiles = butterfly([mid[m * here + h] for m in range(parts)])
                for m in range(parts):
                    v = tiles[m] * (factor * sign_ref[m])
                    col = (m * here + h) * HD
                    rot[pl.ds(at, strip), col : col + HD] = clip_tile(v).astype(jnp.bfloat16)
            return carry

        lax.fori_loop(0, span // strip, turn, 0)

    depth = w_ref.shape[0] // steps
    for i in range(steps):
        part = jnp.dot(
            rot[:, i * depth : (i + 1) * depth],
            w_ref[i * depth : (i + 1) * depth, :],
            preferred_element_type=jnp.float32,
        )
        if i == 0:
            acc[...] = part
        else:
            acc[...] += part

    b = acc[...]
    t = t_ref[chunk * rows : (chunk + 1) * rows, :].astype(jnp.float32)
    b_ref[...] = b
    sums = [jnp.sum(v, axis=-1, keepdims=True) for v in (b * b, b * t, t * t)]
    lane = lax.broadcasted_iota(jnp.int32, (rows, 128), 1)
    wide = jnp.where(lane == 0, sums[0], jnp.where(lane == 1, sums[1], sums[2]))
    s_ref[...] = jnp.transpose(wide)[:8]


def project_out(flips, blocks, w_out, teacher, chunk):
    parts = len(blocks)
    counts = [len(b) for b in blocks]
    rows, width = blocks[0][0].shape
    depth, cols = w_out.shape
    steps = 4
    flat = [p for b in blocks for p in b]
    return pl.pallas_call(
        functools.partial(out_kernel, counts, steps, chunk),
        in_specs=[IN_SMEM] + [IN_VMEM] * (len(flat) + 2),
        out_specs=[IN_VMEM, IN_VMEM],
        out_shape=[
            jax.ShapeDtypeStruct((rows, cols), jnp.float32),
            jax.ShapeDtypeStruct((8, rows), jnp.float32),
        ],
        scratch_shapes=[
            pltpu.VMEM((parts * width // HD, 16, HD), jnp.float32),
            pltpu.VMEM((rows, depth), jnp.bfloat16),
            pltpu.VMEM((rows, cols), jnp.float32),
        ],
        compiler_params=params(OUT_MIB),
        cost_estimate=cost(2 * rows * depth * cols, 2 * depth * (rows + cols) + 6 * rows * cols),
        name="project_out",
    )(flips, teacher, *flat, w_out)


def final_kernel(features, chunks, parts, *refs):
    branches, stats = refs[:chunks], refs[chunks : chunks + parts]
    student_ref, loss_ref = refs[chunks + parts :]
    sums = [stat[...] for stat in stats]
    while len(sums) > 1:
        sums = [x + y for x, y in zip(sums[::2], sums[1::2])]
    total = sums[0]
    inverse = lax.rsqrt(total[0:1] * (1.0 / features) + EPS_OUT)
    loss = inverse * inverse * total[0:1] - 2.0 * inverse * total[1:2] + total[2:3]
    loss_ref[...] = jnp.maximum(loss, 0.0) * (1.0 / features)
    column = jnp.transpose(jnp.broadcast_to(inverse, total.shape))[:, :1]
    rows = branches[0].shape[0]
    for at in range(chunks):
        scale = column[at * rows : (at + 1) * rows]
        student_ref[at * rows : (at + 1) * rows, :] = (branches[at][...] * scale).astype(
            jnp.bfloat16
        )


def final(features, branches, stats):
    chunks, parts = len(branches), len(stats)
    part_rows, cols = branches[0].shape
    rows = part_rows * chunks
    return pl.pallas_call(
        functools.partial(final_kernel, features, chunks, parts),
        grid=(1,),
        in_specs=[whole((part_rows, cols))] * chunks + [whole((8, rows))] * parts,
        out_specs=[whole((rows, cols)), whole((1, rows))],
        out_shape=[
            jax.ShapeDtypeStruct((rows, cols), jnp.bfloat16),
            jax.ShapeDtypeStruct((1, rows), jnp.float32),
        ],
        compiler_params=params(16),
        cost_estimate=cost(2 * rows * cols, 6 * rows * cols),
        name="final",
    )(*branches, *stats)


def swap(x, mask):
    count = lax.axis_size("tp")
    return lax.ppermute(x, "tp", [(i, i ^ mask) for i in range(count)])


def send_up(x, first):
    count = lax.axis_size("ctx")
    return lax.ppermute(x, "ctx", [(i, i + 1) for i in range(first, count - 1)])


def after(x, *others):
    return lax.optimization_barrier((x,) + others)[0]


def gather(own, core_after=None, beside=None, middle=None):
    count = lax.axis_size("tp")
    got = {0: [own]}
    masks = [1 << b for b in range(1, count.bit_length() - 1)]
    if len(masks) >= 2:
        a, b = masks[0], masks[1]
        half = own.shape[0] // (2 * EXTRA) * EXTRA
        via_a, via_b = swap(own, a), swap(own, b)
        got[1] = [swap(own, 1)]
        if beside is not None:
            token = beside(got[1][0])
            via_a, via_b = after(via_a, token), after(via_b, token)
        got[a], got[b] = [via_a], [via_b]
        diagonal = [swap(via_a[:half], b), swap(via_b[half:], a)]
        if core_after is not None:
            diagonal = [after(p, core_after) for p in diagonal]
        got[a | 1], got[b | 1] = [swap(via_a, 1)], [swap(via_b, 1)]
        got[a | b] = diagonal
        if middle is not None:
            token = middle(got)
            diagonal = [after(p, token) for p in diagonal]
        got[a | b | 1] = [swap(p, 1) for p in diagonal]
        masks = masks[2:]
    elif count > 1:
        got[1] = [swap(own, 1)]
    for mask in masks:
        for m in list(got):
            got[m | mask] = [swap(p, mask) for p in got[m]]
    return [got[m] for m in range(count)]


def body(hidden_in, norm_gain, w_query, w_key, w_value, sign_bits, w_out, teacher):
    rows = hidden_in.shape[0]
    half = rows // HALVES
    tp_count = lax.axis_size("tp")
    ctx_count = lax.axis_size("ctx")
    features = hidden_in.shape[1] * tp_count
    tp_at = lax.axis_index("tp")
    ctx_at = jnp.reshape(lax.axis_index("ctx"), (1,)).astype(jnp.int32)
    masks = jnp.arange(tp_count, dtype=jnp.int32)
    order = tp_at ^ masks
    shared = tp_at & masks
    parity = jnp.zeros_like(shared)
    for bit in range(tp_count.bit_length()):
        parity = parity ^ (shared >> bit & 1)
    flips = (1 - 2 * parity).astype(jnp.float32)
    signs = (2 * sign_bits - 1).astype(jnp.float32)
    gain = norm_gain.reshape(-1, GROUP)

    gain, order, ctx_at, flips = lax.optimization_barrier((gain, order, ctx_at, flips))
    clipped = pre(hidden_in, gain)

    kv_cols = w_key.shape[1]
    sharing = HD // kv_cols if kv_cols < HD else 1
    kv_heads = kv_cols * sharing // HD
    loaded = []

    def bring(token):
        first = after(w_query, token, order, ctx_at, flips, signs)
        loaded.extend(load(first, w_key, w_value, w_out))
        return loaded[1]

    early, state = [], []

    def begin(got):
        early.extend(sorted(got)[:-1])
        part = {m: got[m] for m in early}
        state.extend(proj(order, part, rows, (), False, *loaded[:3]))
        return state[-1]

    blocks = gather(clipped, beside=bring, middle=begin)
    if not loaded:
        bring(clipped)
    late = {m: block for m, block in enumerate(blocks) if m not in early}
    q, *kvs = proj(order, late, rows, state, True, *loaded[:3])
    for i, kv in enumerate(kvs):
        if sharing > 1:
            k, v = kv[:, :kv_cols], kv[:, kv_cols:]
            for bit in range(sharing.bit_length() - 1):
                upper = tp_at >> bit & 1 == 1
                k2, v2 = swap(k, 1 << bit), swap(v, 1 << bit)
                k, v = (
                    jnp.where(
                        upper,
                        jnp.concatenate([far, near], axis=1),
                        jnp.concatenate([near, far], axis=1),
                    )
                    for near, far in ((k, k2), (v, v2))
                )
            kv = jnp.concatenate([k, v], axis=1)
        kvs[i] = kv
    far, sent, states = [], kvs, []
    for hop in range(1, ctx_count):
        if hop == 3:
            sent = [after(kv, *[state[0] for state in states]) for kv in sent]
        sent = [send_up(kv, hop - 1) for kv in sent]
        far += [(hop, kv) for kv in sent]
        begun = far if ctx_count > 2 else []
        if hop == 1:
            states = [
                attend(ctx_at, q, at * half, half, kv_heads, kvs[: at + 1], begun, None, None)
                for at in range(HALVES)
            ]
    middle = far[HALVES:-HALVES]
    if middle:
        states = [
            attend(ctx_at, q, at * half, half, kv_heads, [], middle, states[at], None)
            for at in range(HALVES)
        ]
    q = after(q, *[state[0] for state in states])
    branches, stats = [], []
    for at in range(HALVES):
        signed = attend(
            ctx_at, q, at * half, half, kv_heads, [], far[-HALVES:], states[at], signs
        )
        blocks = gather(signed, branches[-1] if at else None)
        b, s = project_out(flips, blocks, loaded[3], teacher, at)
        branches.append(b)
        stats.append(s)
    stat = jnp.concatenate(stats, axis=1)
    if tp_count > 1:
        stat = stat + swap(stat, 1)
    totals = [stat] + [swap(stat, m) for m in range(2, tp_count, 2)]
    student, loss = final(features, branches, totals)
    return student, loss.reshape(rows)


def solution(mesh):
    in_specs = (
        P("ctx", "tp"),
        P("tp"),
        P(None, "tp"),
        P(None, "tp"),
        P(None, "tp"),
        P("tp", None),
        P(None, "tp"),
        P("ctx", "tp"),
    )
    out_specs = (P("ctx", "tp"), P("ctx"))
    return jax.shard_map(body, mesh=mesh, in_specs=in_specs, out_specs=out_specs, check_vma=False)
```
